32 devices in a mesh: seq: 4 (over z), batch: 8 (over y, x, core).
Axes of the slice: x: 2, y: 2, z: 4, core: 2. Of those that a mesh axis runs over, the one named last changes fastest.
Arguments:
- tokens: bfloat16 [24, 2048, 512], P('batch', 'seq'), may hold values from -6 to 6
- cotangent: bfloat16 [24, 2048, 512], P('batch', 'seq'), may hold values from -6 to 6
- start_states: float32 [24, 1024], P('batch'), may hold values from -6 to 6
- lengths: int32 [24], P('batch'), may hold values from 1024 to 2048, as said below
- w_in: float32 [512, 2048], P(('seq', 'batch')), may hold values from -0.25 to 0.25
- w_out: float32 [1024, 512], P(('seq', 'batch')), may hold values from -0.1875 to 0.1875
- w_up: float32 [512, 2048], P(('seq', 'batch')), may hold values from -0.25 to 0.25
- w_down: float32 [2048, 512], P(('seq', 'batch')), may hold values from -0.125 to 0.125
- vectors: float32 [4096], P(('seq', 'batch'))
- first_in: float32 [512, 2048], P(('seq', 'batch')), may hold values from -224 to 224
- second_in: float32 [512, 2048], P(('seq', 'batch')), may hold values from 737.28 to 11796.48
- first_out: float32 [1024, 512], P(('seq', 'batch')), may hold values from -640 to 640
- second_out: float32 [1024, 512], P(('seq', 'batch')), may hold values from 6635.52 to 106168.32
- first_up: float32 [512, 2048], P(('seq', 'batch')), may hold values from -320 to 320
- second_up: float32 [512, 2048], P(('seq', 'batch')), may hold values from 1671.168 to 26542.08
- first_down: float32 [2048, 512], P(('seq', 'batch')), may hold values from -640 to 640
- second_down: float32 [2048, 512], P(('seq', 'batch')), may hold values from 6635.52 to 106168.32
- first_vec: float32 [4096], P(('seq', 'batch')), may hold values from -448 to 448
- second_vec: float32 [4096], P(('seq', 'batch')), may hold values from 2949.12 to 47185.92
Outputs:
- block_out: bfloat16 [24, 2048, 512], P('batch', 'seq')
- stretch_states: float32 [24, 4, 1024], P('batch', 'seq')
- grad_tokens: float32 [24, 2048, 512], P('batch', 'seq')
- new_in: float32 [512, 2048], P(('seq', 'batch'))
- copy_in: bfloat16 [512, 2048], P(('seq', 'batch'))
- moment_in: float32 [512, 2048], P(('seq', 'batch'))
- square_in: float32 [512, 2048], P(('seq', 'batch'))
- new_out: float32 [1024, 512], P(('seq', 'batch'))
- copy_out: bfloat16 [1024, 512], P(('seq', 'batch'))
- moment_out: float32 [1024, 512], P(('seq', 'batch'))
- square_out: float32 [1024, 512], P(('seq', 'batch'))
- new_up: float32 [512, 2048], P(('seq', 'batch'))
- copy_up: bfloat16 [512, 2048], P(('seq', 'batch'))
- moment_up: float32 [512, 2048], P(('seq', 'batch'))
- square_up: float32 [512, 2048], P(('seq', 'batch'))
- new_down: float32 [2048, 512], P(('seq', 'batch'))
- copy_down: bfloat16 [2048, 512], P(('seq', 'batch'))
- moment_down: float32 [2048, 512], P(('seq', 'batch'))
- square_down: float32 [2048, 512], P(('seq', 'batch'))
- new_vec: float32 [4096], P(('seq', 'batch'))
- moment_vec: float32 [4096], P(('seq', 'batch'))
- square_vec: float32 [4096], P(('seq', 'batch'))
The draws below stay inside these ranges and needn't reach their ends.
Inputs may be any that keep to these rules, and one draw needn't show every extreme that they name: `lengths`: in every group of 3 consecutive sequences one has length exactly 2048.
All inputs are finite; a program needn't handle non-finite values.
Results may differ from the reference program's by a relative error of at most 0.012.
The reference program's roundings to bfloat16 on the way count: a program that leaves them out, or rounds other values in their place, can miss the bound.
Values may be sent and summed in bfloat16 or wider, within the bound.
A program may use at most 192 MiB of HBM per device.

```python
import math
import jax
import jax.numpy as jnp
from jax import lax

D = 512
H = 1024
F = 2048
SEQ_LEN = 2048
SEQS_GRP = 3
STEP = 5
STRETCH = 512
SEQUENCES = 24
TOKENS = 49152
VEC = 4096


def draw_vectors(key, part):
    key = jax.random.fold_in(key, 11)
    keys = jax.random.split(key, 5)
    gains = jax.random.uniform(keys[0], (2 * D,), jnp.float32, 0.6, 1.4)
    slow_share = 0.5
    taps = jax.random.uniform(keys[1], (4 * D,), jnp.float32, -0.8, 0.8)
    base = math.log(float(SEQ_LEN))
    slow_mask = jax.random.bernoulli(keys[2], slow_share, (H,))
    slow_bias = jax.random.uniform(keys[3], (H,), jnp.float32, -base - 1.5, -base)
    fast_bias = jax.random.uniform(keys[4], (H,), jnp.float32, -3.5, 0.5)
    bias = jnp.where(slow_mask, slow_bias, fast_bias)
    return jnp.concatenate([gains, taps, bias]).astype(jnp.float32)


def draw_lengths(key, part):
    key = jax.random.fold_in(key, 7)
    keys = jax.random.split(key, 2)
    drawn = jax.random.randint(keys[0], (SEQUENCES,), SEQ_LEN // 2, SEQ_LEN + 1)
    groups = SEQUENCES // SEQS_GRP
    picked = jax.random.randint(keys[1], (groups,), 0, SEQS_GRP)
    full_one = (jnp.arange(SEQS_GRP)[None, :] == picked[:, None]).reshape(-1)
    return jnp.where(full_one, SEQ_LEN, drawn).astype(jnp.int32)


def block_scale(stream_key, shape, cuts, smallest, largest):
    level = 1.0
    for dim, parts in cuts:
        heights = jax.random.uniform(jax.random.fold_in(jax.random.fold_in(stream_key, 6), dim), (parts,), jnp.float32, smallest / len(cuts), largest / len(cuts))
        level = level * jnp.repeat(jnp.exp(heights), shape[dim] // parts).reshape((-1,) + (1,) * (len(shape) - 1 - dim))
    return level


def gaussian(own_key, dims, deviation, most, shards=(), kind=jnp.bfloat16):
    values = deviation * jax.random.normal(own_key, dims, jnp.float32)
    if shards:
        values = values * block_scale(own_key, dims, shards, -0.22, 0.18)
    return jnp.clip(values, -most, most).astype(kind)


def setup_inputs(seed: int = 0) -> dict:
    splits = jax.random.split(jax.random.key(seed), 20)
    tokens = gaussian(splits[0], (SEQUENCES, SEQ_LEN, D), 1.0, 6.0, ((0, 8), (1, 4)))
    cotangent = gaussian(splits[1], (SEQUENCES, SEQ_LEN, D), 1.0, 6.0, ((0, 8), (1, 4)))
    start_states = gaussian(splits[2], (SEQUENCES, H), 1.0, 6.0, ((0, 8),), jnp.float32)
    lengths = draw_lengths(jax.random.fold_in(splits[19], 71), 0)
    w_in = gaussian(splits[4], (D, 2 * H), D ** -0.5, 0.25, ((0, 32),), jnp.float32)
    w_out = gaussian(splits[5], (H, D), H ** -0.5, 0.1875, ((0, 32),), jnp.float32)
    w_up = gaussian(splits[6], (D, F), D ** -0.5, 0.25, ((0, 32),), jnp.float32)
    w_down = gaussian(splits[7], (F, D), F ** -0.5, 0.125, ((0, 32),), jnp.float32)
    vectors = draw_vectors(jax.random.fold_in(splits[19], 71), 0)
    first_in = gaussian(splits[9], (D, 2 * H), (0.17 * TOKENS ** 0.5), 224.0, ((0, 32),), jnp.float32)
    second_in = jnp.clip(jnp.exp(math.log(11796.48) - 2.7725887 * jax.random.uniform(splits[10], (D, 2 * H), jnp.float32) ** block_scale(splits[10], (D, 2 * H), ((0, 32),), -0.2, 0.2)), 737.28, 11796.48)
    first_out = gaussian(splits[11], (H, D), (0.52 * TOKENS ** 0.5), 640.0, ((0, 32),), jnp.float32)
    second_out = jnp.clip(jnp.exp(math.log(106168.32) - 2.7725887 * jax.random.uniform(splits[12], (H, D), jnp.float32) ** block_scale(splits[12], (H, D), ((0, 32),), -0.2, 0.2)), 6635.52, 106168.32)
    first_up = gaussian(splits[13], (D, F), (0.26 * TOKENS ** 0.5), 320.0, ((0, 32),), jnp.float32)
    second_up = jnp.clip(jnp.exp(math.log(26542.08) - 2.76520864 * jax.random.uniform(splits[14], (D, F), jnp.float32) ** block_scale(splits[14], (D, F), ((0, 32),), -0.2, 0.2)), 1671.168, 26542.08)
    first_down = gaussian(splits[15], (F, D), (0.52 * TOKENS ** 0.5), 640.0, ((0, 32),), jnp.float32)
    second_down = jnp.clip(jnp.exp(math.log(106168.32) - 2.7725887 * jax.random.uniform(splits[16], (F, D), jnp.float32) ** block_scale(splits[16], (F, D), ((0, 32),), -0.2, 0.2)), 6635.52, 106168.32)
    first_vec = gaussian(splits[17], (VEC,), (0.35 * TOKENS ** 0.5), 448.0, ((0, 32),), jnp.float32)
    second_vec = jnp.clip(jnp.exp(math.log(47185.92) - 2.7725887 * jax.random.uniform(splits[18], (VEC,), jnp.float32) ** block_scale(splits[18], (VEC,), ((0, 32),), -0.2, 0.2)), 2949.12, 47185.92)
    return dict(tokens=tokens, cotangent=cotangent, start_states=start_states, lengths=lengths, w_in=w_in, w_out=w_out, w_up=w_up, w_down=w_down, vectors=vectors, first_in=first_in, second_in=second_in, first_out=first_out, second_out=second_out, first_up=first_up, second_up=second_up, first_down=first_down, second_down=second_down, first_vec=first_vec, second_vec=second_vec)


@jax.custom_vjp
def low(v):
    return lax.optimization_barrier(v.astype(jnp.bfloat16)).astype(jnp.float32)

@jax.custom_vjp
def low_back(v):
    return v

def low_keep(v):
    return (low(v), None)

def low_pass(kept, grad):
    return (grad,)

def back_keep(v):
    return (v, None)

def back_low(kept, grad):
    return (low(grad),)
low.defvjp(low_keep, low_pass)
low_back.defvjp(back_keep, back_low)
EPS = 1e-06
ADAM_EPS = 1e-08
BETA_ONE = 0.5
BETA_TWO = 0.5
DECAY = 0.1
VEC_RATE = 1.5
HIGH = lax.Precision.HIGHEST

def rms_scale(values, gain):
    return values * lax.rsqrt(lax.optimization_barrier(jnp.mean(values * values, axis=-1, keepdims=True)) + EPS) * gain

def combine_affine(earlier, later):
    return (earlier[0] * later[0], later[0] * earlier[1] + later[1])

def block_forward(inputs, full_in, full_out, full_up, full_down, full_vec, seq_len, start):
    g_one = full_vec[:D]
    g_two = full_vec[D:2 * D]
    taps = full_vec[2 * D:6 * D].reshape(4, D)
    bias = full_vec[6 * D:]
    normed = low(rms_scale(inputs, g_one))
    padded = jnp.pad(normed, ((3, 0), (0, 0)))
    mixed = low(sum((taps[tap_idx] * padded[tap_idx:tap_idx + SEQ_LEN] for tap_idx in range(4))))
    projected = low_back(jnp.dot(mixed, full_in, precision=HIGH))
    valid = (jnp.arange(SEQ_LEN) < seq_len).astype(jnp.float32)[:, None]
    update = jax.nn.sigmoid(projected[:, :H] + bias) * valid
    retain = 1.0 - update
    driven = update * projected[:, H:]
    run_keep, run_drive = lax.associative_scan(combine_affine, (retain, driven), axis=0)
    states = run_keep * start[None, :] + run_drive
    mixer = low_back(jnp.dot(low(states), full_out, precision=HIGH))
    middle = inputs + valid * mixer
    normed_two = low(rms_scale(middle, g_two))
    up_pre = low_back(jnp.dot(normed_two, full_up, precision=HIGH))
    gelu_out = low(jax.nn.gelu(up_pre))
    branch = low_back(jnp.dot(gelu_out, full_down, precision=HIGH))
    result = middle + valid * branch
    stretch_end = states[STRETCH - 1::STRETCH]
    return (result, stretch_end)

def adam_step(weight, grad, first, second, rate, decay):
    moment = BETA_ONE * first + (1.0 - BETA_ONE) * grad
    square = BETA_TWO * second + (1.0 - BETA_TWO) * grad * grad
    corr_one = 1.0 - BETA_ONE ** STEP
    corr_two = 1.0 - BETA_TWO ** STEP
    direction = moment / corr_one / (jnp.sqrt(square / corr_two) + ADAM_EPS)
    fresh = weight - rate * (direction + decay * weight)
    return (fresh, moment, square)

def reference(tokens, cotangent, start_states, lengths, w_in, w_out, w_up, w_down, vectors, first_in, second_in, first_out, second_out, first_up, second_up, first_down, second_down, first_vec, second_vec):
    rounded = tuple((lax.optimization_barrier(w.astype(jnp.bfloat16)).astype(jnp.float32) for w in (w_in, w_out, w_up, w_down, vectors)))

    def per_seq(carry, item):
        seq_x, seq_dy, seq_start, seq_len = item

        def forward_seq(inputs, full_in, full_out, full_up, full_down, full_vec):
            return block_forward(inputs, full_in, full_out, full_up, full_down, full_vec, seq_len, seq_start)
        result, pullback, stretch_end = jax.vjp(forward_seq, seq_x.astype(jnp.float32), *rounded, has_aux=True)
        grads = pullback(seq_dy.astype(jnp.float32))
        carry = tuple((total + piece for total, piece in zip(carry, grads[1:])))
        return (carry, (result.astype(jnp.bfloat16), stretch_end, grads[0]))
    init = tuple((jnp.zeros(w.shape, jnp.float32) for w in rounded))
    totals, (block_out, stretch_states, grad_tokens) = lax.scan(per_seq, init, (tokens, cotangent, start_states, lengths))
    grad_in, grad_out, grad_up, grad_down, grad_vec = totals
    new_in, moment_in, square_in = adam_step(w_in, grad_in, first_in, second_in, D ** (-0.5), DECAY)
    new_out, moment_out, square_out = adam_step(w_out, grad_out, first_out, second_out, H ** (-0.5), DECAY)
    new_up, moment_up, square_up = adam_step(w_up, grad_up, first_up, second_up, D ** (-0.5), DECAY)
    new_down, moment_down, square_down = adam_step(w_down, grad_down, first_down, second_down, F ** (-0.5), DECAY)
    new_vec, moment_vec, square_vec = adam_step(vectors, grad_vec, first_vec, second_vec, VEC_RATE, 0.0)
    return (block_out, stretch_states, grad_tokens, new_in, new_in.astype(jnp.bfloat16), moment_in, square_in, new_out, new_out.astype(jnp.bfloat16), moment_out, square_out, new_up, new_up.astype(jnp.bfloat16), moment_up, square_up, new_down, new_down.astype(jnp.bfloat16), moment_down, square_down, new_vec, moment_vec, square_vec)
```

```python
import functools

import jax
import jax.numpy as jnp
from jax import lax
from jax.experimental import pallas as pl
from jax.experimental.pallas import tpu as pltpu
from jax.sharding import PartitionSpec as P

D = 512
H = 1024
F = 2048
STEP = 5
EPS = 1e-06
ADAM_EPS = 1e-08
BETA_ONE = 0.5
BETA_TWO = 0.5
DECAY = 0.1
VEC_RATE = 1.5
MESH = pl.DeviceIdType.MESH
F32 = jnp.float32
BF16 = jnp.bfloat16
SUB = 8
LANES = 128
SEQS = 3

NN = (((1,), (0,)), ((), ()))
NT = (((1,), (1,)), ((), ()))
TN = (((0,), (0,)), ((), ()))


def dot(a, b, dims=NN):
    return lax.dot_general(a, b, dims, preferred_element_type=F32)


def tiles(v):
    return v.reshape(v.shape[0] // SUB, SUB, v.shape[1])


def flat(v):
    return v.reshape(v.shape[0] * SUB, v.shape[2])


def fold(v):
    return jnp.sum(tiles(v), axis=0)


def row_mean(v):
    return jnp.mean(v, axis=-1, keepdims=True)


IN, OUT, UP, DOWN = range(4)


def step_kernel(
    nz, span,
    tok_hbm, cot_hbm, start_ref, len_ref, w_in_hbm, w_out_hbm, w_up_hbm, w_down_hbm, vec_ref,
    block_hbm, ends_ref, grad_hbm, sum_in, sum_out, sum_up, sum_down, sum_vec,
    cp, mix, win, wout, wup, wdown, upd, cand, st, gl, du, n2, db, mid, gdown, gup,
    r0o, r0u, r0d, r1ai, r1bi, r1ao, r1bo, r1au, r1bu, r1ad, r1bd,
    r2ai, r2bi, r2ao, r2bo, r2au, r2bu, r2ad, r2bd,
    r3ai, r3bi, r3ao, r3bo, r3au, r3bu, r3ad, r3bd,
    perm, clock, vec8, vgrad, vrecv, halo_out, halo_in, back_out, back_in,
    sums, sums_in, bsums, bsums_in,
    io_sem, ag_send, ag_recv, rs_send, rs_recv, v_sem, h_sem, c_send, c_recv, b_send, b_recv, g_sem, free_sem,
):
    nj = span // SUB
    z = lax.axis_index("seq")
    b = lax.axis_index("batch")
    y, x, c = b // 4, lax.rem(b // 2, 2), lax.rem(b, 2)
    me = z * 8 + b
    ndev = nz * 8
    px, py, pc = (z, b + 2 - 4 * x), (z, b + 4 - 8 * y), (z, b + 1 - 2 * c)
    full = (win, wout, wup, wdown)
    masters = (w_in_hbm, w_out_hbm, w_up_hbm, w_down_hbm)
    staged = (sum_in, sum_out, sum_up, sum_down)

    def remote(src, dst, ssem, rsem, dev):
        return pltpu.make_async_remote_copy(
            src_ref=src, dst_ref=dst, send_sem=ssem, recv_sem=rsem, device_id=dev, device_id_type=MESH
        )

    loads = [pltpu.make_async_copy(masters[k], staged[k], io_sem.at[k]) for k in range(4)]
    tok_load = pltpu.make_async_copy(tok_hbm, n2, io_sem.at[4])
    cot_load = pltpu.make_async_copy(cot_hbm, db, io_sem.at[5])
    for cpy in loads:
        cpy.start()
    tok_load.start()
    cot_load.start()

    barrier = pltpu.get_barrier_semaphore()

    def greet(i, carry):
        @pl.when(i != me)
        def _():
            pl.semaphore_signal(barrier, inc=1, device_id=(i // 8, lax.rem(i, 8)), device_id_type=MESH)
        return carry

    lax.fori_loop(0, ndev, greet, 0)

    rows = lax.broadcasted_iota(jnp.int32, (span, span), 0)
    cols = lax.broadcasted_iota(jnp.int32, (span, span), 1)
    perm[...] = jnp.where(cols == lax.rem(rows, SUB) * nj + rows // SUB, 1.0, 0.0).astype(BF16)
    vrow = lax.broadcasted_iota(jnp.int32, (span, LANES), 0)
    when = lax.rem(vrow, SUB) * nj + vrow // SUB + z * span
    clock[...] = when.astype(F32)

    def keep_of(s):
        one = jnp.where(clock[...] < len_ref[s].astype(F32), 1.0, 0.0)
        return jnp.concatenate([one] * (D // LANES), axis=1)

    own_vec = vec_ref[...].astype(BF16).astype(F32)
    vec8[:, pl.ds(pl.multiple_of(me * LANES, LANES), LANES)] = jnp.broadcast_to(own_vec, (SUB, LANES))
    for k in range(4):
        loads[k].wait()
        full[k][z, y, x, c] = staged[k][...].astype(BF16)

    pl.semaphore_wait(barrier, ndev - 1)

    mine = vec8.at[:, pl.ds(pl.multiple_of(me * LANES, LANES), LANES)]

    def spread(i, carry):
        @pl.when(i != me)
        def _():
            remote(mine, mine, v_sem.at[0], v_sem.at[1], (i // 8, lax.rem(i, 8))).start()
        return carry

    lax.fori_loop(0, ndev, spread, 0)

    def half(k, h):
        n = full[k].shape[-1] // 2
        return slice(h * n, (h + 1) * n)

    def ag_z(k):
        block = full[k].at[z, y, x, c]
        return [
            remote(block, block, ag_send.at[k, dz - 1], ag_recv.at[k, dz - 1], (lax.rem(z + dz, nz), b))
            for dz in range(1, nz)
        ]

    def ag_1(k):
        one = full[k].at[:, y, x, c, :, half(k, 0)]
        two = full[k].at[:, y, x, c, :, half(k, 1)]
        return [
            remote(one, one, ag_send.at[k, 3], ag_recv.at[k, 3], px),
            remote(two, two, ag_send.at[k, 4], ag_recv.at[k, 4], py),
        ]

    def ag_2(k):
        one = full[k].at[:, y, :, c, :, half(k, 0)]
        two = full[k].at[:, :, x, c, :, half(k, 1)]
        return [
            remote(one, one, ag_send.at[k, 5], ag_recv.at[k, 5], py),
            remote(two, two, ag_send.at[k, 6], ag_recv.at[k, 6], px),
        ]

    def ag_c(k):
        block = full[k].at[:, :, :, c]
        return [remote(block, block, ag_send.at[k, 7], ag_recv.at[k, 7], pc)]

    stages = (ag_z, ag_1, ag_2, ag_c)

    def ag_start(k, stage):
        for cpy in stages[stage](k):
            cpy.start()

    def ag_wait(k, stage):
        for cpy in stages[stage](k):
            cpy.wait_recv()

    def ag_next(k, stage):
        ag_wait(k, stage - 1)
        ag_start(k, stage)

    def ag_left(k):
        for stage in stages:
            for cpy in stage(k):
                cpy.wait_send()

    for k in (IN, OUT, UP, DOWN):
        ag_start(k, 0)

    tok_load.wait()
    for s in range(SEQS):
        gdown[s] = dot(perm[...], n2[s]).astype(BF16).reshape(gdown.shape[1:])
    cot_load.wait()
    for s in range(SEQS):
        cp[s] = dot(perm[...], db[s]).astype(BF16)
    for s in range(SEQS):
        keep = keep_of(s)
        db[s] = (cp[s].astype(F32) * keep).astype(BF16)

    rest = vec8.at[:, 0:(ndev - 1) * LANES]
    remote(rest, rest, v_sem.at[0], v_sem.at[1], pc).wait_recv()
    ag_next(IN, 1)
    g_one = vec8[:, 0:D]
    g_two = vec8[:, D:2 * D]
    taps = [vec8[:, (2 + k) * D:(3 + k) * D] for k in range(4)]

    def unit_of(v):
        scale = lax.rsqrt(row_mean(v * v) + EPS)
        return v * scale, scale

    sub0 = lax.broadcasted_iota(jnp.int32, (SUB, D), 0)
    for s in range(SEQS):
        unit, _ = unit_of(gdown[s].reshape(span, D).astype(F32))
        normed = (tiles(unit) * g_one).astype(BF16).astype(F32)
        upd[s, 3 * SUB:3 * SUB + span] = flat(normed)
        for i in range(3):
            r = 3 * s + i
            halo_out[r:r + 1, :] = upd[s, span + i * SUB + SUB - 1:span + i * SUB + SUB, :]
    send_halo = remote(halo_out, halo_in, h_sem.at[0], h_sem.at[1], (lax.rem(z + 1, nz), b))
    send_halo.start()
    ag_next(OUT, 1)
    ag_next(IN, 2)
    send_halo.wait_recv()
    for s in range(SEQS):
        for i in range(3):
            r = 3 * s + i
            tile = pltpu.roll(upd[s, span + i * SUB:span + (i + 1) * SUB, :], 1, 0)
            edge = jnp.where(z > 0, halo_in[r:r + 1, :], 0.0)
            upd[s, i * SUB:(i + 1) * SUB] = jnp.where(sub0 == 0, edge, tile)
    for s in range(SEQS):
        total = taps[0] * tiles(upd[s, 0:span])
        for k in range(1, 4):
            total = total + taps[k] * tiles(upd[s, k * SUB:k * SUB + span])
        mix[s] = flat(total).astype(BF16)
    ag_next(UP, 1)
    ag_next(OUT, 2)
    ag_next(IN, 3)
    ag_next(DOWN, 1)
    ag_next(UP, 2)
    ag_next(OUT, 3)
    ag_wait(IN, 3)

    def weight(k, *at):
        v = full[k][at] if at else full[k][...]
        return v

    def cols_of(k, lo, hi):
        v = full[k][:, :, :, :, :, lo:hi]
        return v.reshape(v.shape[0] * 8 * v.shape[4], hi - lo)

    def all_of(k):
        v = full[k][...]
        return v.reshape(v.shape[0] * 8 * v.shape[4], v.shape[5])

    def two(ref, s, j):
        at = pl.multiple_of(j * SUB, SUB)
        return ref[s, pl.ds(at, SUB), :], ref[s, pl.ds(at + span, SUB), :]

    lane_sub = lax.broadcasted_iota(jnp.int32, (SUB, D), 0)

    def project(s, carry):
        keep = keep_of(s)
        rows_in = mix[s]
        for hh in range(2):
            bias = vec8[:, 6 * D + hh * D:6 * D + (hh + 1) * D]
            gate = tiles(dot(rows_in, cols_of(IN, hh * D, (hh + 1) * D))) + bias
            upd[s, hh * span:(hh + 1) * span] = flat(jax.nn.sigmoid(gate)) * keep
            cand[s, hh * span:(hh + 1) * span] = dot(rows_in, cols_of(IN, H + hh * D, H + (hh + 1) * D))
        return carry

    lax.fori_loop(0, SEQS, project, 0)

    def inclusive(keep, drive, reverse):
        for d in (1, 2, 4):
            by = SUB - d if reverse else d
            inside = lane_sub < SUB - d if reverse else lane_sub >= d
            k2 = jnp.where(inside, pltpu.roll(keep, by, 0), 1.0)
            d2 = jnp.where(inside, pltpu.roll(drive, by, 0), 0.0)
            drive = drive + keep * d2
            keep = keep * k2
        return keep, drive

    def exclusive(keep, drive, reverse):
        by = SUB - 1 if reverse else 1
        edge = lane_sub == (SUB - 1 if reverse else 0)
        return (
            jnp.where(edge, 1.0, pltpu.roll(keep, by, 0)),
            jnp.where(edge, 0.0, pltpu.roll(drive, by, 0)),
        )

    def scan_totals(s):
        def body(j, carry):
            u = two(upd, s, j)
            v = two(cand, s, j)
            out = []
            for hh in range(2):
                a, d = carry[2 * hh], carry[2 * hh + 1]
                out += [a * (1.0 - u[hh]), d + u[hh] * (v[hh] - d)]
            return tuple(out)

        one, zero = jnp.ones((SUB, D), F32), jnp.zeros((SUB, D), F32)
        return lax.fori_loop(0, nj, body, (one, zero, one, zero), unroll=4)

    prefix = []
    for s in range(SEQS):
        a0, d0, a1, d1 = scan_totals(s)
        for hh, (a, d) in enumerate(((a0, d0), (a1, d1))):
            a, d = inclusive(a, d, False)
            sums[s:s + 1, hh * D:(hh + 1) * D] = a[SUB - 1:SUB, :]
            sums[SEQS + s:SEQS + s + 1, hh * D:(hh + 1) * D] = d[SUB - 1:SUB, :]
            prefix.append(exclusive(a, d, False))

    def carry_copy(src, dst, ssem, rsem, dz):
        return remote(src, dst.at[z], ssem.at[dz], rsem.at[z], (z + dz, b))

    for dz in range(1, nz):
        @pl.when(z + dz < nz)
        def _():
            carry_copy(sums, sums_in, c_send, c_recv, dz).start()

    ag_next(DOWN, 2)
    ag_next(UP, 3)

    def enter_from(i, carry):
        remote(sums, sums_in.at[i], c_send.at[0], c_recv.at[i], pc).wait_recv()
        got = sums_in[i]
        return got[0:SEQS] * carry + got[SEQS:2 * SEQS]

    entering = lax.fori_loop(0, z, enter_from, start_ref[...])

    for s in range(SEQS):
        def body(i, carry):
            hs = list(carry)
            lows = [[], []]
            for jj in range(2):
                j = i * 2 + jj
                at = pl.multiple_of(j * SUB, SUB)
                u = two(upd, s, j)
                v = two(cand, s, j)
                for hh in range(2):
                    moved = u[hh] * (v[hh] - hs[hh])
                    hs[hh] = hs[hh] + moved
                    cand[s, pl.ds(at + hh * span, SUB), :] = moved * (1.0 - u[hh])
                    lows[hh].append(hs[hh])
            at = pl.multiple_of(i * 2 * SUB, 2 * SUB)
            for hh in range(2):
                st[s, pl.ds(at, 2 * SUB), hh * D:(hh + 1) * D] = jnp.concatenate(lows[hh], axis=0).astype(BF16)
            return tuple(hs)

        init = []
        for hh in range(2):
            ek, ed = prefix[2 * s + hh]
            init.append(ek * entering[s:s + 1, hh * D:(hh + 1) * D] + ed)
        ended = lax.fori_loop(0, nj // 2, body, tuple(init), unroll=2)
        for hh in range(2):
            ends_ref[s, :, hh * D:(hh + 1) * D] = ended[hh][SUB - 1:SUB, :]

    ag_next(DOWN, 3)
    ag_wait(OUT, 3)
    ag_wait(UP, 3)
    ag_wait(DOWN, 3)

    root = 0.7978845608028654
    cubic = 0.044715

    def ffn_one(s, carry):
        keep = keep_of(s)
        middle = gdown[s].reshape(span, D).astype(F32) + keep * dot(st[s], all_of(OUT))
        mid[s] = middle
        scale = lax.rsqrt(row_mean(middle * middle) + EPS)
        low = flat(tiles(middle * scale) * g_two).astype(BF16)
        n2[s] = low
        d_branch = db[s]
        for q in range(F // D):
            pre = dot(low, cols_of(UP, q * D, (q + 1) * D))
            d_gelu = dot(d_branch, wdown[q].reshape(F // nz, D), NT)
            sq = pre * pre
            t = jnp.tanh(root * (pre + cubic * (pre * sq)))
            hp = 0.5 * (1.0 + t)
            gl[s, :, q * D:(q + 1) * D] = (pre * hp).astype(BF16)
            slope = hp + (0.5 * root) * pre * (1.0 - t * t) * (1.0 + (3.0 * cubic) * sq)
            du[s, :, q * D:(q + 1) * D] = (slope * d_gelu).astype(BF16)
        return carry

    lax.fori_loop(0, SEQS, ffn_one, 0)

    partial = (wup, wout, gup, gdown)
    r0 = (r0u, r0o, r0u, r0d)
    r1 = ((r1ai, r1bi), (r1ao, r1bo), (r1au, r1bu), (r1ad, r1bd))
    r2 = ((r2ai, r2bi), (r2ao, r2bo), (r2au, r2bu), (r2ad, r2bd))
    r3 = ((r3ai, r3bi), (r3ao, r3bo), (r3au, r3bu), (r3ad, r3bd))
    finals = (sum_in, sum_out, sum_up, sum_down)

    def rs_copies(k, stage):
        g, ss, rr = partial[k], rs_send, rs_recv
        if stage == 0:
            return [remote(g.at[:, :, :, 1 - c], r0[k], ss.at[k, 0], rr.at[k, 0], pc)]
        if stage == 1:
            return [
                remote(r0[k].at[:, 1 - y, :, :, half(k, 0)], r1[k][0], ss.at[k, 1], rr.at[k, 1], py),
                remote(r0[k].at[:, :, 1 - x, :, half(k, 1)], r1[k][1], ss.at[k, 2], rr.at[k, 2], px),
            ]
        if stage == 2:
            return [
                remote(r1[k][0].at[:, 1 - x], r2[k][0], ss.at[k, 3], rr.at[k, 3], px),
                remote(r1[k][1].at[:, 1 - y], r2[k][1], ss.at[k, 4], rr.at[k, 4], py),
            ]
        out = []
        for dz in range(1, nz):
            to = lax.rem(z + dz, nz)
            for h in range(2):
                at = 5 + 2 * (dz - 1) + h
                out.append(remote(r2[k][h].at[to], r3[k][h].at[dz - 1], ss.at[k, at], rr.at[k, at], (to, b)))
        return out

    def rs_start(k, stage):
        for cpy in rs_copies(k, stage):
            cpy.start()

    def rs_next(k, stage):
        for cpy in rs_copies(k, stage - 1):
            cpy.wait_recv()
        if stage == 1:
            r0[k][...] = (r0[k][...].astype(F32) + partial[k][:, :, :, c].astype(F32)).astype(BF16)
        elif stage == 2:
            r1[k][0][...] = (r1[k][0][...].astype(F32) + r0[k][:, y, :, :, half(k, 0)].astype(F32)).astype(BF16)
            r1[k][1][...] = (r1[k][1][...].astype(F32) + r0[k][:, :, x, :, half(k, 1)].astype(F32)).astype(BF16)
        elif stage == 3:
            r2[k][0][...] = (r2[k][0][...].astype(F32) + r1[k][0][:, x].astype(F32)).astype(BF16)
            r2[k][1][...] = (r2[k][1][...].astype(F32) + r1[k][1][:, y].astype(F32)).astype(BF16)
        else:
            for h in range(2):
                total = r2[k][h][z].astype(F32)
                for i in range(nz - 1):
                    total = total + r3[k][h][i].astype(F32)
                finals[k][:, half(k, h)] = total
        if stage < 4:
            rs_start(k, stage)

    def whole(ref, lo, hi):
        v = ref[:, :, lo:hi]
        return v.reshape(SEQS * span, hi - lo)

    def grad_down(q, carry):
        qs = pl.multiple_of(q * D, D)
        v = gl[:, :, pl.ds(qs, D)].reshape(SEQS * span, D)
        g = dot(v, db[...].reshape(SEQS * span, D), TN)
        gdown[pl.ds(q, 1)] = g.astype(BF16).reshape((1,) + gdown.shape[1:])
        return carry

    lax.fori_loop(0, nz, grad_down, 0)
    rs_start(DOWN, 0)
    low_all = n2[...].reshape(SEQS * span, D)
    for q in range(F // D):
        g = dot(low_all, whole(du, q * D, (q + 1) * D), TN)
        gup[:, :, :, :, :, q * D:(q + 1) * D] = g.astype(BF16).reshape(gup.shape[:5] + (D,))
    rs_start(UP, 0)
    tok_load.start()
    rs_next(DOWN, 1)

    def ffn_two(s, carry):
        keep = keep_of(s)
        middle = mid[s]
        gy = cp[s].astype(F32)
        scale = lax.rsqrt(row_mean(middle * middle) + EPS)
        unit = middle * scale
        block = (middle + keep * dot(gl[s], all_of(DOWN))).astype(BF16)
        d_low = dot(du[s], all_of(UP), NT)
        vgrad[:, D:2 * D] += fold(d_low * unit)
        e = flat(tiles(d_low) * g_two)
        d_middle = gy + scale * (e - unit * row_mean(e * unit))
        mid[s] = d_middle
        d_mixer = (d_middle * keep).astype(BF16)
        db[s] = d_mixer
        cp[s] = dot(perm[...], block, TN).astype(BF16)
        gl[s, :, 0:H] = dot(d_mixer, all_of(OUT), NT).astype(BF16)
        return carry

    vgrad[...] = jnp.zeros_like(vgrad)
    lax.fori_loop(0, SEQS, ffn_two, 0)
    block_store = pltpu.make_async_copy(cp, block_hbm, io_sem.at[6])
    block_store.start()

    def two_low(s, i):
        at = pl.multiple_of(i * 2 * SUB, 2 * SUB)
        v = gl[s, pl.ds(at, 2 * SUB), 0:H].astype(F32)
        return [[v[jj * SUB:(jj + 1) * SUB, hh * D:(hh + 1) * D] for hh in range(2)] for jj in range(2)]

    bprefix = []
    for s in range(SEQS):
        def body(k, carry):
            i = nj // 2 - 1 - k
            vals = list(carry)
            ds = two_low(s, i)
            for jj in (1, 0):
                u = two(upd, s, i * 2 + jj)
                for hh in range(2):
                    om = 1.0 - u[hh]
                    vals[2 * hh] = vals[2 * hh] * om
                    vals[2 * hh + 1] = om * (ds[jj][hh] + vals[2 * hh + 1])
            return tuple(vals)

        one, zero = jnp.ones((SUB, D), F32), jnp.zeros((SUB, D), F32)
        a0, d0, a1, d1 = lax.fori_loop(0, nj // 2, body, (one, zero, one, zero), unroll=2)
        for hh, (a, d) in enumerate(((a0, d0), (a1, d1))):
            a, d = inclusive(a, d, True)
            bsums[s:s + 1, hh * D:(hh + 1) * D] = a[0:1, :]
            bsums[SEQS + s:SEQS + s + 1, hh * D:(hh + 1) * D] = d[0:1, :]
            bprefix.append(exclusive(a, d, True))
    for dz in range(1, nz):
        @pl.when(z - dz >= 0)
        def _():
            remote(bsums, bsums_in.at[z], b_send.at[dz], b_recv.at[z], (z - dz, b)).start()

    ag_left(OUT)
    def grad_out(q, carry):
        qs = pl.multiple_of(q * (H // nz), H // nz)
        v = st[:, :, pl.ds(qs, H // nz)].reshape(SEQS * span, H // nz)
        g = dot(v, db[...].reshape(SEQS * span, D), TN)
        wout[pl.ds(q, 1)] = g.astype(BF16).reshape((1,) + wout.shape[1:])
        return carry

    lax.fori_loop(0, nz, grad_out, 0)
    rs_start(OUT, 0)
    rs_next(UP, 1)
    rs_next(DOWN, 2)

    def leave_from(k, carry):
        i = nz - 1 - k
        remote(bsums, bsums_in.at[i], b_send.at[0], b_recv.at[i], pc).wait_recv()
        got = bsums_in[i]
        return got[0:SEQS] * carry + got[SEQS:2 * SEQS]

    leaving = lax.fori_loop(0, nz - 1 - z, leave_from, jnp.zeros((SEQS, H), F32))

    for s in range(SEQS):
        def body(k, carry):
            i = nj // 2 - 1 - k
            vals = list(carry)
            ds = two_low(s, i)
            gates, cands = [[None] * 2, [None] * 2], [[None] * 2, [None] * 2]
            for jj in (1, 0):
                u = two(upd, s, i * 2 + jj)
                q = two(cand, s, i * 2 + jj)
                for hh in range(2):
                    adj = ds[jj][hh] + vals[hh]
                    vals[hh] = (1.0 - u[hh]) * adj
                    gate = adj * q[hh]
                    vals[2 + hh] = vals[2 + hh] + gate
                    gates[hh][jj] = gate
                    cands[hh][jj] = adj * u[hh]
            at = pl.multiple_of(i * 2 * SUB, 2 * SUB)
            for hh in range(2):
                du[s, pl.ds(at, 2 * SUB), hh * D:(hh + 1) * D] = jnp.concatenate(gates[hh], axis=0).astype(BF16)
                du[s, pl.ds(at, 2 * SUB), H + hh * D:H + (hh + 1) * D] = jnp.concatenate(cands[hh], axis=0).astype(BF16)
            return tuple(vals)

        init = []
        for hh in range(2):
            ek, ed = bprefix[2 * s + hh]
            init.append(ek * leaving[s:s + 1, hh * D:(hh + 1) * D] + ed)
        zero = jnp.zeros((SUB, D), F32)
        done = lax.fori_loop(0, nj // 2, body, tuple(init) + (zero, zero), unroll=2)
        for hh in range(2):
            vgrad[:, 6 * D + hh * D:6 * D + (hh + 1) * D] += done[2 + hh]

    ag_left(UP)
    mix_all = mix[...].reshape(SEQS * span, D)
    for q in range(2 * H // D):
        g = dot(mix_all, whole(du, q * D, (q + 1) * D), TN)
        wup[:, :, :, :, :, q * D:(q + 1) * D] = g.astype(BF16).reshape(wup.shape[:5] + (D,))
    rs_next(UP, 2)
    for cpy in rs_copies(UP, 1):
        cpy.wait_send()
    pl.semaphore_signal(free_sem, inc=1, device_id=pc, device_id_type=MESH)
    pl.semaphore_wait(free_sem, 1)
    rs_start(IN, 0)
    rs_next(OUT, 1)
    rs_next(DOWN, 3)

    def back_project(s, carry):
        upd[s, 0:span] = dot(du[s], all_of(IN), NT)
        return carry

    lax.fori_loop(0, SEQS, back_project, 0)
    for s in range(SEQS):
        for i in range(3):
            r = 3 * s + i
            back_out[r:r + 1, :] = upd[s, i * SUB:i * SUB + 1, :]
    send_back = remote(back_out, back_in, h_sem.at[2], h_sem.at[3], (lax.rem(z + nz - 1, nz), b))
    send_back.start()
    rs_next(IN, 1)
    rs_next(OUT, 2)
    rs_next(UP, 3)
    send_back.wait_recv()
    for s in range(SEQS):
        for i in range(3):
            r = 3 * s + i
            tile = pltpu.roll(upd[s, i * SUB:(i + 1) * SUB, :], SUB - 1, 0)
            edge = jnp.where(z < nz - 1, back_in[r:r + 1, :], 0.0)
            upd[s, span + i * SUB:span + (i + 1) * SUB] = jnp.where(sub0 == SUB - 1, edge, tile)

    tok_load.wait()

    def back_norm(s, carry):
        unit, scale = unit_of(dot(perm[...], n2[s]))
        normed = (tiles(unit) * g_one).astype(BF16).astype(F32)
        d_normed = jnp.zeros((nj, SUB, D), F32)
        for k in range(4):
            ahead = tiles(upd[s, (3 - k) * SUB:(3 - k) * SUB + span])
            d_normed = d_normed + taps[k] * ahead
            vgrad[:, (2 + k) * D:(3 + k) * D] += jnp.sum(normed * ahead, axis=0)
        vgrad[:, 0:D] += jnp.sum(d_normed * tiles(unit), axis=0)
        e = flat(d_normed * g_one)
        out = mid[s] + scale * (e - unit * row_mean(e * unit))
        high = out.astype(BF16)
        rest_low = (out - high.astype(F32)).astype(BF16)
        mid[s] = dot(perm[...], high, TN) + dot(perm[...], rest_low, TN)
        return carry

    lax.fori_loop(0, SEQS, back_norm, 0)
    grad_store = pltpu.make_async_copy(mid, grad_hbm, io_sem.at[7])
    grad_store.start()

    def to_owner(i, carry):
        @pl.when(i != me)
        def _():
            src = vgrad.at[:, pl.ds(pl.multiple_of(i * LANES, LANES), LANES)]
            remote(src, vrecv.at[me], g_sem.at[0], g_sem.at[1], (i // 8, lax.rem(i, 8))).start()
        return carry

    lax.fori_loop(0, ndev, to_owner, 0)
    vrecv[me] = vgrad[:, pl.ds(pl.multiple_of(me * LANES, LANES), LANES)]
    rs_next(IN, 2)
    rs_next(OUT, 3)
    rs_next(DOWN, 4)
    rs_next(UP, 4)
    rs_next(IN, 3)
    rs_next(OUT, 4)
    many = vrecv.at[0:ndev - 1]
    remote(many, many, g_sem.at[0], g_sem.at[1], pc).wait_recv()
    sum_vec[...] = jnp.sum(jnp.sum(vrecv[...], axis=0), axis=0, keepdims=True)
    rs_next(IN, 4)

    for k in range(4):
        for stage in range(4):
            if (k, stage) != (UP, 1):
                for cpy in rs_copies(k, stage):
                    cpy.wait_send()
    ag_left(IN)
    ag_left(DOWN)
    remote(rest, rest, v_sem.at[0], v_sem.at[1], pc).wait_send()
    remote(many, many, g_sem.at[0], g_sem.at[1], pc).wait_send()
    send_halo.wait_send()
    send_back.wait_send()
    for dz in range(1, nz):
        @pl.when(z + dz < nz)
        def _():
            carry_copy(sums, sums_in, c_send, c_recv, dz).wait_send()

        @pl.when(z - dz >= 0)
        def _():
            remote(bsums, bsums_in.at[z], b_send.at[dz], b_recv.at[z], (z - dz, b)).wait_send()
    block_store.wait()
    grad_store.wait()


def adam_math(weight, grad, first, second, rate, decay):
    moment = BETA_ONE * first + (1.0 - BETA_ONE) * grad
    square = BETA_TWO * second + (1.0 - BETA_TWO) * grad * grad
    corr_one = 1.0 - BETA_ONE**STEP
    corr_two = 1.0 - BETA_TWO**STEP
    direction = moment / corr_one / (jnp.sqrt(square / corr_two) + ADAM_EPS)
    fresh = weight - rate * (direction + decay * weight)
    return fresh, moment, square


def adam_kernel(rates, *refs):
    ins, outs = refs[:20], refs[20:]
    at = 0
    for k in range(5):
        rate, decay = rates[k]
        w, g, m, v = (r[...] for r in ins[4 * k:4 * k + 4])
        fresh, moment, square = adam_math(w, g, m, v, rate, decay)
        outs[at][...] = fresh
        at += 1
        if k < 4:
            outs[at][...] = fresh.astype(BF16)
            at += 1
        outs[at][...] = moment
        outs[at + 1][...] = square
        at += 2


def fast_shards(nz, *args):
    (tokens, cotangent, start, lengths, w_in, w_out, w_up, w_down, vectors,
     m_in, v_in, m_out, v_out, m_up, v_up, m_down, v_down, m_vec, v_vec) = args
    span = tokens.shape[1]
    hbm = pl.BlockSpec(memory_space=pl.ANY)
    vmem = pl.BlockSpec(memory_space=pltpu.VMEM)
    smem = pl.BlockSpec(memory_space=pltpu.SMEM)
    rows = [w.shape[0] for w in (w_in, w_out, w_up, w_down)]
    cols = [w.shape[1] for w in (w_in, w_out, w_up, w_down)]
    vec_row = vectors.reshape(1, LANES)

    def S(*shape, dtype=F32):
        return jax.ShapeDtypeStruct(shape, dtype)

    def low(*shape):
        return pltpu.VMEM(shape, BF16)

    def wide(*shape):
        return pltpu.VMEM(shape, F32)

    dma = pltpu.SemaphoreType.DMA
    nsend = 5 + 2 * (nz - 1)
    ndev = nz * 8
    scratch = [
        low(SEQS, span, D), low(SEQS, span, D),
        *[low(nz, 2, 2, 2, r, n) for r, n in zip(rows, cols)],
        wide(SEQS, 2 * span, D), wide(SEQS, 2 * span, D),
        low(SEQS, span, H), low(SEQS, span, F), low(SEQS, span, F),
        low(SEQS, span, D), low(SEQS, span, D), wide(SEQS, span, D),
        low(nz, 2, 2, 2, rows[3], cols[3]), low(nz, 2, 2, 2, rows[2], cols[2]),
        *[low(nz, 2, 2, r, n) for r, n in zip(rows[1:], cols[1:])],
        *[low(nz, 2, r, n // 2) for r, n in zip(rows, cols) for _ in range(2)],
        *[low(nz, r, n // 2) for r, n in zip(rows, cols) for _ in range(2)],
        *[low(nz - 1, r, n // 2) for r, n in zip(rows, cols) for _ in range(2)],
        low(span, span), wide(span, LANES),
        wide(SUB, 8 * D), wide(SUB, 8 * D), wide(ndev, SUB, LANES),
        wide(16, D), wide(16, D), wide(16, D), wide(16, D),
        wide(SUB, H), wide(nz, SUB, H), wide(SUB, H), wide(nz, SUB, H),
        dma((8,)), dma((4, 8)), dma((4, 8)), dma((4, nsend)), dma((4, nsend)),
        dma((2,)), dma((4,)), dma((nz,)), dma((nz,)), dma((nz,)), dma((nz,)), dma((2,)), pltpu.SemaphoreType.REGULAR,
    ]
    block, ends, grad, s_in, s_out, s_up, s_down, s_vec = pl.pallas_call(
        functools.partial(step_kernel, nz, span),
        out_shape=[
            S(SEQS, span, D, dtype=BF16), S(SEQS, 1, H), S(SEQS, span, D),
            *[S(r, n) for r, n in zip(rows, cols)], S(1, LANES),
        ],
        in_specs=[hbm, hbm, vmem, smem, hbm, hbm, hbm, hbm, vmem],
        out_specs=[hbm, vmem, hbm, vmem, vmem, vmem, vmem, vmem],
        scratch_shapes=scratch,
        compiler_params=pltpu.CompilerParams(
            collective_id=0, has_side_effects=True, vmem_limit_bytes=64 * 2**20 - 2**18
        ),
    )(tokens, cotangent, start, lengths, w_in, w_out, w_up, w_down, vec_row)

    rates = ((D**-0.5, DECAY), (H**-0.5, DECAY), (D**-0.5, DECAY), (F**-0.5, DECAY), (VEC_RATE, 0.0))
    outs = []
    for k in range(4):
        outs += [S(rows[k], cols[k]), S(rows[k], cols[k], dtype=BF16), S(rows[k], cols[k]), S(rows[k], cols[k])]
    outs += [S(1, LANES)] * 3
    fresh = pl.pallas_call(
        functools.partial(adam_kernel, rates),
        out_shape=outs,
        in_specs=[vmem] * 20,
        out_specs=[vmem] * 19,
        compiler_params=pltpu.CompilerParams(vmem_limit_bytes=32 * 2**20),
    )(
        w_in, s_in, m_in, v_in, w_out, s_out, m_out, v_out, w_up, s_up, m_up, v_up,
        w_down, s_down, m_down, v_down,
        vec_row, s_vec, m_vec.reshape(1, LANES), v_vec.reshape(1, LANES),
    )
    return (block, ends, grad, *fresh[:16], *[v.reshape(LANES) for v in fresh[16:]])


def entering_2(value, axis, combine, identity, reverse):
    size, mine = (lax.axis_size(axis), lax.axis_index(axis))
    everything = jax.tree.map(lambda part: lax.all_gather(part, axis), value)
    start = jax.tree.map(
        lambda part, zero: jnp.broadcast_to(jnp.asarray(zero, part.dtype), part.shape),
        value,
        identity,
    )

    def step(k, before):
        at = size - 1 - k if reverse else k
        reached = at > mine if reverse else at < mine
        new = combine(before, jax.tree.map(lambda part: part[at], everything))
        return jax.tree.map(lambda a, b: jnp.where(reached, a, b), new, before)

    return lax.fori_loop(0, size, step, start)


def shifted_2(value, axis, by):
    size = lax.axis_size(axis)
    pairs = [(i, i + by) for i in range(size) if 0 <= i + by < size]
    return lax.ppermute(value, axis, pairs)


def combine_affine(earlier, later):
    return (earlier[0] * later[0], later[0] * earlier[1] + later[1])


def carry_forward(keep_total, drive_total):
    return entering_2(
        (keep_total, drive_total),
        "seq",
        combine_affine,
        (jnp.ones_like(keep_total), jnp.zeros_like(drive_total)),
        False,
    )


def carry_backward(keep_total, drive_total):
    return entering_2(
        (keep_total, drive_total),
        "seq",
        combine_affine,
        (jnp.ones_like(keep_total), jnp.zeros_like(drive_total)),
        True,
    )


def adam_step(weight, grad, first, second, rate, decay):
    moment = BETA_ONE * first + (1.0 - BETA_ONE) * grad
    square = BETA_TWO * second + (1.0 - BETA_TWO) * grad * grad
    corr_one = 1.0 - BETA_ONE**STEP
    corr_two = 1.0 - BETA_TWO**STEP
    direction = moment / corr_one / (jnp.sqrt(square / corr_two) + ADAM_EPS)
    fresh = weight - rate * (direction + decay * weight)
    return (fresh, moment, square)


def shards(
    tokens,
    cotangent,
    start_states,
    lengths,
    w_in,
    w_out,
    w_up,
    w_down,
    vectors,
    first_in,
    second_in,
    first_out,
    second_out,
    first_up,
    second_up,
    first_down,
    second_down,
    first_vec,
    second_vec,
):
    f32 = jnp.float32
    bf16 = jnp.bfloat16
    full_in, full_out, full_up, full_down, full_vec = (
        lax.all_gather(w_in.astype(bf16), ("seq", "batch"), axis=0, tiled=True),
        lax.all_gather(w_out.astype(bf16), ("seq", "batch"), axis=0, tiled=True),
        lax.all_gather(w_up.astype(bf16), ("seq", "batch"), axis=0, tiled=True),
        lax.all_gather(w_down.astype(bf16), ("seq", "batch"), axis=0, tiled=True),
        lax.all_gather(vectors.astype(bf16), ("seq", "batch"), axis=0, tiled=True),
    )
    vec_full = full_vec.astype(f32)
    g_one = vec_full[:D]
    g_two = vec_full[D : 2 * D]
    taps = vec_full[2 * D : 6 * D].reshape(4, D)
    bias = vec_full[6 * D :]
    span_len = tokens.shape[1]
    offset = lax.axis_index("seq") * span_len
    valid = ((offset + jnp.arange(span_len))[None, :] < lengths[:, None]).astype(f32)[..., None]
    inputs = tokens.astype(f32)
    scale_one = lax.rsqrt(jnp.mean(inputs * inputs, axis=-1, keepdims=True) + EPS)
    unit_one = inputs * scale_one
    normed = (unit_one * g_one).astype(bf16)
    rim_in = shifted_2(normed[:, span_len - 3 :, :], "seq", 1)
    extended = jnp.concatenate([rim_in, normed], axis=1).astype(f32)
    mixed = sum((taps[tap_idx] * extended[:, tap_idx : tap_idx + span_len] for tap_idx in range(4)))
    mixed_low = mixed.astype(bf16)
    projected = jnp.einsum("scd,dk->sck", mixed_low, full_in, preferred_element_type=f32)
    cand = projected[..., H:]
    gate_sig = jax.nn.sigmoid(projected[..., :H] + bias)
    update = gate_sig * valid
    retain = 1.0 - update
    driven = update * cand
    run_keep, run_drive = lax.associative_scan(combine_affine, (retain, driven), axis=1)
    enter_keep, enter_drive = carry_forward(run_keep[:, -1], run_drive[:, -1])
    entering = enter_keep * start_states + enter_drive
    states = run_keep * entering[:, None] + run_drive
    stretch_end = states[:, span_len - 1 :]
    state_low = states.astype(bf16)
    mixer = jnp.einsum("sch,hd->scd", state_low, full_out, preferred_element_type=f32)
    middle = inputs + valid * mixer
    scale_two = lax.rsqrt(jnp.mean(middle * middle, axis=-1, keepdims=True) + EPS)
    unit_two = middle * scale_two
    normed_two = (unit_two * g_two).astype(bf16)
    up_pre = jnp.einsum("scd,df->scf", normed_two, full_up, preferred_element_type=f32)
    gelu_out, gelu_pull = jax.vjp(jax.nn.gelu, up_pre)
    gelu_low = gelu_out.astype(bf16)
    branch = jnp.einsum("scf,fd->scd", gelu_low, full_down, preferred_element_type=f32)
    block_out = (middle + valid * branch).astype(bf16)
    grad_y = cotangent.astype(f32)
    d_branch = (grad_y * valid).astype(bf16)
    grad_down = jnp.einsum("scf,scd->fd", gelu_low, d_branch, preferred_element_type=f32)
    d_gelu = jnp.einsum("scd,fd->scf", d_branch, full_down, preferred_element_type=f32)
    d_up = gelu_pull(d_gelu)[0].astype(bf16)
    grad_up = jnp.einsum("scd,scf->df", normed_two, d_up, preferred_element_type=f32)
    d_normed_two = jnp.einsum("scf,df->scd", d_up, full_up, preferred_element_type=f32)
    grad_g_two = jnp.sum(d_normed_two * unit_two, axis=(0, 1))
    e_two = d_normed_two * g_two
    d_middle = grad_y + scale_two * (
        e_two - unit_two * jnp.mean(e_two * unit_two, axis=-1, keepdims=True)
    )
    d_mixer = (d_middle * valid).astype(bf16)
    grad_out = jnp.einsum("sch,scd->hd", state_low, d_mixer, preferred_element_type=f32)
    d_states = jnp.einsum("scd,hd->sch", d_mixer, full_out, preferred_element_type=f32)
    shifted = jnp.concatenate([retain[:, 1:], jnp.ones_like(retain[:, :1])], axis=1)
    back_keep, back_drive = lax.associative_scan(
        combine_affine, (shifted, d_states), axis=1, reverse=True
    )
    send_keep = retain[:, 0] * back_keep[:, 0]
    send_drive = retain[:, 0] * back_drive[:, 0]
    unused_keep, incoming = carry_backward(send_keep, send_drive)
    adjoint = back_keep * incoming[:, None] + back_drive
    prev_state = jnp.concatenate([entering[:, None], states[:, :-1]], axis=1)
    d_update = adjoint * (cand - prev_state)
    d_gate = d_update * valid * gate_sig * (1.0 - gate_sig)
    grad_bias = jnp.sum(d_gate, axis=(0, 1))
    gate_low = d_gate.astype(bf16)
    cand_low = (adjoint * update).astype(bf16)
    grad_in = jnp.concatenate(
        [
            jnp.einsum("scd,sck->dk", mixed_low, gate_low, preferred_element_type=f32),
            jnp.einsum("scd,sck->dk", mixed_low, cand_low, preferred_element_type=f32),
        ],
        axis=1,
    )
    d_mixed = jnp.einsum(
        "sck,dk->scd", gate_low, full_in[:, :H], preferred_element_type=f32
    ) + jnp.einsum("sck,dk->scd", cand_low, full_in[:, H:], preferred_element_type=f32)
    grad_taps = jnp.stack(
        [
            jnp.sum(d_mixed * extended[:, tap_idx : tap_idx + span_len], axis=(0, 1))
            for tap_idx in range(4)
        ]
    )
    rim_terms = jnp.stack(
        [
            sum((taps[tap_idx] * d_mixed[:, lead - tap_idx] for tap_idx in range(lead + 1)))
            for lead in range(3)
        ],
        axis=1,
    )
    mixed_tail = jnp.concatenate([d_mixed, jnp.zeros_like(d_mixed[:, :3])], axis=1)
    d_normed = sum(
        (
            taps[tap_idx] * mixed_tail[:, 3 - tap_idx : 3 - tap_idx + span_len]
            for tap_idx in range(4)
        )
    )
    rim_back = shifted_2(rim_terms, "seq", -1)
    d_normed = d_normed.at[:, span_len - 3 :].add(rim_back)
    grad_g_one = jnp.sum(d_normed * unit_one, axis=(0, 1))
    e_one = d_normed * g_one
    grad_tokens = d_middle + scale_one * (
        e_one - unit_one * jnp.mean(e_one * unit_one, axis=-1, keepdims=True)
    )
    grad_vec = jnp.concatenate([grad_g_one, grad_g_two, grad_taps.reshape(-1), grad_bias])
    sum_in, sum_out, sum_up, sum_down, sum_vec = (
        lax.psum_scatter(grad_in, ("seq", "batch"), scatter_dimension=0, tiled=True),
        lax.psum_scatter(grad_out, ("seq", "batch"), scatter_dimension=0, tiled=True),
        lax.psum_scatter(grad_up, ("seq", "batch"), scatter_dimension=0, tiled=True),
        lax.psum_scatter(grad_down, ("seq", "batch"), scatter_dimension=0, tiled=True),
        lax.psum_scatter(grad_vec, ("seq", "batch"), scatter_dimension=0, tiled=True),
    )
    new_in, moment_in, square_in = adam_step(w_in, sum_in, first_in, second_in, D ** (-0.5), DECAY)
    new_out, moment_out, square_out = adam_step(
        w_out, sum_out, first_out, second_out, H ** (-0.5), DECAY
    )
    new_up, moment_up, square_up = adam_step(w_up, sum_up, first_up, second_up, D ** (-0.5), DECAY)
    new_down, moment_down, square_down = adam_step(
        w_down, sum_down, first_down, second_down, F ** (-0.5), DECAY
    )
    new_vec, moment_vec, square_vec = adam_step(
        vectors, sum_vec, first_vec, second_vec, VEC_RATE, 0.0
    )
    return (
        block_out,
        stretch_end,
        grad_tokens,
        new_in,
        new_in.astype(bf16),
        moment_in,
        square_in,
        new_out,
        new_out.astype(bf16),
        moment_out,
        square_out,
        new_up,
        new_up.astype(bf16),
        moment_up,
        square_up,
        new_down,
        new_down.astype(bf16),
        moment_down,
        square_down,
        new_vec,
        moment_vec,
        square_vec,
    )


def solution(mesh):
    placed = (
        P("batch", "seq", None),
        P("batch", "seq", None),
        P("batch", None),
        P("batch"),
        P(("seq", "batch"), None),
        P(("seq", "batch"), None),
        P(("seq", "batch"), None),
        P(("seq", "batch"), None),
        P(("seq", "batch")),
        P(("seq", "batch"), None),
        P(("seq", "batch"), None),
        P(("seq", "batch"), None),
        P(("seq", "batch"), None),
        P(("seq", "batch"), None),
        P(("seq", "batch"), None),
        P(("seq", "batch"), None),
        P(("seq", "batch"), None),
        P(("seq", "batch")),
        P(("seq", "batch")),
    )
    nz, nb = mesh.shape["seq"], mesh.shape["batch"]
    fits = nb == 8 and nz == 4
    return jax.shard_map(
        functools.partial(fast_shards, nz) if fits else shards,
        mesh=mesh,
        in_specs=placed,
        out_specs=(
            P("batch", "seq", None),
            P("batch", "seq", None),
            P("batch", "seq", None),
            P(("seq", "batch"), None),
            P(("seq", "batch"), None),
            P(("seq", "batch"), None),
            P(("seq", "batch"), None),
            P(("seq", "batch"), None),
            P(("seq", "batch"), None),
            P(("seq", "batch"), None),
            P(("seq", "batch"), None),
            P(("seq", "batch"), None),
            P(("seq", "batch"), None),
            P(("seq", "batch"), None),
            P(("seq", "batch"), None),
            P(("seq", "batch"), None),
            P(("seq", "batch"), None),
            P(("seq", "batch"), None),
            P(("seq", "batch"), None),
            P(("seq", "batch")),
            P(("seq", "batch")),
            P(("seq", "batch")),
        ),
        check_vma=False,
    )
```

```python
import functools

import jax
import jax.numpy as jnp
from jax import lax
from jax.experimental import pallas as pl
from jax.experimental.pallas import tpu as pltpu
from jax.sharding import PartitionSpec as P

D = 512
H = 1024
F = 2048
STEP = 5
EPS = 1e-06
ADAM_EPS = 1e-08
BETA_ONE = 0.5
BETA_TWO = 0.5
DECAY = 0.1
VEC_RATE = 1.5
MESH = pl.DeviceIdType.MESH
F32 = jnp.float32
BF16 = jnp.bfloat16
SUB = 8
LANES = 128
SEQS = 3

NN = (((1,), (0,)), ((), ()))
NT = (((1,), (1,)), ((), ()))
TN = (((0,), (0,)), ((), ()))


def dot(a, b, dims=NN):
    return lax.dot_general(a, b, dims, preferred_element_type=F32)


def tiles(v):
    return v.reshape(v.shape[0] // SUB, SUB, v.shape[1])


def flat(v):
    return v.reshape(v.shape[0] * SUB, v.shape[2])


def fold(v):
    return jnp.sum(tiles(v), axis=0)


def row_mean(v):
    return jnp.mean(v, axis=-1, keepdims=True)


IN, OUT, UP, DOWN = range(4)

PIECES = ((IN, 0), (IN, 1), (OUT, 0), (UP, 0), (UP, 1), (DOWN, 0), (DOWN, 1))


def step_kernel(
    nz, span,
    tok_hbm, cot_hbm, start_ref, len_ref, w_in_hbm, w_out_hbm, w_up_hbm, w_down_hbm, vec_ref,
    block_hbm, ends_ref, grad_hbm, sum_in, sum_out, sum_up, sum_down, sum_vec,
    cp, mix, win, wout, wup, wdown, upd, cand, st, gl, du, n2, db, mid, gdown, gup,
    r0o, r0u, r0d, r1ai, r1bi, r1ao, r1bo, r1au, r1bu, r1ad, r1bd,
    r2ai, r2bi, r2ao, r2bo, r2au, r2bu, r2ad, r2bd,
    r3ai, r3bi, r3ao, r3bo, r3au, r3bu, r3ad, r3bd,
    perm, clock, vec, vec8, vgrad, vquad, vsum, vline, halo_in, back_out, back_in,
    sums0, sums1, sums_in0, sums_in1, bsums0, bsums1, bsums_in0, bsums_in1,
    io_sem, ag_send, ag_recv, rs_send, rs_recv, v_send, v_recv, g_send, g_recv, h_sem,
    c_send, c_recv, b_send, b_recv, free_sem,
):
    nj = span // SUB
    z = lax.axis_index("seq")
    b = lax.axis_index("batch")
    y, x, c = b // 4, lax.rem(b // 2, 2), lax.rem(b, 2)
    px, py, pc = (z, b + 2 - 4 * x), (z, b + 4 - 8 * y), (z, b + 1 - 2 * c)
    full = (win, wout, wup, wdown)
    masters = (w_in_hbm, w_out_hbm, w_up_hbm, w_down_hbm)
    staged = (sum_in, sum_out, sum_up, sum_down)

    def remote(src, dst, ssem, rsem, dev):
        return pltpu.make_async_remote_copy(
            src_ref=src, dst_ref=dst, send_sem=ssem, recv_sem=rsem, device_id=dev, device_id_type=MESH
        )

    def up_z(d):
        return (lax.rem(z + d, nz), b)

    def peer(d):
        return (z, lax.rem(b + d, 8))

    barrier = pltpu.get_barrier_semaphore()
    for dev in [up_z(d) for d in range(1, nz)] + [peer(d) for d in range(1, 8)]:
        pl.semaphore_signal(barrier, inc=1, device_id=dev, device_id_type=MESH)

    loads = [pltpu.make_async_copy(masters[k], staged[k], io_sem.at[k]) for k in range(4)]
    tok_load = pltpu.make_async_copy(tok_hbm, n2, io_sem.at[4])
    cot_load = pltpu.make_async_copy(cot_hbm, db, io_sem.at[5])
    for cpy in loads:
        cpy.start()
    tok_load.start()
    cot_load.start()

    vec[z, b] = jnp.broadcast_to(vec_ref[...].astype(BF16).astype(F32), (SUB, LANES))
    for k in range(4):
        loads[k].wait()
        full[k][z, y, x, c] = staged[k][...].astype(BF16)

    def piece_cols(k, h):
        w, part = PIECES[k]
        if w == IN:
            return slice(h * H + part * D, h * H + (part + 1) * D)
        if w == UP:
            return slice(part * H + h * D, part * H + (h + 1) * D)
        return slice(h * (D // 2), (h + 1) * (D // 2))

    def piece_rows(k):
        w, part = PIECES[k]
        n = full[w].shape[4]
        return slice(part * (n // 2), (part + 1) * (n // 2)) if w == DOWN else slice(0, n)

    def ag_copies(k, stage):
        ref, rws = full[PIECES[k][0]], piece_rows(k)
        out = []

        def add(at, sem, dev):
            out.append(remote(ref.at[at], ref.at[at], ag_send.at[k, sem], ag_recv.at[k, sem], dev))

        for h in range(2):
            n = piece_cols(k, h)
            if stage == 3:
                add((slice(None), slice(None), slice(None), c, rws, n), 10 + h, pc)
            elif stage == 0:
                for dz in range(1, nz):
                    add((z, y, x, c, rws, n), 3 * h + dz - 1, up_z(dz))
            elif stage == 1:
                add((slice(None), y, x, c, rws, n), 6 + h, (px, py)[h])
            else:
                at = (slice(None), y, slice(None), c, rws, n) if h == 0 else (slice(None), slice(None), x, c, rws, n)
                add(at, 8 + h, (py, px)[h])
        return out

    def ag(*events):
        for k, stage in events:
            if stage > 0:
                for cpy in ag_copies(k, stage - 1):
                    cpy.wait_recv()
            if stage < 4:
                for cpy in ag_copies(k, stage):
                    cpy.start()

    def ag_left(*weights):
        for k, (w, _) in enumerate(PIECES):
            if w in weights:
                for stage in range(4):
                    for cpy in ag_copies(k, stage):
                        cpy.wait_send()

    def vec_line(d):
        return remote(vec.at[z, b], vec.at[z, b], v_send.at[d - 1], v_recv.at[d - 1], up_z(d))

    def vec_peer(d):
        return remote(vec.at[:, b], vec.at[:, b], v_send.at[nz - 2 + d], v_recv.at[nz - 2 + d], peer(d))

    pl.semaphore_wait(barrier, nz - 1 + 7)
    for d in range(1, nz):
        vec_line(d).start()
    tok_load.wait()
    send_halo = remote(n2.at[:, span - 2 * SUB:span], halo_in, h_sem.at[0], h_sem.at[1], up_z(1))
    send_halo.start()
    ag((0, 0), (1, 0))

    rows = lax.broadcasted_iota(jnp.int32, (span, span), 0)
    cols = lax.broadcasted_iota(jnp.int32, (span, span), 1)
    perm[...] = jnp.where(cols == lax.rem(rows, SUB) * nj + rows // SUB, 1.0, 0.0).astype(BF16)
    vrow = lax.broadcasted_iota(jnp.int32, (span, LANES), 0)
    clock[...] = (lax.rem(vrow, SUB) * nj + vrow // SUB + z * span).astype(F32)

    def keep_of(s):
        one = jnp.where(clock[...] < len_ref[s].astype(F32), 1.0, 0.0)
        return jnp.concatenate([one] * (D // LANES), axis=1)

    for s in range(SEQS):
        gdown[s] = dot(perm[...], n2[s]).astype(BF16).reshape(gdown.shape[1:])
    for d in range(1, nz):
        vec_line(d).wait_recv()
    for d in range(1, 8):
        vec_peer(d).start()

    def unit_of(v):
        scale = lax.rsqrt(row_mean(v * v) + EPS)
        return v * scale, scale

    cot_load.wait()
    for s in range(SEQS):
        low = dot(perm[...], db[s])
        cp[s] = low.astype(BF16)
        db[s] = (low * keep_of(s)).astype(BF16)
    ag((0, 1), (2, 0))
    for d in range(1, 8):
        vec_peer(d).wait_recv()
    for i in range(nz * 8):
        vec8[:, i * LANES:(i + 1) * LANES] = vec[i // 8, i % 8]
    g_one = vec8[:, 0:D]
    g_two = vec8[:, D:2 * D]
    taps = [vec8[:, (2 + k) * D:(3 + k) * D] for k in range(4)]

    sub0 = lax.broadcasted_iota(jnp.int32, (SUB, D), 0)
    send_halo.wait_recv()
    for s in range(SEQS):
        unit, _ = unit_of(gdown[s].reshape(span, D).astype(F32))
        normed = (tiles(unit) * g_one).astype(BF16).astype(F32)
        upd[s, 3 * SUB:3 * SUB + span] = flat(normed)
        edges, _ = unit_of(halo_in[s].astype(F32))
        edges = (edges[SUB:2 * SUB] * g_one).astype(BF16).astype(F32)
        for i in range(3):
            tile = pltpu.roll(upd[s, span + i * SUB:span + (i + 1) * SUB, :], 1, 0)
            edge = jnp.where(z > 0, edges[SUB - 3 + i:SUB - 2 + i, :], 0.0)
            upd[s, i * SUB:(i + 1) * SUB] = jnp.where(sub0 == 0, edge, tile)
        total = taps[0] * tiles(upd[s, 0:span])
        for k in range(1, 4):
            total = total + taps[k] * tiles(upd[s, k * SUB:k * SUB + span])
        mix[s] = flat(total).astype(BF16)
        if s == 0:
            ag((1, 1), (3, 0))
        if s == 1:
            ag((0, 2))
    ag((2, 1), (4, 0), (1, 2), (3, 1), (5, 0), (0, 3), (2, 2), (0, 4))

    def cols_of(k, lo, hi):
        v = full[k][:, :, :, :, :, lo:hi]
        return v.reshape(v.shape[0] * 8 * v.shape[4], hi - lo)

    def all_of(k):
        v = full[k][...]
        return v.reshape(v.shape[0] * 8 * v.shape[4], v.shape[5])

    lane_sub = lax.broadcasted_iota(jnp.int32, (SUB, D), 0)

    def inclusive(keep, drive, reverse):
        for d in (1, 2, 4):
            by = SUB - d if reverse else d
            inside = lane_sub < SUB - d if reverse else lane_sub >= d
            k2 = jnp.where(inside, pltpu.roll(keep, by, 0), 1.0)
            d2 = jnp.where(inside, pltpu.roll(drive, by, 0), 0.0)
            drive = drive + keep * d2
            keep = keep * k2
        return keep, drive

    def exclusive(keep, drive, reverse):
        by = SUB - 1 if reverse else 1
        edge = lane_sub == (SUB - 1 if reverse else 0)
        return (
            jnp.where(edge, 1.0, pltpu.roll(keep, by, 0)),
            jnp.where(edge, 0.0, pltpu.roll(drive, by, 0)),
        )

    def tile_at(hh, j):
        return pl.ds(pl.multiple_of(j * SUB, SUB) + hh * span, SUB)

    def project(s, hh):
        bias = vec8[:, 6 * D + hh * D:6 * D + (hh + 1) * D]
        gate = tiles(dot(mix[s], cols_of(IN, hh * D, (hh + 1) * D))) + bias
        upd[s, hh * span:(hh + 1) * span] = flat(jax.nn.sigmoid(gate)) * keep_of(s)
        cand[s, hh * span:(hh + 1) * span] = dot(mix[s], cols_of(IN, H + hh * D, H + (hh + 1) * D))

    prefix = {}
    sums, sums_in = (sums0, sums1), (sums_in0, sums_in1)
    one, zero = jnp.ones((SUB, D), F32), jnp.zeros((SUB, D), F32)

    def totals(hh):
        def body(j, carry):
            out = []
            for s in range(SEQS):
                a, d = carry[2 * s], carry[2 * s + 1]
                u, v = upd[s, tile_at(hh, j), :], cand[s, tile_at(hh, j), :]
                out += [a * (1.0 - u), d + u * (v - d)]
            return tuple(out)

        got = lax.fori_loop(0, nj, body, (one, zero) * SEQS, unroll=4)
        for s in range(SEQS):
            a, d = inclusive(got[2 * s], got[2 * s + 1], False)
            sums[hh][s:s + 1, :] = a[SUB - 1:SUB, :]
            sums[hh][SEQS + s:SEQS + s + 1, :] = d[SUB - 1:SUB, :]
            prefix[s, hh] = exclusive(a, d, False)
        for dz in range(1, nz):
            @pl.when(z + dz < nz)
            def _():
                carry_copy(hh, dz).start()

    def carry_copy(hh, dz):
        return remote(sums[hh], sums_in[hh].at[z], c_send.at[hh, dz], c_recv.at[hh, z], (z + dz, b))

    def run_states(hh):
        def enter_from(i, carry):
            remote(sums[hh], sums_in[hh].at[i], c_send.at[hh, 0], c_recv.at[hh, i], pc).wait_recv()
            got = sums_in[hh][i]
            return got[0:SEQS] * carry + got[SEQS:2 * SEQS]

        entering = lax.fori_loop(0, z, enter_from, start_ref[:, hh * D:(hh + 1) * D])

        def body(i, carry):
            hs = list(carry)
            for s in range(SEQS):
                lows = []
                for jj in range(2):
                    j = i * 2 + jj
                    u, v = upd[s, tile_at(hh, j), :], cand[s, tile_at(hh, j), :]
                    moved = u * (v - hs[s])
                    hs[s] = hs[s] + moved
                    cand[s, tile_at(hh, j), :] = moved * (1.0 - u)
                    lows.append(hs[s])
                at = pl.multiple_of(i * 2 * SUB, 2 * SUB)
                st[s, pl.ds(at, 2 * SUB), hh * D:(hh + 1) * D] = jnp.concatenate(lows, axis=0).astype(BF16)
            return tuple(hs)

        init = []
        for s in range(SEQS):
            ek, ed = prefix[s, hh]
            init.append(ek * entering[s:s + 1] + ed)
        ended = lax.fori_loop(0, nj // 2, body, tuple(init), unroll=2)
        for s in range(SEQS):
            ends_ref[s, :, hh * D:(hh + 1) * D] = ended[s][SUB - 1:SUB, :]

    project(0, 0)
    ag((4, 1), (6, 0))
    project(1, 0)
    ag((1, 3))
    project(2, 0)
    totals(0)
    ag((3, 2), (5, 1), (1, 4))
    project(0, 1)
    project(1, 1)
    ag((2, 3))
    project(2, 1)
    totals(1)
    ag((6, 1), (4, 2), (2, 4))
    run_states(0)
    ag((3, 3))
    run_states(1)
    ag((5, 2), (3, 4))

    root = 0.7978845608028654
    cubic = 0.044715

    def ffn_in(s):
        middle = gdown[s].reshape(span, D).astype(F32) + keep_of(s) * dot(st[s], all_of(OUT))
        mid[s] = middle
        scale = lax.rsqrt(row_mean(middle * middle) + EPS)
        n2[s] = flat(tiles(middle * scale) * g_two).astype(BF16)

    def ffn_up(s, part):
        for q in (2 * part, 2 * part + 1):
            pre = dot(n2[s], cols_of(UP, q * D, (q + 1) * D))
            sq = pre * pre
            hp = 0.5 + 0.5 * jnp.tanh(pre * (root + (root * cubic) * sq))
            g = pre * hp
            gl[s, :, q * D:(q + 1) * D] = g.astype(BF16)
            slope = hp + (g * (1.0 - hp)) * (2.0 * root + (6.0 * root * cubic) * sq)
            du[s, :, q * D:(q + 1) * D] = slope.astype(BF16)

    def ffn_hidden_grad(s):
        for q in range(F // D):
            d_gelu = dot(db[s], wdown[q].reshape(F // nz, D), NT)
            at = (s, slice(None), slice(q * D, (q + 1) * D))
            du[at] = (du[at].astype(F32) * d_gelu).astype(BF16)

    send_halo.wait_send()
    ffn_in(0)
    ag((6, 2))
    ffn_in(1)
    ffn_in(2)
    ag((4, 3))
    ffn_up(0, 0)
    ffn_up(1, 0)
    ag((4, 4), (5, 3))
    ffn_up(2, 0)
    ffn_up(0, 1)
    ag((5, 4), (6, 3))
    ffn_up(1, 1)
    ffn_up(2, 1)
    ag((6, 4))
    for s in range(SEQS):
        ffn_hidden_grad(s)

    RS = ((DOWN, 0), (UP, 0), (OUT, 0), (IN, 0), (IN, 1))
    partial = (wup, wout, gup, gdown)
    r0 = (r0u, r0o, r0u, r0d)
    r1 = ((r1ai, r1bi), (r1ao, r1bo), (r1au, r1bu), (r1ad, r1bd))
    r2 = ((r2ai, r2bi), (r2ao, r2bo), (r2au, r2bu), (r2ad, r2bd))
    r3 = ((r3ai, r3bi), (r3ao, r3bo), (r3au, r3bu), (r3ad, r3bd))
    finals = (sum_in, sum_out, sum_up, sum_down)

    def wide_cols(r, h):
        w, part = RS[r]
        n = full[w].shape[5] // 2
        if w == IN:
            return slice(h * n + part * D, h * n + (part + 1) * D), slice(part * D, (part + 1) * D)
        return slice(h * n, (h + 1) * n), slice(0, n)

    def rs_copies(r, stage, halves=(0, 1)):
        w = RS[r][0]
        out = []
        for h in halves:
            n, m = wide_cols(r, h)

            def add(src, dst, sem, dev):
                out.append(remote(src, dst, rs_send.at[r, sem], rs_recv.at[r, sem], dev))

            if stage == 0:
                add(partial[w].at[:, :, :, 1 - c, :, n], r0[w].at[:, :, :, :, n], h, pc)
            elif stage == 1:
                src = r0[w].at[:, 1 - y, :, :, n] if h == 0 else r0[w].at[:, :, 1 - x, :, n]
                add(src, r1[w][h].at[:, :, :, m], 2 + h, (py, px)[h])
            elif stage == 2:
                away = 1 - x if h == 0 else 1 - y
                add(r1[w][h].at[:, away, :, m], r2[w][h].at[:, :, m], 4 + h, (px, py)[h])
            else:
                for dz in range(1, nz):
                    to = lax.rem(z + dz, nz)
                    add(r2[w][h].at[to, :, m], r3[w][h].at[dz - 1, :, m], 6 + 2 * (dz - 1) + h, (to, b))
        return out

    def rs_start(r):
        for cpy in rs_copies(r, 0):
            cpy.start()

    def rs_next(r, stage):
        w = RS[r][0]
        for h in range(2):
            n, m = wide_cols(r, h)
            for cpy in rs_copies(r, stage - 1, (h,)):
                cpy.wait_recv()
            if stage == 1:
                r0[w][:, :, :, :, n] = (
                    r0[w][:, :, :, :, n].astype(F32) + partial[w][:, :, :, c, :, n].astype(F32)
                ).astype(BF16)
            elif stage == 2:
                own = r0[w][:, y, :, :, n] if h == 0 else r0[w][:, :, x, :, n]
                r1[w][h][:, :, :, m] = (r1[w][h][:, :, :, m].astype(F32) + own.astype(F32)).astype(BF16)
            elif stage == 3:
                own = r1[w][h][:, x, :, m] if h == 0 else r1[w][h][:, y, :, m]
                r2[w][h][:, :, m] = (r2[w][h][:, :, m].astype(F32) + own.astype(F32)).astype(BF16)
            else:
                total = r2[w][h][z, :, m].astype(F32)
                for i in range(nz - 1):
                    total = total + r3[w][h][i, :, m].astype(F32)
                finals[w][:, n] = total
            if stage < 4:
                for cpy in rs_copies(r, stage, (h,)):
                    cpy.start()

    def whole(ref, lo, hi):
        v = ref[:, :, lo:hi]
        return v.reshape(SEQS * span, hi - lo)

    def everything(ref):
        return whole(ref, 0, ref.shape[2])

    RD, RU, RO, RI0, RI1 = range(5)

    def grad_rows(out, left, right, q):
        n = left.shape[2] // nz
        g = dot(whole(left, q * n, (q + 1) * n), everything(right), TN)
        out[q] = g.astype(BF16).reshape(out.shape[1:])

    def grad_cols(out, left, right, q):
        g = dot(everything(left), whole(right, q * D, (q + 1) * D), TN)
        out[:, :, :, :, :, q * D:(q + 1) * D] = g.astype(BF16).reshape(out.shape[:5] + (D,))

    vgrad[...] = jnp.zeros_like(vgrad)

    def vec_add(at, v):
        for i in range(v.shape[1] // LANES):
            t = at // LANES + i
            vgrad[t // 8, t % 8] += v[:, i * LANES:(i + 1) * LANES]

    for q in range(F // D):
        grad_cols(gup, n2, du, q)
    rs_start(RU)

    def ffn_back(s):
        keep = keep_of(s)
        middle = mid[s]
        gy = cp[s].astype(F32)
        scale = lax.rsqrt(row_mean(middle * middle) + EPS)
        unit = middle * scale
        n2[s] = middle.astype(BF16)
        d_low = dot(du[s], all_of(UP), NT)
        vec_add(D, fold(d_low * unit))
        e = flat(tiles(d_low) * g_two)
        d_middle = gy + scale * (e - unit * row_mean(e * unit))
        mid[s] = d_middle
        d_mixer = (d_middle * keep).astype(BF16)
        cp[s] = d_mixer
        du[s, :, 0:H] = dot(d_mixer, all_of(OUT), NT).astype(BF16)

    ffn_back(0)
    rs_next(RU, 1)
    ffn_back(1)
    ffn_back(2)

    bsums, bsums_in = (bsums0, bsums1), (bsums_in0, bsums_in1)
    bprefix = {}

    def two_low(s, hh, i):
        at = pl.multiple_of(i * 2 * SUB, 2 * SUB)
        v = du[s, pl.ds(at, 2 * SUB), hh * D:(hh + 1) * D].astype(F32)
        return v[0:SUB], v[SUB:2 * SUB]

    def back_totals(hh):
        def body(k, carry):
            i = nj // 2 - 1 - k
            vals = list(carry)
            for s in range(SEQS):
                ds = two_low(s, hh, i)
                for jj in (1, 0):
                    om = 1.0 - upd[s, tile_at(hh, i * 2 + jj), :]
                    vals[2 * s] = vals[2 * s] * om
                    vals[2 * s + 1] = om * (ds[jj] + vals[2 * s + 1])
            return tuple(vals)

        got = lax.fori_loop(0, nj // 2, body, (one, zero) * SEQS, unroll=2)
        for s in range(SEQS):
            a, d = inclusive(got[2 * s], got[2 * s + 1], True)
            bsums[hh][s:s + 1, :] = a[0:1, :]
            bsums[hh][SEQS + s:SEQS + s + 1, :] = d[0:1, :]
            bprefix[s, hh] = exclusive(a, d, True)
        for dz in range(1, nz):
            @pl.when(z - dz >= 0)
            def _():
                back_copy(hh, dz).start()

    def back_copy(hh, dz):
        return remote(bsums[hh], bsums_in[hh].at[z], b_send.at[hh, dz], b_recv.at[hh, z], (z - dz, b))

    def run_adjoint(hh):
        def leave_from(k, carry):
            i = nz - 1 - k
            remote(bsums[hh], bsums_in[hh].at[i], b_send.at[hh, 0], b_recv.at[hh, i], pc).wait_recv()
            got = bsums_in[hh][i]
            return got[0:SEQS] * carry + got[SEQS:2 * SEQS]

        leaving = lax.fori_loop(0, nz - 1 - z, leave_from, jnp.zeros((SEQS, D), F32))

        def body(k, carry):
            i = nj // 2 - 1 - k
            vals = list(carry)
            at = pl.multiple_of(i * 2 * SUB, 2 * SUB)
            for s in range(SEQS):
                ds = two_low(s, hh, i)
                gates, cands = [None] * 2, [None] * 2
                for jj in (1, 0):
                    u, q = upd[s, tile_at(hh, i * 2 + jj), :], cand[s, tile_at(hh, i * 2 + jj), :]
                    adj = ds[jj] + vals[2 * s]
                    vals[2 * s] = (1.0 - u) * adj
                    gates[jj] = adj * q
                    cands[jj] = adj * u
                    vals[2 * s + 1] = vals[2 * s + 1] + gates[jj]
                du[s, pl.ds(at, 2 * SUB), hh * D:(hh + 1) * D] = jnp.concatenate(gates, axis=0).astype(BF16)
                du[s, pl.ds(at, 2 * SUB), H + hh * D:H + (hh + 1) * D] = jnp.concatenate(cands, axis=0).astype(BF16)
            return tuple(vals)

        init = []
        for s in range(SEQS):
            ek, ed = bprefix[s, hh]
            init += [ek * leaving[s:s + 1] + ed, zero]
        done = lax.fori_loop(0, nj // 2, body, tuple(init), unroll=2)
        vec_add(6 * D + hh * D, done[1] + done[3] + done[5])

    back_totals(0)
    back_totals(1)
    rs_next(RU, 2)
    for q in range(nz):
        grad_rows(gdown, gl, db, q)
    rs_start(RD)
    tok_load = pltpu.make_async_copy(tok_hbm, db, io_sem.at[4])
    tok_load.start()
    run_adjoint(0)
    rs_next(RU, 3)
    run_adjoint(1)

    ag_left(UP, OUT)
    grad_cols(wup, mix, du, 0)
    grad_cols(wup, mix, du, 2)
    for cpy in rs_copies(RU, 1):
        cpy.wait_send()
    pl.semaphore_signal(free_sem, inc=1, device_id=pc, device_id_type=MESH)
    pl.semaphore_wait(free_sem, 1)
    rs_start(RI0)
    rs_next(RD, 1)
    grad_cols(wup, mix, du, 1)
    grad_cols(wup, mix, du, 3)
    rs_start(RI1)
    rs_next(RI0, 1)
    for q in range(nz):
        grad_rows(wout, st, cp, q)
    rs_start(RO)
    rs_next(RI1, 1)

    def back_project(s):
        upd[s, 0:span] = dot(du[s], all_of(IN), NT)
        for i in range(3):
            r = 3 * s + i
            back_out[r:r + 1, :] = upd[s, i * SUB:i * SUB + 1, :]

    back_project(0)
    rs_next(RD, 2)
    rs_next(RO, 1)
    back_project(1)
    rs_next(RI0, 2)
    back_project(2)
    send_back = remote(back_out, back_in, h_sem.at[2], h_sem.at[3], up_z(nz - 1))
    send_back.start()
    rs_next(RI1, 2)

    def ffn_out(s):
        block = (n2[s].astype(F32) + keep_of(s) * dot(gl[s], all_of(DOWN))).astype(BF16)
        n2[s] = dot(perm[...], block, TN).astype(BF16)

    ffn_out(0)
    rs_next(RD, 3)
    rs_next(RO, 2)
    ffn_out(1)
    rs_next(RI0, 3)
    ffn_out(2)
    block_store = pltpu.make_async_copy(n2, block_hbm, io_sem.at[6])
    block_store.start()
    send_back.wait_recv()
    rs_next(RI1, 3)
    tok_load.wait()

    def back_norm(s):
        for i in range(3):
            r = 3 * s + i
            tile = pltpu.roll(upd[s, i * SUB:(i + 1) * SUB, :], SUB - 1, 0)
            edge = jnp.where(z < nz - 1, back_in[r:r + 1, :], 0.0)
            upd[s, span + i * SUB:span + (i + 1) * SUB] = jnp.where(sub0 == SUB - 1, edge, tile)
        unit, scale = unit_of(dot(perm[...], db[s]))
        normed = (tiles(unit) * g_one).astype(BF16).astype(F32)
        d_normed = jnp.zeros((nj, SUB, D), F32)
        for k in range(4):
            ahead = tiles(upd[s, (3 - k) * SUB:(3 - k) * SUB + span])
            d_normed = d_normed + taps[k] * ahead
            vec_add((2 + k) * D, jnp.sum(normed * ahead, axis=0))
        vec_add(0, jnp.sum(d_normed * tiles(unit), axis=0))
        e = flat(d_normed * g_one)
        out = mid[s] + scale * (e - unit * row_mean(e * unit))
        high = out.astype(BF16)
        rest_low = (out - high.astype(F32)).astype(BF16)
        mid[s] = dot(perm[...], high, TN) + dot(perm[...], rest_low, TN)

    back_norm(0)
    rs_next(RD, 4)
    rs_next(RO, 3)
    back_norm(1)
    back_norm(2)

    def quad_copy(d):
        return remote(vgrad.at[:, lax.rem(b + d, 8)], vquad.at[d - 1], g_send.at[d - 1], g_recv.at[d - 1], peer(d))

    def line_copy(d):
        return remote(vsum.at[lax.rem(z + d, nz)], vline.at[d - 1], g_send.at[6 + d], g_recv.at[6 + d], up_z(d))

    for d in range(1, 8):
        quad_copy(d).start()
    grad_store = pltpu.make_async_copy(mid, grad_hbm, io_sem.at[7])
    grad_store.start()
    rs_next(RU, 4)
    rs_next(RI0, 4)
    for d in range(1, 8):
        quad_copy(d).wait_recv()
    vsum[...] = vgrad[:, b] + jnp.sum(vquad[...], axis=0)
    for d in range(1, nz):
        line_copy(d).start()
    rs_next(RO, 4)
    rs_next(RI1, 4)
    for d in range(1, nz):
        line_copy(d).wait_recv()
    sum_vec[...] = jnp.sum(vsum[z] + jnp.sum(vline[...], axis=0), axis=0, keepdims=True)

    ag_left(IN, DOWN)
    for r in range(5):
        for stage in range(4):
            if (r, stage) != (RU, 1):
                for cpy in rs_copies(r, stage):
                    cpy.wait_send()
    for d in range(1, nz):
        vec_line(d).wait_send()
        line_copy(d).wait_send()
    for d in range(1, 8):
        vec_peer(d).wait_send()
        quad_copy(d).wait_send()
    send_back.wait_send()
    for dz in range(1, nz):
        for hh in range(2):
            @pl.when(z + dz < nz)
            def _():
                carry_copy(hh, dz).wait_send()

            @pl.when(z - dz >= 0)
            def _():
                back_copy(hh, dz).wait_send()
    block_store.wait()
    grad_store.wait()


def adam_math(weight, grad, first, second, rate, decay):
    moment = BETA_ONE * first + (1.0 - BETA_ONE) * grad
    square = BETA_TWO * second + (1.0 - BETA_TWO) * grad * grad
    corr_one = 1.0 - BETA_ONE**STEP
    corr_two = 1.0 - BETA_TWO**STEP
    direction = moment / corr_one / (jnp.sqrt(square / corr_two) + ADAM_EPS)
    fresh = weight - rate * (direction + decay * weight)
    return fresh, moment, square


def adam_kernel(rates, *refs):
    ins, moved_in, outs, moved_out = refs[:20], refs[20:23], refs[23:42], refs[42:45]
    held, made, passing = refs[45:65], refs[65:84], refs[84:87]
    in_sem, out_sem, move_in_sem, move_out_sem = refs[87:]
    loads = [pltpu.make_async_copy(ins[i], held[i], in_sem.at[i]) for i in range(20)]
    parts = [(i, s) for i in range(3) for s in range(SEQS)]
    comes = [pltpu.make_async_copy(moved_in[i].at[s], passing[i].at[s], move_in_sem.at[i, s]) for i, s in parts]
    goes = [pltpu.make_async_copy(passing[i].at[s], moved_out[i].at[s], move_out_sem.at[i, s]) for i, s in parts]
    for cpy in loads:
        cpy.start()
    for cpy in comes:
        cpy.start()
    stores = []
    at = 0
    for k in range(5):
        rate, decay = rates[k]
        for cpy in loads[4 * k:4 * k + 4]:
            cpy.wait()
        w, g, m, v = (r[...] for r in held[4 * k:4 * k + 4])
        fresh, moment, square = adam_math(w, g, m, v, rate, decay)
        for out in (fresh, fresh.astype(BF16), moment, square) if k < 4 else (fresh, moment, square):
            made[at][...] = out
            stores.append(pltpu.make_async_copy(made[at], outs[at], out_sem.at[at]))
            stores[-1].start()
            at += 1
    for come, go in zip(comes, goes):
        come.wait()
        go.start()
    for cpy in stores + goes:
        cpy.wait()


def fast_shards(nz, *args):
    (tokens, cotangent, start, lengths, w_in, w_out, w_up, w_down, vectors,
     m_in, v_in, m_out, v_out, m_up, v_up, m_down, v_down, m_vec, v_vec) = args
    span = tokens.shape[1]
    hbm = pl.BlockSpec(memory_space=pl.ANY)
    vmem = pl.BlockSpec(memory_space=pltpu.VMEM)
    smem = pl.BlockSpec(memory_space=pltpu.SMEM)
    rows = [w.shape[0] for w in (w_in, w_out, w_up, w_down)]
    cols = [w.shape[1] for w in (w_in, w_out, w_up, w_down)]
    vec_row = vectors.reshape(1, LANES)

    def S(*shape, dtype=F32):
        return jax.ShapeDtypeStruct(shape, dtype)

    def low(*shape):
        return pltpu.VMEM(shape, BF16)

    def wide(*shape):
        return pltpu.VMEM(shape, F32)

    dma = pltpu.SemaphoreType.DMA
    nsend = 6 + 2 * (nz - 1)
    ndev = nz * 8
    scratch = [
        low(SEQS, span, D), low(SEQS, span, D),
        *[low(nz, 2, 2, 2, r, n) for r, n in zip(rows, cols)],
        wide(SEQS, 2 * span, D), wide(SEQS, 2 * span, D),
        low(SEQS, span, H), low(SEQS, span, F), low(SEQS, span, F),
        low(SEQS, span, D), low(SEQS, span, D), wide(SEQS, span, D),
        low(nz, 2, 2, 2, rows[3], cols[3]), low(nz, 2, 2, 2, rows[2], cols[2]),
        *[low(nz, 2, 2, r, n) for r, n in zip(rows[1:], cols[1:])],
        *[low(nz, 2, r, n // 2) for r, n in zip(rows, cols) for _ in range(2)],
        *[low(nz, r, n // 2) for r, n in zip(rows, cols) for _ in range(2)],
        *[low(nz - 1, r, n // 2) for r, n in zip(rows, cols) for _ in range(2)],
        low(span, span), wide(span, LANES),
        wide(nz, 8, SUB, LANES), wide(SUB, 8 * D), wide(nz, 8, SUB, LANES),
        wide(7, nz, SUB, LANES), wide(nz, SUB, LANES), wide(nz - 1, SUB, LANES),
        low(SEQS, 2 * SUB, D), wide(16, D), wide(16, D),
        *[wide(SUB, D), wide(SUB, D), wide(nz, SUB, D), wide(nz, SUB, D)] * 2,
        dma((8,)), dma((7, 12)), dma((7, 12)), dma((5, nsend)), dma((5, nsend)),
        dma((10,)), dma((10,)), dma((10,)), dma((10,)), dma((4,)),
        *[dma((2, nz)) for _ in range(4)], pltpu.SemaphoreType.REGULAR,
    ]
    block, ends, grad, s_in, s_out, s_up, s_down, s_vec = pl.pallas_call(
        functools.partial(step_kernel, nz, span),
        out_shape=[
            S(SEQS, span, D, dtype=BF16), S(SEQS, 1, H), S(SEQS, span, D),
            *[S(r, n) for r, n in zip(rows, cols)], S(1, LANES),
        ],
        in_specs=[hbm, hbm, vmem, smem, hbm, hbm, hbm, hbm, vmem],
        out_specs=[hbm, vmem, hbm, vmem, vmem, vmem, vmem, vmem],
        scratch_shapes=scratch,
        compiler_params=pltpu.CompilerParams(
            collective_id=0, has_side_effects=True, vmem_limit_bytes=64 * 2**20 - 2**18
        ),
    )(tokens, cotangent, start, lengths, w_in, w_out, w_up, w_down, vec_row)

    rates = ((D**-0.5, DECAY), (H**-0.5, DECAY), (D**-0.5, DECAY), (F**-0.5, DECAY), (VEC_RATE, 0.0))
    outs = []
    for k in range(4):
        outs += [S(rows[k], cols[k]), S(rows[k], cols[k], dtype=BF16), S(rows[k], cols[k]), S(rows[k], cols[k])]
    outs += [S(1, LANES)] * 3
    ins = (
        w_in, s_in, m_in, v_in, w_out, s_out, m_out, v_out, w_up, s_up, m_up, v_up,
        w_down, s_down, m_down, v_down,
        vec_row, s_vec, m_vec.reshape(1, LANES), v_vec.reshape(1, LANES),
    )
    moved = (block, ends, grad)
    fresh = pl.pallas_call(
        functools.partial(adam_kernel, rates),
        out_shape=outs + [S(*v.shape, dtype=v.dtype) for v in moved],
        in_specs=[hbm] * 23,
        out_specs=[hbm] * 22,
        scratch_shapes=[
            *[pltpu.VMEM(v.shape, F32) for v in ins], *[pltpu.VMEM(v.shape, v.dtype) for v in outs],
            *[pltpu.VMEM(v.shape, v.dtype) for v in moved],
            dma((20,)), dma((19,)), dma((3, SEQS)), dma((3, SEQS)),
        ],
        compiler_params=pltpu.CompilerParams(vmem_limit_bytes=63 * 2**20),
    )(*ins, *moved)
    block, ends, grad = fresh[19:]
    return (block, ends, grad, *fresh[:16], *[v.reshape(LANES) for v in fresh[16:19]])


def entering_2(value, axis, combine, identity, reverse):
    size, mine = (lax.axis_size(axis), lax.axis_index(axis))
    everything = jax.tree.map(lambda part: lax.all_gather(part, axis), value)
    start = jax.tree.map(
        lambda part, zero: jnp.broadcast_to(jnp.asarray(zero, part.dtype), part.shape),
        value,
        identity,
    )

    def step(k, before):
        at = size - 1 - k if reverse else k
        reached = at > mine if reverse else at < mine
        new = combine(before, jax.tree.map(lambda part: part[at], everything))
        return jax.tree.map(lambda a, b: jnp.where(reached, a, b), new, before)

    return lax.fori_loop(0, size, step, start)


def shifted_2(value, axis, by):
    size = lax.axis_size(axis)
    pairs = [(i, i + by) for i in range(size) if 0 <= i + by < size]
    return lax.ppermute(value, axis, pairs)


def combine_affine(earlier, later):
    return (earlier[0] * later[0], later[0] * earlier[1] + later[1])


def carry_forward(keep_total, drive_total):
    return entering_2(
        (keep_total, drive_total),
        "seq",
        combine_affine,
        (jnp.ones_like(keep_total), jnp.zeros_like(drive_total)),
        False,
    )


def carry_backward(keep_total, drive_total):
    return entering_2(
        (keep_total, drive_total),
        "seq",
        combine_affine,
        (jnp.ones_like(keep_total), jnp.zeros_like(drive_total)),
        True,
    )


def adam_step(weight, grad, first, second, rate, decay):
    moment = BETA_ONE * first + (1.0 - BETA_ONE) * grad
    square = BETA_TWO * second + (1.0 - BETA_TWO) * grad * grad
    corr_one = 1.0 - BETA_ONE**STEP
    corr_two = 1.0 - BETA_TWO**STEP
    direction = moment / corr_one / (jnp.sqrt(square / corr_two) + ADAM_EPS)
    fresh = weight - rate * (direction + decay * weight)
    return (fresh, moment, square)


def shards(
    tokens,
    cotangent,
    start_states,
    lengths,
    w_in,
    w_out,
    w_up,
    w_down,
    vectors,
    first_in,
    second_in,
    first_out,
    second_out,
    first_up,
    second_up,
    first_down,
    second_down,
    first_vec,
    second_vec,
):
    f32 = jnp.float32
    bf16 = jnp.bfloat16
    full_in, full_out, full_up, full_down, full_vec = (
        lax.all_gather(w_in.astype(bf16), ("seq", "batch"), axis=0, tiled=True),
        lax.all_gather(w_out.astype(bf16), ("seq", "batch"), axis=0, tiled=True),
        lax.all_gather(w_up.astype(bf16), ("seq", "batch"), axis=0, tiled=True),
        lax.all_gather(w_down.astype(bf16), ("seq", "batch"), axis=0, tiled=True),
        lax.all_gather(vectors.astype(bf16), ("seq", "batch"), axis=0, tiled=True),
    )
    vec_full = full_vec.astype(f32)
    g_one = vec_full[:D]
    g_two = vec_full[D : 2 * D]
    taps = vec_full[2 * D : 6 * D].reshape(4, D)
    bias = vec_full[6 * D :]
    span_len = tokens.shape[1]
    offset = lax.axis_index("seq") * span_len
    valid = ((offset + jnp.arange(span_len))[None, :] < lengths[:, None]).astype(f32)[..., None]
    inputs = tokens.astype(f32)
    scale_one = lax.rsqrt(jnp.mean(inputs * inputs, axis=-1, keepdims=True) + EPS)
    unit_one = inputs * scale_one
    normed = (unit_one * g_one).astype(bf16)
    rim_in = shifted_2(normed[:, span_len - 3 :, :], "seq", 1)
    extended = jnp.concatenate([rim_in, normed], axis=1).astype(f32)
    mixed = sum((taps[tap_idx] * extended[:, tap_idx : tap_idx + span_len] for tap_idx in range(4)))
    mixed_low = mixed.astype(bf16)
    projected = jnp.einsum("scd,dk->sck", mixed_low, full_in, preferred_element_type=f32)
    cand = projected[..., H:]
    gate_sig = jax.nn.sigmoid(projected[..., :H] + bias)
    update = gate_sig * valid
    retain = 1.0 - update
    driven = update * cand
    run_keep, run_drive = lax.associative_scan(combine_affine, (retain, driven), axis=1)
    enter_keep, enter_drive = carry_forward(run_keep[:, -1], run_drive[:, -1])
    entering = enter_keep * start_states + enter_drive
    states = run_keep * entering[:, None] + run_drive
    stretch_end = states[:, span_len - 1 :]
    state_low = states.astype(bf16)
    mixer = jnp.einsum("sch,hd->scd", state_low, full_out, preferred_element_type=f32)
    middle = inputs + valid * mixer
    scale_two = lax.rsqrt(jnp.mean(middle * middle, axis=-1, keepdims=True) + EPS)
    unit_two = middle * scale_two
    normed_two = (unit_two * g_two).astype(bf16)
    up_pre = jnp.einsum("scd,df->scf", normed_two, full_up, preferred_element_type=f32)
    gelu_out, gelu_pull = jax.vjp(jax.nn.gelu, up_pre)
    gelu_low = gelu_out.astype(bf16)
    branch = jnp.einsum("scf,fd->scd", gelu_low, full_down, preferred_element_type=f32)
    block_out = (middle + valid * branch).astype(bf16)
    grad_y = cotangent.astype(f32)
    d_branch = (grad_y * valid).astype(bf16)
    grad_down = jnp.einsum("scf,scd->fd", gelu_low, d_branch, preferred_element_type=f32)
    d_gelu = jnp.einsum("scd,fd->scf", d_branch, full_down, preferred_element_type=f32)
    d_up = gelu_pull(d_gelu)[0].astype(bf16)
    grad_up = jnp.einsum("scd,scf->df", normed_two, d_up, preferred_element_type=f32)
    d_normed_two = jnp.einsum("scf,df->scd", d_up, full_up, preferred_element_type=f32)
    grad_g_two = jnp.sum(d_normed_two * unit_two, axis=(0, 1))
    e_two = d_normed_two * g_two
    d_middle = grad_y + scale_two * (
        e_two - unit_two * jnp.mean(e_two * unit_two, axis=-1, keepdims=True)
    )
    d_mixer = (d_middle * valid).astype(bf16)
    grad_out = jnp.einsum("sch,scd->hd", state_low, d_mixer, preferred_element_type=f32)
    d_states = jnp.einsum("scd,hd->sch", d_mixer, full_out, preferred_element_type=f32)
    shifted = jnp.concatenate([retain[:, 1:], jnp.ones_like(retain[:, :1])], axis=1)
    back_keep, back_drive = lax.associative_scan(
        combine_affine, (shifted, d_states), axis=1, reverse=True
    )
    send_keep = retain[:, 0] * back_keep[:, 0]
    send_drive = retain[:, 0] * back_drive[:, 0]
    unused_keep, incoming = carry_backward(send_keep, send_drive)
    adjoint = back_keep * incoming[:, None] + back_drive
    prev_state = jnp.concatenate([entering[:, None], states[:, :-1]], axis=1)
    d_update = adjoint * (cand - prev_state)
    d_gate = d_update * valid * gate_sig * (1.0 - gate_sig)
    grad_bias = jnp.sum(d_gate, axis=(0, 1))
    gate_low = d_gate.astype(bf16)
    cand_low = (adjoint * update).astype(bf16)
    grad_in = jnp.concatenate(
        [
            jnp.einsum("scd,sck->dk", mixed_low, gate_low, preferred_element_type=f32),
            jnp.einsum("scd,sck->dk", mixed_low, cand_low, preferred_element_type=f32),
        ],
        axis=1,
    )
    d_mixed = jnp.einsum(
        "sck,dk->scd", gate_low, full_in[:, :H], preferred_element_type=f32
    ) + jnp.einsum("sck,dk->scd", cand_low, full_in[:, H:], preferred_element_type=f32)
    grad_taps = jnp.stack(
        [
            jnp.sum(d_mixed * extended[:, tap_idx : tap_idx + span_len], axis=(0, 1))
            for tap_idx in range(4)
        ]
    )
    rim_terms = jnp.stack(
        [
            sum((taps[tap_idx] * d_mixed[:, lead - tap_idx] for tap_idx in range(lead + 1)))
            for lead in range(3)
        ],
        axis=1,
    )
    mixed_tail = jnp.concatenate([d_mixed, jnp.zeros_like(d_mixed[:, :3])], axis=1)
    d_normed = sum(
        (
            taps[tap_idx] * mixed_tail[:, 3 - tap_idx : 3 - tap_idx + span_len]
            for tap_idx in range(4)
        )
    )
    rim_back = shifted_2(rim_terms, "seq", -1)
    d_normed = d_normed.at[:, span_len - 3 :].add(rim_back)
    grad_g_one = jnp.sum(d_normed * unit_one, axis=(0, 1))
    e_one = d_normed * g_one
    grad_tokens = d_middle + scale_one * (
        e_one - unit_one * jnp.mean(e_one * unit_one, axis=-1, keepdims=True)
    )
    grad_vec = jnp.concatenate([grad_g_one, grad_g_two, grad_taps.reshape(-1), grad_bias])
    sum_in, sum_out, sum_up, sum_down, sum_vec = (
        lax.psum_scatter(grad_in, ("seq", "batch"), scatter_dimension=0, tiled=True),
        lax.psum_scatter(grad_out, ("seq", "batch"), scatter_dimension=0, tiled=True),
        lax.psum_scatter(grad_up, ("seq", "batch"), scatter_dimension=0, tiled=True),
        lax.psum_scatter(grad_down, ("seq", "batch"), scatter_dimension=0, tiled=True),
        lax.psum_scatter(grad_vec, ("seq", "batch"), scatter_dimension=0, tiled=True),
    )
    new_in, moment_in, square_in = adam_step(w_in, sum_in, first_in, second_in, D ** (-0.5), DECAY)
    new_out, moment_out, square_out = adam_step(
        w_out, sum_out, first_out, second_out, H ** (-0.5), DECAY
    )
    new_up, moment_up, square_up = adam_step(w_up, sum_up, first_up, second_up, D ** (-0.5), DECAY)
    new_down, moment_down, square_down = adam_step(
        w_down, sum_down, first_down, second_down, F ** (-0.5), DECAY
    )
    new_vec, moment_vec, square_vec = adam_step(
        vectors, sum_vec, first_vec, second_vec, VEC_RATE, 0.0
    )
    return (
        block_out,
        stretch_end,
        grad_tokens,
        new_in,
        new_in.astype(bf16),
        moment_in,
        square_in,
        new_out,
        new_out.astype(bf16),
        moment_out,
        square_out,
        new_up,
        new_up.astype(bf16),
        moment_up,
        square_up,
        new_down,
        new_down.astype(bf16),
        moment_down,
        square_down,
        new_vec,
        moment_vec,
        square_vec,
    )


def solution(mesh):
    placed = (
        P("batch", "seq", None),
        P("batch", "seq", None),
        P("batch", None),
        P("batch"),
        P(("seq", "batch"), None),
        P(("seq", "batch"), None),
        P(("seq", "batch"), None),
        P(("seq", "batch"), None),
        P(("seq", "batch")),
        P(("seq", "batch"), None),
        P(("seq", "batch"), None),
        P(("seq", "batch"), None),
        P(("seq", "batch"), None),
        P(("seq", "batch"), None),
        P(("seq", "batch"), None),
        P(("seq", "batch"), None),
        P(("seq", "batch"), None),
        P(("seq", "batch")),
        P(("seq", "batch")),
    )
    nz, nb = mesh.shape["seq"], mesh.shape["batch"]
    fits = nb == 8 and nz == 4
    return jax.shard_map(
        functools.partial(fast_shards, nz) if fits else shards,
        mesh=mesh,
        in_specs=placed,
        out_specs=(
            P("batch", "seq", None),
            P("batch", "seq", None),
            P("batch", "seq", None),
            P(("seq", "batch"), None),
            P(("seq", "batch"), None),
            P(("seq", "batch"), None),
            P(("seq", "batch"), None),
            P(("seq", "batch"), None),
            P(("seq", "batch"), None),
            P(("seq", "batch"), None),
            P(("seq", "batch"), None),
            P(("seq", "batch"), None),
            P(("seq", "batch"), None),
            P(("seq", "batch"), None),
            P(("seq", "batch"), None),
            P(("seq", "batch"), None),
            P(("seq", "batch"), None),
            P(("seq", "batch"), None),
            P(("seq", "batch"), None),
            P(("seq", "batch")),
            P(("seq", "batch")),
            P(("seq", "batch")),
        ),
        check_vma=False,
    )
```

```python
import functools

import jax
import jax.numpy as jnp
from jax import lax
from jax.experimental import pallas as pl
from jax.experimental.pallas import tpu as pltpu
from jax.sharding import PartitionSpec as P

D = 512
H = 1024
F = 2048
STEP = 5
EPS = 1e-06
ADAM_EPS = 1e-08
BETA_ONE = 0.5
BETA_TWO = 0.5
DECAY = 0.1
VEC_RATE = 1.5
MESH = pl.DeviceIdType.MESH
F32 = jnp.float32
BF16 = jnp.bfloat16
SUB = 8
LANES = 128
SEQS = 3

NN = (((1,), (0,)), ((), ()))
NT = (((1,), (1,)), ((), ()))
TN = (((0,), (0,)), ((), ()))


def dot(a, b, dims=NN):
    return lax.dot_general(a, b, dims, preferred_element_type=F32)


def tiles(v):
    return v.reshape(v.shape[0] // SUB, SUB, v.shape[1])


def flat(v):
    return v.reshape(v.shape[0] * SUB, v.shape[2])


def fold(v):
    return jnp.sum(tiles(v), axis=0)


def row_mean(v):
    return jnp.mean(v, axis=-1, keepdims=True)


IN, OUT, UP, DOWN = range(4)

PIECES = ((IN, 0), (IN, 1), (OUT, 0), (UP, 0), (UP, 1), (DOWN, 0), (DOWN, 1))


def step_kernel(
    nz, span,
    tok_hbm, cot_hbm, start_ref, len_ref, w_in_hbm, w_out_hbm, w_up_hbm, w_down_hbm, vec_ref,
    block_hbm, ends_ref, grad_hbm, sum_in, sum_out, sum_up, sum_down, sum_vec,
    cp, mix, win, wout, wup, wdown, upd, cand, st, gl, du, n2, db, mid, gdown, gup,
    r0o, r0u, r0d, r1ai, r1bi, r1ao, r1bo, r1au, r1bu, r1ad, r1bd,
    r2ai, r2bi, r2ao, r2bo, r2au, r2bu, r2ad, r2bd,
    r3ai, r3bi, r3ao, r3bo, r3au, r3bu, r3ad, r3bd,
    perm, clock, vec, vec8, vgrad, vquad, vsum, vline, halo_in, back_out, back_in,
    sums0, sums1, sums_in0, sums_in1, bsums0, bsums1, bsums_in0, bsums_in1,
    io_sem, ag_send, ag_recv, rs_send, rs_recv, v_send, v_recv, g_send, g_recv, h_sem,
    c_send, c_recv, b_send, b_recv, free_sem,
):
    nj = span // SUB
    z = lax.axis_index("seq")
    b = lax.axis_index("batch")
    y, x, c = b // 4, lax.rem(b // 2, 2), lax.rem(b, 2)
    px, py, pc = (z, b + 2 - 4 * x), (z, b + 4 - 8 * y), (z, b + 1 - 2 * c)
    full = (win, wout, wup, wdown)
    masters = (w_in_hbm, w_out_hbm, w_up_hbm, w_down_hbm)
    staged = (sum_in, sum_out, sum_up, sum_down)

    def remote(src, dst, ssem, rsem, dev):
        return pltpu.make_async_remote_copy(
            src_ref=src, dst_ref=dst, send_sem=ssem, recv_sem=rsem, device_id=dev, device_id_type=MESH
        )

    def up_z(d):
        return (lax.rem(z + d, nz), b)

    def peer(d):
        return (z, lax.rem(b + d, 8))

    barrier = pltpu.get_barrier_semaphore()
    for dev in [up_z(d) for d in range(1, nz)] + [peer(d) for d in range(1, 8)]:
        pl.semaphore_signal(barrier, inc=1, device_id=dev, device_id_type=MESH)

    loads = [pltpu.make_async_copy(masters[k], staged[k], io_sem.at[k]) for k in range(4)]
    tok_load = pltpu.make_async_copy(tok_hbm, n2, io_sem.at[4])
    cot_load = pltpu.make_async_copy(cot_hbm, db, io_sem.at[5])
    for cpy in loads:
        cpy.start()
    tok_load.start()
    cot_load.start()

    vec[z, b] = jnp.broadcast_to(vec_ref[...].astype(BF16).astype(F32), (SUB, LANES))
    for k in range(4):
        loads[k].wait()
        full[k][z, y, x, c] = staged[k][...].astype(BF16)

    def piece_cols(k, h):
        w, part = PIECES[k]
        if w == IN:
            return slice(h * H + part * D, h * H + (part + 1) * D)
        if w == UP:
            return slice(part * H + h * D, part * H + (h + 1) * D)
        return slice(h * (D // 2), (h + 1) * (D // 2))

    def piece_rows(k):
        w, part = PIECES[k]
        n = full[w].shape[4]
        return slice(part * (n // 2), (part + 1) * (n // 2)) if w == DOWN else slice(0, n)

    def ag_copies(k, stage):
        ref, rws = full[PIECES[k][0]], piece_rows(k)
        out = []

        def add(at, sem, dev):
            out.append(remote(ref.at[at], ref.at[at], ag_send.at[k, sem], ag_recv.at[k, sem], dev))

        for h in range(2):
            n = piece_cols(k, h)
            if stage == 3:
                add((slice(None), slice(None), slice(None), c, rws, n), 10 + h, pc)
            elif stage == 0:
                for dz in range(1, nz):
                    add((z, y, x, c, rws, n), 3 * h + dz - 1, up_z(dz))
            elif stage == 1:
                add((slice(None), y, x, c, rws, n), 6 + h, (px, py)[h])
            else:
                at = (slice(None), y, slice(None), c, rws, n) if h == 0 else (slice(None), slice(None), x, c, rws, n)
                add(at, 8 + h, (py, px)[h])
        return out

    def ag(*events):
        for k, stage in events:
            if stage > 0:
                for cpy in ag_copies(k, stage - 1):
                    cpy.wait_recv()
            if stage < 4:
                for cpy in ag_copies(k, stage):
                    cpy.start()

    def ag_left(*weights):
        for k, (w, _) in enumerate(PIECES):
            if w in weights:
                for stage in range(4):
                    for cpy in ag_copies(k, stage):
                        cpy.wait_send()

    def vec_line(d):
        return remote(vec.at[z, b], vec.at[z, b], v_send.at[d - 1], v_recv.at[d - 1], up_z(d))

    def vec_peer(d):
        return remote(vec.at[:, b], vec.at[:, b], v_send.at[nz - 2 + d], v_recv.at[nz - 2 + d], peer(d))

    pl.semaphore_wait(barrier, nz - 1 + 7)
    for d in range(1, nz):
        vec_line(d).start()
    tok_load.wait()
    send_halo = remote(n2.at[:, span - 2 * SUB:span], halo_in, h_sem.at[0], h_sem.at[1], up_z(1))
    send_halo.start()
    ag((0, 0), (1, 0))

    rows = lax.broadcasted_iota(jnp.int32, (span, span), 0)
    cols = lax.broadcasted_iota(jnp.int32, (span, span), 1)
    perm[...] = jnp.where(cols == lax.rem(rows, SUB) * nj + rows // SUB, 1.0, 0.0).astype(BF16)
    vrow = lax.broadcasted_iota(jnp.int32, (span, LANES), 0)
    clock[...] = (lax.rem(vrow, SUB) * nj + vrow // SUB + z * span).astype(F32)

    def keep_of(s):
        one = jnp.where(clock[...] < len_ref[s].astype(F32), 1.0, 0.0)
        return jnp.concatenate([one] * (D // LANES), axis=1)

    for s in range(SEQS):
        gdown[s] = dot(perm[...], n2[s]).astype(BF16).reshape(gdown.shape[1:])
    for d in range(1, nz):
        vec_line(d).wait_recv()
    for d in range(1, 8):
        vec_peer(d).start()

    def unit_of(v):
        scale = lax.rsqrt(row_mean(v * v) + EPS)
        return v * scale, scale

    cot_load.wait()
    for s in range(SEQS):
        low = dot(perm[...], db[s])
        cp[s] = low.astype(BF16)
        db[s] = (low * keep_of(s)).astype(BF16)
    ag((0, 1), (2, 0))
    for d in range(1, 8):
        vec_peer(d).wait_recv()
    for i in range(nz * 8):
        vec8[:, i * LANES:(i + 1) * LANES] = vec[i // 8, i % 8]
    g_one = vec8[:, 0:D]
    g_two = vec8[:, D:2 * D]
    taps = [vec8[:, (2 + k) * D:(3 + k) * D] for k in range(4)]

    sub0 = lax.broadcasted_iota(jnp.int32, (SUB, D), 0)
    send_halo.wait_recv()
    for s in range(SEQS):
        unit, _ = unit_of(gdown[s].reshape(span, D).astype(F32))
        normed = (tiles(unit) * g_one).astype(BF16).astype(F32)
        upd[s, 3 * SUB:3 * SUB + span] = flat(normed)
        edges, _ = unit_of(halo_in[s].astype(F32))
        edges = (edges[SUB:2 * SUB] * g_one).astype(BF16).astype(F32)
        for i in range(3):
            tile = pltpu.roll(upd[s, span + i * SUB:span + (i + 1) * SUB, :], 1, 0)
            edge = jnp.where(z > 0, edges[SUB - 3 + i:SUB - 2 + i, :], 0.0)
            upd[s, i * SUB:(i + 1) * SUB] = jnp.where(sub0 == 0, edge, tile)
        total = taps[0] * tiles(upd[s, 0:span])
        for k in range(1, 4):
            total = total + taps[k] * tiles(upd[s, k * SUB:k * SUB + span])
        mix[s] = flat(total).astype(BF16)
        if s == 0:
            ag((1, 1), (3, 0))
        if s == 1:
            ag((0, 2))
    ag((2, 1), (4, 0), (1, 2), (3, 1), (5, 0), (0, 3), (2, 2), (0, 4))

    def cols_of(k, lo, hi):
        v = full[k][:, :, :, :, :, lo:hi]
        return v.reshape(v.shape[0] * 8 * v.shape[4], hi - lo)

    def all_of(k):
        v = full[k][...]
        return v.reshape(v.shape[0] * 8 * v.shape[4], v.shape[5])

    lane_sub = lax.broadcasted_iota(jnp.int32, (SUB, D), 0)

    def inclusive(keep, drive, reverse):
        for d in (1, 2, 4):
            by = SUB - d if reverse else d
            inside = lane_sub < SUB - d if reverse else lane_sub >= d
            k2 = jnp.where(inside, pltpu.roll(keep, by, 0), 1.0)
            d2 = jnp.where(inside, pltpu.roll(drive, by, 0), 0.0)
            drive = drive + keep * d2
            keep = keep * k2
        return keep, drive

    def exclusive(keep, drive, reverse):
        by = SUB - 1 if reverse else 1
        edge = lane_sub == (SUB - 1 if reverse else 0)
        return (
            jnp.where(edge, 1.0, pltpu.roll(keep, by, 0)),
            jnp.where(edge, 0.0, pltpu.roll(drive, by, 0)),
        )

    def tile_at(hh, j):
        return pl.ds(pl.multiple_of(j * SUB, SUB) + hh * span, SUB)

    def project(s, hh):
        bias = vec8[:, 6 * D + hh * D:6 * D + (hh + 1) * D]
        gate = tiles(dot(mix[s], cols_of(IN, hh * D, (hh + 1) * D))) + bias
        upd[s, hh * span:(hh + 1) * span] = flat(jax.nn.sigmoid(gate)) * keep_of(s)
        cand[s, hh * span:(hh + 1) * span] = dot(mix[s], cols_of(IN, H + hh * D, H + (hh + 1) * D))

    prefix = {}
    sums, sums_in = (sums0, sums1), (sums_in0, sums_in1)
    one, zero = jnp.ones((SUB, D), F32), jnp.zeros((SUB, D), F32)

    def totals(hh):
        def body(j, carry):
            out = []
            for s in range(SEQS):
                a, d = carry[2 * s], carry[2 * s + 1]
                u, v = upd[s, tile_at(hh, j), :], cand[s, tile_at(hh, j), :]
                out += [a * (1.0 - u), d + u * (v - d)]
            return tuple(out)

        got = lax.fori_loop(0, nj, body, (one, zero) * SEQS, unroll=4)
        for s in range(SEQS):
            a, d = inclusive(got[2 * s], got[2 * s + 1], False)
            sums[hh][s:s + 1, :] = a[SUB - 1:SUB, :]
            sums[hh][SEQS + s:SEQS + s + 1, :] = d[SUB - 1:SUB, :]
            prefix[s, hh] = exclusive(a, d, False)
        for dz in range(1, nz):
            @pl.when(z + dz < nz)
            def _():
                carry_copy(hh, dz).start()

    def carry_copy(hh, dz):
        return remote(sums[hh], sums_in[hh].at[z], c_send.at[hh, dz], c_recv.at[hh, z], (z + dz, b))

    def run_states(hh):
        def enter_from(i, carry):
            remote(sums[hh], sums_in[hh].at[i], c_send.at[hh, 0], c_recv.at[hh, i], pc).wait_recv()
            got = sums_in[hh][i]
            return got[0:SEQS] * carry + got[SEQS:2 * SEQS]

        entering = lax.fori_loop(0, z, enter_from, start_ref[:, hh * D:(hh + 1) * D])

        def body(i, carry):
            hs = list(carry)
            for s in range(SEQS):
                lows = []
                for jj in range(2):
                    j = i * 2 + jj
                    u, v = upd[s, tile_at(hh, j), :], cand[s, tile_at(hh, j), :]
                    moved = u * (v - hs[s])
                    hs[s] = hs[s] + moved
                    cand[s, tile_at(hh, j), :] = moved * (1.0 - u)
                    lows.append(hs[s])
                at = pl.multiple_of(i * 2 * SUB, 2 * SUB)
                st[s, pl.ds(at, 2 * SUB), hh * D:(hh + 1) * D] = jnp.concatenate(lows, axis=0).astype(BF16)
            return tuple(hs)

        init = []
        for s in range(SEQS):
            ek, ed = prefix[s, hh]
            init.append(ek * entering[s:s + 1] + ed)
        ended = lax.fori_loop(0, nj // 2, body, tuple(init), unroll=2)
        for s in range(SEQS):
            ends_ref[s, :, hh * D:(hh + 1) * D] = ended[s][SUB - 1:SUB, :]

    project(0, 0)
    ag((4, 1), (6, 0))
    project(1, 0)
    ag((1, 3))
    project(2, 0)
    totals(0)
    ag((3, 2), (5, 1), (1, 4))
    project(0, 1)
    project(1, 1)
    ag((2, 3))
    project(2, 1)
    totals(1)
    ag((6, 1), (4, 2), (2, 4))
    run_states(0)
    ag((3, 3))
    run_states(1)
    ag((5, 2), (3, 4))

    root = 0.7978845608028654
    cubic = 0.044715

    def ffn_in(s):
        middle = gdown[s].reshape(span, D).astype(F32) + keep_of(s) * dot(st[s], all_of(OUT))
        mid[s] = middle
        scale = lax.rsqrt(row_mean(middle * middle) + EPS)
        n2[s] = flat(tiles(middle * scale) * g_two).astype(BF16)

    def ffn_up(s, part):
        for q in (2 * part, 2 * part + 1):
            pre = dot(n2[s], cols_of(UP, q * D, (q + 1) * D))
            sq = pre * pre
            hp = 0.5 + 0.5 * jnp.tanh(pre * (root + (root * cubic) * sq))
            g = pre * hp
            gl[s, :, q * D:(q + 1) * D] = g.astype(BF16)
            slope = hp + (g * (1.0 - hp)) * (2.0 * root + (6.0 * root * cubic) * sq)
            du[s, :, q * D:(q + 1) * D] = slope.astype(BF16)

    def ffn_hidden_grad(s):
        for q in range(F // D):
            d_gelu = dot(db[s], wdown[q].reshape(F // nz, D), NT)
            at = (s, slice(None), slice(q * D, (q + 1) * D))
            du[at] = (du[at].astype(F32) * d_gelu).astype(BF16)

    RS = ((DOWN, 0), (UP, 0), (OUT, 0), (IN, 0), (IN, 1))
    partial = (wup, wout, gup, gdown)
    r0 = (r0u, r0o, r0u, r0d)
    r1 = ((r1ai, r1bi), (r1ao, r1bo), (r1au, r1bu), (r1ad, r1bd))
    r2 = ((r2ai, r2bi), (r2ao, r2bo), (r2au, r2bu), (r2ad, r2bd))
    r3 = ((r3ai, r3bi), (r3ao, r3bo), (r3au, r3bu), (r3ad, r3bd))
    finals = (sum_in, sum_out, sum_up, sum_down)

    def wide_cols(r, h):
        w, part = RS[r]
        n = full[w].shape[5] // 2
        if w == IN:
            return slice(h * n + part * D, h * n + (part + 1) * D), slice(part * D, (part + 1) * D)
        return slice(h * n, (h + 1) * n), slice(0, n)

    def rs_copies(r, stage, halves=(0, 1)):
        w = RS[r][0]
        out = []
        for h in halves:
            n, m = wide_cols(r, h)

            def add(src, dst, sem, dev):
                out.append(remote(src, dst, rs_send.at[r, sem], rs_recv.at[r, sem], dev))

            if stage == 0:
                add(partial[w].at[:, :, :, 1 - c, :, n], r0[w].at[:, :, :, :, n], h, pc)
            elif stage == 1:
                src = r0[w].at[:, 1 - y, :, :, n] if h == 0 else r0[w].at[:, :, 1 - x, :, n]
                add(src, r1[w][h].at[:, :, :, m], 2 + h, (py, px)[h])
            elif stage == 2:
                away = 1 - x if h == 0 else 1 - y
                add(r1[w][h].at[:, away, :, m], r2[w][h].at[:, :, m], 4 + h, (px, py)[h])
            else:
                for dz in range(1, nz):
                    to = lax.rem(z + dz, nz)
                    add(r2[w][h].at[to, :, m], r3[w][h].at[dz - 1, :, m], 6 + 2 * (dz - 1) + h, (to, b))
        return out

    def rs_start(r):
        for cpy in rs_copies(r, 0):
            cpy.start()

    def rs_next(r, stage):
        w = RS[r][0]
        for h in range(2):
            n, m = wide_cols(r, h)
            for cpy in rs_copies(r, stage - 1, (h,)):
                cpy.wait_recv()
            if stage == 1:
                r0[w][:, :, :, :, n] = (
                    r0[w][:, :, :, :, n].astype(F32) + partial[w][:, :, :, c, :, n].astype(F32)
                ).astype(BF16)
            elif stage == 2:
                own = r0[w][:, y, :, :, n] if h == 0 else r0[w][:, :, x, :, n]
                r1[w][h][:, :, :, m] = (r1[w][h][:, :, :, m].astype(F32) + own.astype(F32)).astype(BF16)
            elif stage == 3:
                own = r1[w][h][:, x, :, m] if h == 0 else r1[w][h][:, y, :, m]
                r2[w][h][:, :, m] = (r2[w][h][:, :, m].astype(F32) + own.astype(F32)).astype(BF16)
            else:
                total = r2[w][h][z, :, m].astype(F32)
                for i in range(nz - 1):
                    total = total + r3[w][h][i, :, m].astype(F32)
                finals[w][:, n] = total
            if stage < 4:
                for cpy in rs_copies(r, stage, (h,)):
                    cpy.start()

    def whole(ref, lo, hi):
        v = ref[:, :, lo:hi]
        return v.reshape(SEQS * span, hi - lo)

    def everything(ref):
        return whole(ref, 0, ref.shape[2])

    RD, RU, RO, RI0, RI1 = range(5)

    def grad_rows(out, left, right, q):
        n = left.shape[2] // nz
        g = dot(whole(left, q * n, (q + 1) * n), everything(right), TN)
        out[q] = g.astype(BF16).reshape(out.shape[1:])

    def grad_cols(out, left, right, q):
        g = dot(everything(left), whole(right, q * D, (q + 1) * D), TN)
        out[:, :, :, :, :, q * D:(q + 1) * D] = g.astype(BF16).reshape(out.shape[:5] + (D,))

    vgrad[...] = jnp.zeros_like(vgrad)

    def vec_add(at, v):
        for i in range(v.shape[1] // LANES):
            t = at // LANES + i
            vgrad[t // 8, t % 8] += v[:, i * LANES:(i + 1) * LANES]

    send_halo.wait_send()
    ffn_in(0)
    ag((6, 2))
    ffn_in(1)
    ffn_in(2)
    ag((4, 3))
    ffn_up(0, 0)
    ffn_up(1, 0)
    ag((4, 4), (5, 3))
    ffn_up(2, 0)
    grad_rows(gdown, gl, db, 0)
    ag((5, 4))
    grad_rows(gdown, gl, db, 1)
    ag((6, 3))
    ffn_up(0, 1)
    ffn_up(1, 1)
    ffn_up(2, 1)
    ag((6, 4))
    grad_rows(gdown, gl, db, 2)
    grad_rows(gdown, gl, db, 3)
    rs_start(RD)
    for s in range(SEQS):
        ffn_hidden_grad(s)
    tok_load = pltpu.make_async_copy(tok_hbm, db, io_sem.at[4])
    tok_load.start()
    rs_next(RD, 1)
    for q in range(F // D):
        grad_cols(gup, n2, du, q)
    rs_start(RU)

    def ffn_back(s):
        keep = keep_of(s)
        middle = mid[s]
        gy = cp[s].astype(F32)
        scale = lax.rsqrt(row_mean(middle * middle) + EPS)
        unit = middle * scale
        n2[s] = middle.astype(BF16)
        d_low = dot(du[s], all_of(UP), NT)
        vec_add(D, fold(d_low * unit))
        e = flat(tiles(d_low) * g_two)
        d_middle = gy + scale * (e - unit * row_mean(e * unit))
        mid[s] = d_middle
        d_mixer = (d_middle * keep).astype(BF16)
        cp[s] = d_mixer
        du[s, :, 0:H] = dot(d_mixer, all_of(OUT), NT).astype(BF16)

    ffn_back(0)
    rs_next(RU, 1)
    ffn_back(1)
    ffn_back(2)
    rs_next(RD, 2)

    bsums, bsums_in = (bsums0, bsums1), (bsums_in0, bsums_in1)
    bprefix = {}

    def two_low(s, hh, i):
        at = pl.multiple_of(i * 2 * SUB, 2 * SUB)
        v = du[s, pl.ds(at, 2 * SUB), hh * D:(hh + 1) * D].astype(F32)
        return v[0:SUB], v[SUB:2 * SUB]

    def back_totals(hh):
        def body(k, carry):
            i = nj // 2 - 1 - k
            vals = list(carry)
            for s in range(SEQS):
                ds = two_low(s, hh, i)
                for jj in (1, 0):
                    om = 1.0 - upd[s, tile_at(hh, i * 2 + jj), :]
                    vals[2 * s] = vals[2 * s] * om
                    vals[2 * s + 1] = om * (ds[jj] + vals[2 * s + 1])
            return tuple(vals)

        got = lax.fori_loop(0, nj // 2, body, (one, zero) * SEQS, unroll=2)
        for s in range(SEQS):
            a, d = inclusive(got[2 * s], got[2 * s + 1], True)
            bsums[hh][s:s + 1, :] = a[0:1, :]
            bsums[hh][SEQS + s:SEQS + s + 1, :] = d[0:1, :]
            bprefix[s, hh] = exclusive(a, d, True)
        for dz in range(1, nz):
            @pl.when(z - dz >= 0)
            def _():
                back_copy(hh, dz).start()

    def back_copy(hh, dz):
        return remote(bsums[hh], bsums_in[hh].at[z], b_send.at[hh, dz], b_recv.at[hh, z], (z - dz, b))

    def run_adjoint(hh):
        def leave_from(k, carry):
            i = nz - 1 - k
            remote(bsums[hh], bsums_in[hh].at[i], b_send.at[hh, 0], b_recv.at[hh, i], pc).wait_recv()
            got = bsums_in[hh][i]
            return got[0:SEQS] * carry + got[SEQS:2 * SEQS]

        leaving = lax.fori_loop(0, nz - 1 - z, leave_from, jnp.zeros((SEQS, D), F32))

        def body(k, carry):
            i = nj // 2 - 1 - k
            vals = list(carry)
            at = pl.multiple_of(i * 2 * SUB, 2 * SUB)
            for s in range(SEQS):
                ds = two_low(s, hh, i)
                gates, cands = [None] * 2, [None] * 2
                for jj in (1, 0):
                    u, q = upd[s, tile_at(hh, i * 2 + jj), :], cand[s, tile_at(hh, i * 2 + jj), :]
                    adj = ds[jj] + vals[2 * s]
                    vals[2 * s] = (1.0 - u) * adj
                    gates[jj] = adj * q
                    cands[jj] = adj * u
                    vals[2 * s + 1] = vals[2 * s + 1] + gates[jj]
                du[s, pl.ds(at, 2 * SUB), hh * D:(hh + 1) * D] = jnp.concatenate(gates, axis=0).astype(BF16)
                du[s, pl.ds(at, 2 * SUB), H + hh * D:H + (hh + 1) * D] = jnp.concatenate(cands, axis=0).astype(BF16)
            return tuple(vals)

        init = []
        for s in range(SEQS):
            ek, ed = bprefix[s, hh]
            init += [ek * leaving[s:s + 1] + ed, zero]
        done = lax.fori_loop(0, nj // 2, body, tuple(init), unroll=2)
        vec_add(6 * D + hh * D, done[1] + done[3] + done[5])

    back_totals(0)
    back_totals(1)
    ag_left(OUT)
    for q in range(nz):
        grad_rows(wout, st, cp, q)
    rs_start(RO)
    run_adjoint(0)
    rs_next(RU, 2)
    run_adjoint(1)

    first = jnp.concatenate([du[s, 0:4 * SUB, :] for s in range(SEQS)], axis=0)
    first = dot(first, all_of(IN), NT)
    for s in range(SEQS):
        for i in range(3):
            r = 3 * s + i
            back_out[r:r + 1, :] = first[(4 * s + i) * SUB:(4 * s + i) * SUB + 1, :]
    send_back = remote(back_out, back_in, h_sem.at[2], h_sem.at[3], up_z(nz - 1))
    send_back.start()
    rs_next(RO, 1)

    ag_left(UP)
    grad_cols(wup, mix, du, 0)
    grad_cols(wup, mix, du, 2)
    for cpy in rs_copies(RU, 1):
        cpy.wait_send()
    pl.semaphore_signal(free_sem, inc=1, device_id=pc, device_id_type=MESH)
    pl.semaphore_wait(free_sem, 1)
    rs_start(RI0)
    rs_next(RD, 3)
    grad_cols(wup, mix, du, 1)
    grad_cols(wup, mix, du, 3)
    rs_start(RI1)
    rs_next(RI0, 1)
    rs_next(RU, 3)

    def back_project(s):
        upd[s, 0:span] = dot(du[s], all_of(IN), NT)

    def ffn_out(s):
        block = (n2[s].astype(F32) + keep_of(s) * dot(gl[s], all_of(DOWN))).astype(BF16)
        n2[s] = dot(perm[...], block, TN).astype(BF16)

    def back_norm(s):
        for i in range(3):
            r = 3 * s + i
            tile = pltpu.roll(upd[s, i * SUB:(i + 1) * SUB, :], SUB - 1, 0)
            edge = jnp.where(z < nz - 1, back_in[r:r + 1, :], 0.0)
            upd[s, span + i * SUB:span + (i + 1) * SUB] = jnp.where(sub0 == SUB - 1, edge, tile)
        unit, scale = unit_of(dot(perm[...], db[s]))
        normed = (tiles(unit) * g_one).astype(BF16).astype(F32)
        d_normed = jnp.zeros((nj, SUB, D), F32)
        for k in range(4):
            ahead = tiles(upd[s, (3 - k) * SUB:(3 - k) * SUB + span])
            d_normed = d_normed + taps[k] * ahead
            vec_add((2 + k) * D, jnp.sum(normed * ahead, axis=0))
        vec_add(0, jnp.sum(d_normed * tiles(unit), axis=0))
        e = flat(d_normed * g_one)
        out = mid[s] + scale * (e - unit * row_mean(e * unit))
        high = out.astype(BF16)
        rest_low = (out - high.astype(F32)).astype(BF16)
        mid[s] = dot(perm[...], high, TN) + dot(perm[...], rest_low, TN)

    back_project(0)
    rs_next(RI1, 1)
    back_project(1)
    rs_next(RO, 2)
    back_project(2)
    tok_load.wait()
    send_back.wait_recv()
    back_norm(0)
    rs_next(RI0, 2)
    back_norm(1)
    rs_next(RI1, 2)
    back_norm(2)
    def quad_copy(d):
        return remote(vgrad.at[:, lax.rem(b + d, 8)], vquad.at[d - 1], g_send.at[d - 1], g_recv.at[d - 1], peer(d))

    def line_copy(d):
        return remote(vsum.at[lax.rem(z + d, nz)], vline.at[d - 1], g_send.at[6 + d], g_recv.at[6 + d], up_z(d))

    for d in range(1, 8):
        quad_copy(d).start()
    grad_store = pltpu.make_async_copy(mid, grad_hbm, io_sem.at[7])
    grad_store.start()
    rs_next(RO, 3)
    ffn_out(0)
    rs_next(RI0, 3)
    ffn_out(1)
    rs_next(RI1, 3)
    for d in range(1, 8):
        quad_copy(d).wait_recv()
    vsum[...] = vgrad[:, b] + jnp.sum(vquad[...], axis=0)
    for d in range(1, nz):
        line_copy(d).start()
    ffn_out(2)
    block_store = pltpu.make_async_copy(n2, block_hbm, io_sem.at[6])
    block_store.start()
    rs_next(RD, 4)
    rs_next(RU, 4)
    rs_next(RO, 4)
    rs_next(RI0, 4)
    rs_next(RI1, 4)
    for d in range(1, nz):
        line_copy(d).wait_recv()
    sum_vec[...] = jnp.sum(vsum[z] + jnp.sum(vline[...], axis=0), axis=0, keepdims=True)

    ag_left(IN, DOWN)
    for r in range(5):
        for stage in range(4):
            if (r, stage) != (RU, 1):
                for cpy in rs_copies(r, stage):
                    cpy.wait_send()
    for d in range(1, nz):
        vec_line(d).wait_send()
        line_copy(d).wait_send()
    for d in range(1, 8):
        vec_peer(d).wait_send()
        quad_copy(d).wait_send()
    send_back.wait_send()
    for dz in range(1, nz):
        for hh in range(2):
            @pl.when(z + dz < nz)
            def _():
                carry_copy(hh, dz).wait_send()

            @pl.when(z - dz >= 0)
            def _():
                back_copy(hh, dz).wait_send()
    block_store.wait()
    grad_store.wait()


def adam_math(weight, grad, first, second, rate, decay):
    moment = BETA_ONE * first + (1.0 - BETA_ONE) * grad
    square = BETA_TWO * second + (1.0 - BETA_TWO) * grad * grad
    corr_one = 1.0 - BETA_ONE**STEP
    corr_two = 1.0 - BETA_TWO**STEP
    direction = moment / corr_one / (jnp.sqrt(square / corr_two) + ADAM_EPS)
    fresh = weight - rate * (direction + decay * weight)
    return fresh, moment, square


def adam_kernel(rates, *refs):
    ins, moved_in, outs, moved_out = refs[:20], refs[20:23], refs[23:42], refs[42:45]
    held, made, passing = refs[45:65], refs[65:84], refs[84:87]
    in_sem, out_sem, move_in_sem, move_out_sem = refs[87:]
    loads = [pltpu.make_async_copy(ins[i], held[i], in_sem.at[i]) for i in range(20)]
    parts = [(i, s) for i in range(3) for s in range(SEQS)]
    comes = [pltpu.make_async_copy(moved_in[i].at[s], passing[i].at[s], move_in_sem.at[i, s]) for i, s in parts]
    goes = [pltpu.make_async_copy(passing[i].at[s], moved_out[i].at[s], move_out_sem.at[i, s]) for i, s in parts]
    for cpy in loads:
        cpy.start()
    for cpy in comes:
        cpy.start()
    stores = []
    at = 0
    for k in range(5):
        rate, decay = rates[k]
        for cpy in loads[4 * k:4 * k + 4]:
            cpy.wait()
        w, g, m, v = (r[...] for r in held[4 * k:4 * k + 4])
        fresh, moment, square = adam_math(w, g, m, v, rate, decay)
        for out in (fresh, fresh.astype(BF16), moment, square) if k < 4 else (fresh, moment, square):
            made[at][...] = out
            stores.append(pltpu.make_async_copy(made[at], outs[at], out_sem.at[at]))
            stores[-1].start()
            at += 1
    for come, go in zip(comes, goes):
        come.wait()
        go.start()
    for cpy in stores + goes:
        cpy.wait()


def fast_shards(nz, *args):
    (tokens, cotangent, start, lengths, w_in, w_out, w_up, w_down, vectors,
     m_in, v_in, m_out, v_out, m_up, v_up, m_down, v_down, m_vec, v_vec) = args
    span = tokens.shape[1]
    hbm = pl.BlockSpec(memory_space=pl.ANY)
    vmem = pl.BlockSpec(memory_space=pltpu.VMEM)
    smem = pl.BlockSpec(memory_space=pltpu.SMEM)
    rows = [w.shape[0] for w in (w_in, w_out, w_up, w_down)]
    cols = [w.shape[1] for w in (w_in, w_out, w_up, w_down)]
    vec_row = vectors.reshape(1, LANES)

    def S(*shape, dtype=F32):
        return jax.ShapeDtypeStruct(shape, dtype)

    def low(*shape):
        return pltpu.VMEM(shape, BF16)

    def wide(*shape):
        return pltpu.VMEM(shape, F32)

    dma = pltpu.SemaphoreType.DMA
    nsend = 6 + 2 * (nz - 1)
    ndev = nz * 8
    scratch = [
        low(SEQS, span, D), low(SEQS, span, D),
        *[low(nz, 2, 2, 2, r, n) for r, n in zip(rows, cols)],
        wide(SEQS, 2 * span, D), wide(SEQS, 2 * span, D),
        low(SEQS, span, H), low(SEQS, span, F), low(SEQS, span, F),
        low(SEQS, span, D), low(SEQS, span, D), wide(SEQS, span, D),
        low(nz, 2, 2, 2, rows[3], cols[3]), low(nz, 2, 2, 2, rows[2], cols[2]),
        *[low(nz, 2, 2, r, n) for r, n in zip(rows[1:], cols[1:])],
        *[low(nz, 2, r, n // 2) for r, n in zip(rows, cols) for _ in range(2)],
        *[low(nz, r, n // 2) for r, n in zip(rows, cols) for _ in range(2)],
        *[low(nz - 1, r, n // 2) for r, n in zip(rows, cols) for _ in range(2)],
        low(span, span), wide(span, LANES),
        wide(nz, 8, SUB, LANES), wide(SUB, 8 * D), wide(nz, 8, SUB, LANES),
        wide(7, nz, SUB, LANES), wide(nz, SUB, LANES), wide(nz - 1, SUB, LANES),
        low(SEQS, 2 * SUB, D), wide(16, D), wide(16, D),
        *[wide(SUB, D), wide(SUB, D), wide(nz, SUB, D), wide(nz, SUB, D)] * 2,
        dma((8,)), dma((7, 12)), dma((7, 12)), dma((5, nsend)), dma((5, nsend)),
        dma((10,)), dma((10,)), dma((10,)), dma((10,)), dma((4,)),
        *[dma((2, nz)) for _ in range(4)], pltpu.SemaphoreType.REGULAR,
    ]
    block, ends, grad, s_in, s_out, s_up, s_down, s_vec = pl.pallas_call(
        functools.partial(step_kernel, nz, span),
        out_shape=[
            S(SEQS, span, D, dtype=BF16), S(SEQS, 1, H), S(SEQS, span, D),
            *[S(r, n) for r, n in zip(rows, cols)], S(1, LANES),
        ],
        in_specs=[hbm, hbm, vmem, smem, hbm, hbm, hbm, hbm, vmem],
        out_specs=[hbm, vmem, hbm, vmem, vmem, vmem, vmem, vmem],
        scratch_shapes=scratch,
        compiler_params=pltpu.CompilerParams(
            collective_id=0, has_side_effects=True, vmem_limit_bytes=64 * 2**20 - 2**18
        ),
    )(tokens, cotangent, start, lengths, w_in, w_out, w_up, w_down, vec_row)

    rates = ((D**-0.5, DECAY), (H**-0.5, DECAY), (D**-0.5, DECAY), (F**-0.5, DECAY), (VEC_RATE, 0.0))
    outs = []
    for k in range(4):
        outs += [S(rows[k], cols[k]), S(rows[k], cols[k], dtype=BF16), S(rows[k], cols[k]), S(rows[k], cols[k])]
    outs += [S(1, LANES)] * 3
    ins = (
        w_in, s_in, m_in, v_in, w_out, s_out, m_out, v_out, w_up, s_up, m_up, v_up,
        w_down, s_down, m_down, v_down,
        vec_row, s_vec, m_vec.reshape(1, LANES), v_vec.reshape(1, LANES),
    )
    moved = (block, ends, grad)
    fresh = pl.pallas_call(
        functools.partial(adam_kernel, rates),
        out_shape=outs + [S(*v.shape, dtype=v.dtype) for v in moved],
        in_specs=[hbm] * 23,
        out_specs=[hbm] * 22,
        scratch_shapes=[
            *[pltpu.VMEM(v.shape, F32) for v in ins], *[pltpu.VMEM(v.shape, v.dtype) for v in outs],
            *[pltpu.VMEM(v.shape, v.dtype) for v in moved],
            dma((20,)), dma((19,)), dma((3, SEQS)), dma((3, SEQS)),
        ],
        compiler_params=pltpu.CompilerParams(vmem_limit_bytes=63 * 2**20),
    )(*ins, *moved)
    block, ends, grad = fresh[19:]
    return (block, ends, grad, *fresh[:16], *[v.reshape(LANES) for v in fresh[16:19]])


def entering_2(value, axis, combine, identity, reverse):
    size, mine = (lax.axis_size(axis), lax.axis_index(axis))
    everything = jax.tree.map(lambda part: lax.all_gather(part, axis), value)
    start = jax.tree.map(
        lambda part, zero: jnp.broadcast_to(jnp.asarray(zero, part.dtype), part.shape),
        value,
        identity,
    )

    def step(k, before):
        at = size - 1 - k if reverse else k
        reached = at > mine if reverse else at < mine
        new = combine(before, jax.tree.map(lambda part: part[at], everything))
        return jax.tree.map(lambda a, b: jnp.where(reached, a, b), new, before)

    return lax.fori_loop(0, size, step, start)


def shifted_2(value, axis, by):
    size = lax.axis_size(axis)
    pairs = [(i, i + by) for i in range(size) if 0 <= i + by < size]
    return lax.ppermute(value, axis, pairs)


def combine_affine(earlier, later):
    return (earlier[0] * later[0], later[0] * earlier[1] + later[1])


def carry_forward(keep_total, drive_total):
    return entering_2(
        (keep_total, drive_total),
        "seq",
        combine_affine,
        (jnp.ones_like(keep_total), jnp.zeros_like(drive_total)),
        False,
    )


def carry_backward(keep_total, drive_total):
    return entering_2(
        (keep_total, drive_total),
        "seq",
        combine_affine,
        (jnp.ones_like(keep_total), jnp.zeros_like(drive_total)),
        True,
    )


def adam_step(weight, grad, first, second, rate, decay):
    moment = BETA_ONE * first + (1.0 - BETA_ONE) * grad
    square = BETA_TWO * second + (1.0 - BETA_TWO) * grad * grad
    corr_one = 1.0 - BETA_ONE**STEP
    corr_two = 1.0 - BETA_TWO**STEP
    direction = moment / corr_one / (jnp.sqrt(square / corr_two) + ADAM_EPS)
    fresh = weight - rate * (direction + decay * weight)
    return (fresh, moment, square)


def shards(
    tokens,
    cotangent,
    start_states,
    lengths,
    w_in,
    w_out,
    w_up,
    w_down,
    vectors,
    first_in,
    second_in,
    first_out,
    second_out,
    first_up,
    second_up,
    first_down,
    second_down,
    first_vec,
    second_vec,
):
    f32 = jnp.float32
    bf16 = jnp.bfloat16
    full_in, full_out, full_up, full_down, full_vec = (
        lax.all_gather(w_in.astype(bf16), ("seq", "batch"), axis=0, tiled=True),
        lax.all_gather(w_out.astype(bf16), ("seq", "batch"), axis=0, tiled=True),
        lax.all_gather(w_up.astype(bf16), ("seq", "batch"), axis=0, tiled=True),
        lax.all_gather(w_down.astype(bf16), ("seq", "batch"), axis=0, tiled=True),
        lax.all_gather(vectors.astype(bf16), ("seq", "batch"), axis=0, tiled=True),
    )
    vec_full = full_vec.astype(f32)
    g_one = vec_full[:D]
    g_two = vec_full[D : 2 * D]
    taps = vec_full[2 * D : 6 * D].reshape(4, D)
    bias = vec_full[6 * D :]
    span_len = tokens.shape[1]
    offset = lax.axis_index("seq") * span_len
    valid = ((offset + jnp.arange(span_len))[None, :] < lengths[:, None]).astype(f32)[..., None]
    inputs = tokens.astype(f32)
    scale_one = lax.rsqrt(jnp.mean(inputs * inputs, axis=-1, keepdims=True) + EPS)
    unit_one = inputs * scale_one
    normed = (unit_one * g_one).astype(bf16)
    rim_in = shifted_2(normed[:, span_len - 3 :, :], "seq", 1)
    extended = jnp.concatenate([rim_in, normed], axis=1).astype(f32)
    mixed = sum((taps[tap_idx] * extended[:, tap_idx : tap_idx + span_len] for tap_idx in range(4)))
    mixed_low = mixed.astype(bf16)
    projected = jnp.einsum("scd,dk->sck", mixed_low, full_in, preferred_element_type=f32)
    cand = projected[..., H:]
    gate_sig = jax.nn.sigmoid(projected[..., :H] + bias)
    update = gate_sig * valid
    retain = 1.0 - update
    driven = update * cand
    run_keep, run_drive = lax.associative_scan(combine_affine, (retain, driven), axis=1)
    enter_keep, enter_drive = carry_forward(run_keep[:, -1], run_drive[:, -1])
    entering = enter_keep * start_states + enter_drive
    states = run_keep * entering[:, None] + run_drive
    stretch_end = states[:, span_len - 1 :]
    state_low = states.astype(bf16)
    mixer = jnp.einsum("sch,hd->scd", state_low, full_out, preferred_element_type=f32)
    middle = inputs + valid * mixer
    scale_two = lax.rsqrt(jnp.mean(middle * middle, axis=-1, keepdims=True) + EPS)
    unit_two = middle * scale_two
    normed_two = (unit_two * g_two).astype(bf16)
    up_pre = jnp.einsum("scd,df->scf", normed_two, full_up, preferred_element_type=f32)
    gelu_out, gelu_pull = jax.vjp(jax.nn.gelu, up_pre)
    gelu_low = gelu_out.astype(bf16)
    branch = jnp.einsum("scf,fd->scd", gelu_low, full_down, preferred_element_type=f32)
    block_out = (middle + valid * branch).astype(bf16)
    grad_y = cotangent.astype(f32)
    d_branch = (grad_y * valid).astype(bf16)
    grad_down = jnp.einsum("scf,scd->fd", gelu_low, d_branch, preferred_element_type=f32)
    d_gelu = jnp.einsum("scd,fd->scf", d_branch, full_down, preferred_element_type=f32)
    d_up = gelu_pull(d_gelu)[0].astype(bf16)
    grad_up = jnp.einsum("scd,scf->df", normed_two, d_up, preferred_element_type=f32)
    d_normed_two = jnp.einsum("scf,df->scd", d_up, full_up, preferred_element_type=f32)
    grad_g_two = jnp.sum(d_normed_two * unit_two, axis=(0, 1))
    e_two = d_normed_two * g_two
    d_middle = grad_y + scale_two * (
        e_two - unit_two * jnp.mean(e_two * unit_two, axis=-1, keepdims=True)
    )
    d_mixer = (d_middle * valid).astype(bf16)
    grad_out = jnp.einsum("sch,scd->hd", state_low, d_mixer, preferred_element_type=f32)
    d_states = jnp.einsum("scd,hd->sch", d_mixer, full_out, preferred_element_type=f32)
    shifted = jnp.concatenate([retain[:, 1:], jnp.ones_like(retain[:, :1])], axis=1)
    back_keep, back_drive = lax.associative_scan(
        combine_affine, (shifted, d_states), axis=1, reverse=True
    )
    send_keep = retain[:, 0] * back_keep[:, 0]
    send_drive = retain[:, 0] * back_drive[:, 0]
    unused_keep, incoming = carry_backward(send_keep, send_drive)
    adjoint = back_keep * incoming[:, None] + back_drive
    prev_state = jnp.concatenate([entering[:, None], states[:, :-1]], axis=1)
    d_update = adjoint * (cand - prev_state)
    d_gate = d_update * valid * gate_sig * (1.0 - gate_sig)
    grad_bias = jnp.sum(d_gate, axis=(0, 1))
    gate_low = d_gate.astype(bf16)
    cand_low = (adjoint * update).astype(bf16)
    grad_in = jnp.concatenate(
        [
            jnp.einsum("scd,sck->dk", mixed_low, gate_low, preferred_element_type=f32),
            jnp.einsum("scd,sck->dk", mixed_low, cand_low, preferred_element_type=f32),
        ],
        axis=1,
    )
    d_mixed = jnp.einsum(
        "sck,dk->scd", gate_low, full_in[:, :H], preferred_element_type=f32
    ) + jnp.einsum("sck,dk->scd", cand_low, full_in[:, H:], preferred_element_type=f32)
    grad_taps = jnp.stack(
        [
            jnp.sum(d_mixed * extended[:, tap_idx : tap_idx + span_len], axis=(0, 1))
            for tap_idx in range(4)
        ]
    )
    rim_terms = jnp.stack(
        [
            sum((taps[tap_idx] * d_mixed[:, lead - tap_idx] for tap_idx in range(lead + 1)))
            for lead in range(3)
        ],
        axis=1,
    )
    mixed_tail = jnp.concatenate([d_mixed, jnp.zeros_like(d_mixed[:, :3])], axis=1)
    d_normed = sum(
        (
            taps[tap_idx] * mixed_tail[:, 3 - tap_idx : 3 - tap_idx + span_len]
            for tap_idx in range(4)
        )
    )
    rim_back = shifted_2(rim_terms, "seq", -1)
    d_normed = d_normed.at[:, span_len - 3 :].add(rim_back)
    grad_g_one = jnp.sum(d_normed * unit_one, axis=(0, 1))
    e_one = d_normed * g_one
    grad_tokens = d_middle + scale_one * (
        e_one - unit_one * jnp.mean(e_one * unit_one, axis=-1, keepdims=True)
    )
    grad_vec = jnp.concatenate([grad_g_one, grad_g_two, grad_taps.reshape(-1), grad_bias])
    sum_in, sum_out, sum_up, sum_down, sum_vec = (
        lax.psum_scatter(grad_in, ("seq", "batch"), scatter_dimension=0, tiled=True),
        lax.psum_scatter(grad_out, ("seq", "batch"), scatter_dimension=0, tiled=True),
        lax.psum_scatter(grad_up, ("seq", "batch"), scatter_dimension=0, tiled=True),
        lax.psum_scatter(grad_down, ("seq", "batch"), scatter_dimension=0, tiled=True),
        lax.psum_scatter(grad_vec, ("seq", "batch"), scatter_dimension=0, tiled=True),
    )
    new_in, moment_in, square_in = adam_step(w_in, sum_in, first_in, second_in, D ** (-0.5), DECAY)
    new_out, moment_out, square_out = adam_step(
        w_out, sum_out, first_out, second_out, H ** (-0.5), DECAY
    )
    new_up, moment_up, square_up = adam_step(w_up, sum_up, first_up, second_up, D ** (-0.5), DECAY)
    new_down, moment_down, square_down = adam_step(
        w_down, sum_down, first_down, second_down, F ** (-0.5), DECAY
    )
    new_vec, moment_vec, square_vec = adam_step(
        vectors, sum_vec, first_vec, second_vec, VEC_RATE, 0.0
    )
    return (
        block_out,
        stretch_end,
        grad_tokens,
        new_in,
        new_in.astype(bf16),
        moment_in,
        square_in,
        new_out,
        new_out.astype(bf16),
        moment_out,
        square_out,
        new_up,
        new_up.astype(bf16),
        moment_up,
        square_up,
        new_down,
        new_down.astype(bf16),
        moment_down,
        square_down,
        new_vec,
        moment_vec,
        square_vec,
    )


def solution(mesh):
    placed = (
        P("batch", "seq", None),
        P("batch", "seq", None),
        P("batch", None),
        P("batch"),
        P(("seq", "batch"), None),
        P(("seq", "batch"), None),
        P(("seq", "batch"), None),
        P(("seq", "batch"), None),
        P(("seq", "batch")),
        P(("seq", "batch"), None),
        P(("seq", "batch"), None),
        P(("seq", "batch"), None),
        P(("seq", "batch"), None),
        P(("seq", "batch"), None),
        P(("seq", "batch"), None),
        P(("seq", "batch"), None),
        P(("seq", "batch"), None),
        P(("seq", "batch")),
        P(("seq", "batch")),
    )
    nz, nb = mesh.shape["seq"], mesh.shape["batch"]
    fits = nb == 8 and nz == 4
    return jax.shard_map(
        functools.partial(fast_shards, nz) if fits else shards,
        mesh=mesh,
        in_specs=placed,
        out_specs=(
            P("batch", "seq", None),
            P("batch", "seq", None),
            P("batch", "seq", None),
            P(("seq", "batch"), None),
            P(("seq", "batch"), None),
            P(("seq", "batch"), None),
            P(("seq", "batch"), None),
            P(("seq", "batch"), None),
            P(("seq", "batch"), None),
            P(("seq", "batch"), None),
            P(("seq", "batch"), None),
            P(("seq", "batch"), None),
            P(("seq", "batch"), None),
            P(("seq", "batch"), None),
            P(("seq", "batch"), None),
            P(("seq", "batch"), None),
            P(("seq", "batch"), None),
            P(("seq", "batch"), None),
            P(("seq", "batch"), None),
            P(("seq", "batch")),
            P(("seq", "batch")),
            P(("seq", "batch")),
        ),
        check_vma=False,
    )
```

```python
import functools

import jax
import jax.numpy as jnp
from jax import lax
from jax.experimental import pallas as pl
from jax.experimental.pallas import tpu as pltpu
from jax.sharding import PartitionSpec as P

D = 512
H = 1024
F = 2048
STEP = 5
EPS = 1e-06
ADAM_EPS = 1e-08
BETA_ONE = 0.5
BETA_TWO = 0.5
DECAY = 0.1
VEC_RATE = 1.5
MESH = pl.DeviceIdType.MESH
F32 = jnp.float32
BF16 = jnp.bfloat16
SUB = 8
LANES = 128
SEQS = 3

NN = (((1,), (0,)), ((), ()))
NT = (((1,), (1,)), ((), ()))
TN = (((0,), (0,)), ((), ()))


def dot(a, b, dims=NN):
    return lax.dot_general(a, b, dims, preferred_element_type=F32)


def tiles(v):
    return v.reshape(v.shape[0] // SUB, SUB, v.shape[1])


def flat(v):
    return v.reshape(v.shape[0] * SUB, v.shape[2])


def fold(v):
    return jnp.sum(tiles(v), axis=0)


def row_mean(v):
    return jnp.mean(v, axis=-1, keepdims=True)


IN, OUT, UP, DOWN = range(4)

PIECES = ((IN, 0), (IN, 1), (OUT, 0), (UP, 0), (UP, 1), (DOWN, 0), (DOWN, 1))


def step_kernel(
    nz, span,
    tok_hbm, cot_hbm, start_hbm, len_ref, w_in_hbm, w_out_hbm, w_up_hbm, w_down_hbm, vec_hbm,
    block_hbm, ends_hbm, grad_hbm, in_hbm, out_hbm, up_hbm, down_hbm, sum_vec_hbm,
    start_ref, vec_ref, ends_ref, sum_in, sum_out, sum_up, sum_down, sum_vec,
    cp, mix, win, wout, wup, wdown, upd, cand, st, gl, du, n2, db, mid, gdown, gup,
    r0o, r0u, r0d, r1ai, r1bi, r1ao, r1bo, r1au, r1bu, r1ad, r1bd,
    r2ai, r2bi, r2ao, r2bo, r2au, r2bu, r2ad, r2bd,
    r3ai, r3bi, r3ao, r3bo, r3au, r3bu, r3ad, r3bd,
    perm, clock, vec, vec8, vgrad, vquad, vsum, vline, halo_in, back_out, back_in,
    sums0, sums1, sums_in0, sums_in1, bsums0, bsums1, bsums_in0, bsums_in1,
    io_sem, ag_send, ag_recv, rs_send, rs_recv, v_send, v_recv, g_send, g_recv, h_sem,
    c_send, c_recv, b_send, b_recv, free_sem,
):
    nj = span // SUB
    z = lax.axis_index("seq")
    b = lax.axis_index("batch")
    y, x, c = b // 4, lax.rem(b // 2, 2), lax.rem(b, 2)
    px, py, pc = (z, b + 2 - 4 * x), (z, b + 4 - 8 * y), (z, b + 1 - 2 * c)
    full = (win, wout, wup, wdown)
    masters = (w_in_hbm, w_out_hbm, w_up_hbm, w_down_hbm)
    staged = (sum_in, sum_out, sum_up, sum_down)

    def remote(src, dst, ssem, rsem, dev):
        return pltpu.make_async_remote_copy(
            src_ref=src, dst_ref=dst, send_sem=ssem, recv_sem=rsem, device_id=dev, device_id_type=MESH
        )

    def up_z(d):
        return (lax.rem(z + d, nz), b)

    def peer(d):
        return (z, lax.rem(b + d, 8))

    barrier = pltpu.get_barrier_semaphore()
    for dev in [up_z(d) for d in range(1, nz)] + [peer(d) for d in range(1, 8)]:
        pl.semaphore_signal(barrier, inc=1, device_id=dev, device_id_type=MESH)

    loads = [pltpu.make_async_copy(masters[k], staged[k], io_sem.at[k]) for k in range(4)]
    tok_load = pltpu.make_async_copy(tok_hbm, n2, io_sem.at[4])
    cot_load = pltpu.make_async_copy(cot_hbm, db, io_sem.at[5])
    vec_load = pltpu.make_async_copy(vec_hbm, vec_ref, io_sem.at[8])
    start_load = pltpu.make_async_copy(start_hbm, start_ref, io_sem.at[9])
    vec_load.start()
    for cpy in loads:
        cpy.start()
    start_load.start()
    tok_load.start()
    cot_load.start()

    vec_load.wait()
    vec[z, b] = jnp.broadcast_to(vec_ref[...].astype(BF16).astype(F32), (SUB, LANES))
    for k in range(4):
        loads[k].wait()
        full[k][z, y, x, c] = staged[k][...].astype(BF16)

    def piece_cols(k, h):
        w, part = PIECES[k]
        if w == IN:
            return slice(h * H + part * D, h * H + (part + 1) * D)
        if w == UP:
            return slice(part * H + h * D, part * H + (h + 1) * D)
        return slice(h * (D // 2), (h + 1) * (D // 2))

    def piece_rows(k):
        w, part = PIECES[k]
        n = full[w].shape[4]
        return slice(part * (n // 2), (part + 1) * (n // 2)) if w == DOWN else slice(0, n)

    def ag_copies(k, stage):
        ref, rws = full[PIECES[k][0]], piece_rows(k)
        out = []

        def add(at, sem, dev):
            out.append(remote(ref.at[at], ref.at[at], ag_send.at[k, sem], ag_recv.at[k, sem], dev))

        for h in range(2):
            n = piece_cols(k, h)
            if stage == 3:
                add((slice(None), slice(None), slice(None), c, rws, n), 10 + h, pc)
            elif stage == 0:
                for dz in range(1, nz):
                    add((z, y, x, c, rws, n), 3 * h + dz - 1, up_z(dz))
            elif stage == 1:
                add((slice(None), y, x, c, rws, n), 6 + h, (px, py)[h])
            else:
                at = (slice(None), y, slice(None), c, rws, n) if h == 0 else (slice(None), slice(None), x, c, rws, n)
                add(at, 8 + h, (py, px)[h])
        return out

    def ag(*events):
        for k, stage in events:
            if stage > 0:
                for cpy in ag_copies(k, stage - 1):
                    cpy.wait_recv()
            if stage < 4:
                for cpy in ag_copies(k, stage):
                    cpy.start()

    def ag_left(*weights):
        for k, (w, _) in enumerate(PIECES):
            if w in weights:
                for stage in range(4):
                    for cpy in ag_copies(k, stage):
                        cpy.wait_send()

    def vec_line(d):
        return remote(vec.at[z, b], vec.at[z, b], v_send.at[d - 1], v_recv.at[d - 1], up_z(d))

    def vec_peer(d):
        return remote(vec.at[:, b], vec.at[:, b], v_send.at[nz - 2 + d], v_recv.at[nz - 2 + d], peer(d))

    pl.semaphore_wait(barrier, nz - 1 + 7)
    for d in range(1, nz):
        vec_line(d).start()
    tok_load.wait()
    send_halo = remote(n2.at[:, span - 2 * SUB:span], halo_in, h_sem.at[0], h_sem.at[1], up_z(1))
    send_halo.start()
    ag((0, 0), (1, 0))

    rows = lax.broadcasted_iota(jnp.int32, (span, span), 0)
    cols = lax.broadcasted_iota(jnp.int32, (span, span), 1)
    perm[...] = jnp.where(cols == lax.rem(rows, SUB) * nj + rows // SUB, 1.0, 0.0).astype(BF16)
    vrow = lax.broadcasted_iota(jnp.int32, (span, LANES), 0)
    clock[...] = (lax.rem(vrow, SUB) * nj + vrow // SUB + z * span).astype(F32)

    def keep_of(s):
        one = jnp.where(clock[...] < len_ref[s].astype(F32), 1.0, 0.0)
        return jnp.concatenate([one] * (D // LANES), axis=1)

    for s in range(SEQS):
        gdown[s] = dot(perm[...], n2[s]).astype(BF16).reshape(gdown.shape[1:])
    for d in range(1, nz):
        vec_line(d).wait_recv()
    for d in range(1, 8):
        vec_peer(d).start()

    def unit_of(v):
        scale = lax.rsqrt(row_mean(v * v) + EPS)
        return v * scale, scale

    cot_load.wait()
    for s in range(SEQS):
        low = dot(perm[...], db[s])
        cp[s] = low.astype(BF16)
        db[s] = (low * keep_of(s)).astype(BF16)
    ag((0, 1), (2, 0))
    for d in range(1, 8):
        vec_peer(d).wait_recv()
    for i in range(nz * 8):
        vec8[:, i * LANES:(i + 1) * LANES] = vec[i // 8, i % 8]
    g_one = vec8[:, 0:D]
    g_two = vec8[:, D:2 * D]
    taps = [vec8[:, (2 + k) * D:(3 + k) * D] for k in range(4)]

    sub0 = lax.broadcasted_iota(jnp.int32, (SUB, D), 0)
    send_halo.wait_recv()
    for s in range(SEQS):
        unit, _ = unit_of(gdown[s].reshape(span, D).astype(F32))
        normed = (tiles(unit) * g_one).astype(BF16).astype(F32)
        upd[s, 3 * SUB:3 * SUB + span] = flat(normed)
        edges, _ = unit_of(halo_in[s].astype(F32))
        edges = (edges[SUB:2 * SUB] * g_one).astype(BF16).astype(F32)
        for i in range(3):
            tile = pltpu.roll(upd[s, span + i * SUB:span + (i + 1) * SUB, :], 1, 0)
            edge = jnp.where(z > 0, edges[SUB - 3 + i:SUB - 2 + i, :], 0.0)
            upd[s, i * SUB:(i + 1) * SUB] = jnp.where(sub0 == 0, edge, tile)
        total = taps[0] * tiles(upd[s, 0:span])
        for k in range(1, 4):
            total = total + taps[k] * tiles(upd[s, k * SUB:k * SUB + span])
        mix[s] = flat(total).astype(BF16)
        if s == 0:
            ag((1, 1), (3, 0))
        if s == 1:
            ag((0, 2))
    ag((2, 1), (4, 0), (1, 2), (3, 1), (5, 0), (0, 3), (2, 2), (0, 4))

    def cols_of(k, lo, hi):
        v = full[k][:, :, :, :, :, lo:hi]
        return v.reshape(v.shape[0] * 8 * v.shape[4], hi - lo)

    def all_of(k):
        v = full[k][...]
        return v.reshape(v.shape[0] * 8 * v.shape[4], v.shape[5])

    lane_sub = lax.broadcasted_iota(jnp.int32, (SUB, D), 0)

    def inclusive(keep, drive, reverse):
        for d in (1, 2, 4):
            by = SUB - d if reverse else d
            inside = lane_sub < SUB - d if reverse else lane_sub >= d
            k2 = jnp.where(inside, pltpu.roll(keep, by, 0), 1.0)
            d2 = jnp.where(inside, pltpu.roll(drive, by, 0), 0.0)
            drive = drive + keep * d2
            keep = keep * k2
        return keep, drive

    def exclusive(keep, drive, reverse):
        by = SUB - 1 if reverse else 1
        edge = lane_sub == (SUB - 1 if reverse else 0)
        return (
            jnp.where(edge, 1.0, pltpu.roll(keep, by, 0)),
            jnp.where(edge, 0.0, pltpu.roll(drive, by, 0)),
        )

    def tile_at(hh, j):
        return pl.ds(pl.multiple_of(j * SUB, SUB) + hh * span, SUB)

    def project(s, hh):
        bias = vec8[:, 6 * D + hh * D:6 * D + (hh + 1) * D]
        gate = tiles(dot(mix[s], cols_of(IN, hh * D, (hh + 1) * D))) + bias
        upd[s, hh * span:(hh + 1) * span] = flat(jax.nn.sigmoid(gate)) * keep_of(s)
        cand[s, hh * span:(hh + 1) * span] = dot(mix[s], cols_of(IN, H + hh * D, H + (hh + 1) * D))

    prefix = {}
    sums, sums_in = (sums0, sums1), (sums_in0, sums_in1)
    one, zero = jnp.ones((SUB, D), F32), jnp.zeros((SUB, D), F32)

    def totals(hh):
        def body(j, carry):
            out = []
            for s in range(SEQS):
                a, d = carry[2 * s], carry[2 * s + 1]
                u, v = upd[s, tile_at(hh, j), :], cand[s, tile_at(hh, j), :]
                out += [a * (1.0 - u), d + u * (v - d)]
            return tuple(out)

        got = lax.fori_loop(0, nj, body, (one, zero) * SEQS, unroll=4)
        for s in range(SEQS):
            a, d = inclusive(got[2 * s], got[2 * s + 1], False)
            sums[hh][s:s + 1, :] = a[SUB - 1:SUB, :]
            sums[hh][SEQS + s:SEQS + s + 1, :] = d[SUB - 1:SUB, :]
            prefix[s, hh] = exclusive(a, d, False)
        for dz in range(1, nz):
            @pl.when(z + dz < nz)
            def _():
                carry_copy(hh, dz).start()

    def carry_copy(hh, dz):
        return remote(sums[hh], sums_in[hh].at[z], c_send.at[hh, dz], c_recv.at[hh, z], (z + dz, b))

    def run_states(hh):
        def enter_from(i, carry):
            remote(sums[hh], sums_in[hh].at[i], c_send.at[hh, 0], c_recv.at[hh, i], pc).wait_recv()
            got = sums_in[hh][i]
            return got[0:SEQS] * carry + got[SEQS:2 * SEQS]

        entering = lax.fori_loop(0, z, enter_from, start_ref[:, hh * D:(hh + 1) * D])

        def body(i, carry):
            hs = list(carry)
            for s in range(SEQS):
                lows = []
                for jj in range(2):
                    j = i * 2 + jj
                    u, v = upd[s, tile_at(hh, j), :], cand[s, tile_at(hh, j), :]
                    moved = u * (v - hs[s])
                    hs[s] = hs[s] + moved
                    cand[s, tile_at(hh, j), :] = moved * (1.0 - u)
                    lows.append(hs[s])
                at = pl.multiple_of(i * 2 * SUB, 2 * SUB)
                st[s, pl.ds(at, 2 * SUB), hh * D:(hh + 1) * D] = jnp.concatenate(lows, axis=0).astype(BF16)
            return tuple(hs)

        init = []
        for s in range(SEQS):
            ek, ed = prefix[s, hh]
            init.append(ek * entering[s:s + 1] + ed)
        ended = lax.fori_loop(0, nj // 2, body, tuple(init), unroll=2)
        for s in range(SEQS):
            ends_ref[s, :, hh * D:(hh + 1) * D] = ended[s][SUB - 1:SUB, :]

    project(0, 0)
    ag((4, 1), (6, 0))
    project(1, 0)
    ag((1, 3))
    project(2, 0)
    totals(0)
    ag((3, 2), (5, 1), (1, 4))
    project(0, 1)
    project(1, 1)
    ag((2, 3))
    project(2, 1)
    totals(1)
    ag((6, 1), (4, 2), (2, 4))
    start_load.wait()
    run_states(0)
    ag((3, 3))
    run_states(1)
    ends_store = pltpu.make_async_copy(ends_ref, ends_hbm, io_sem.at[10])
    ends_store.start()
    ag((5, 2), (3, 4))

    root = 0.7978845608028654
    cubic = 0.044715

    def ffn_in(s):
        middle = gdown[s].reshape(span, D).astype(F32) + keep_of(s) * dot(st[s], all_of(OUT))
        mid[s] = middle
        scale = lax.rsqrt(row_mean(middle * middle) + EPS)
        n2[s] = flat(tiles(middle * scale) * g_two).astype(BF16)

    def ffn_up(s, part):
        for q in (2 * part, 2 * part + 1):
            pre = dot(n2[s], cols_of(UP, q * D, (q + 1) * D))
            sq = pre * pre
            hp = 0.5 + 0.5 * jnp.tanh(pre * (root + (root * cubic) * sq))
            g = pre * hp
            gl[s, :, q * D:(q + 1) * D] = g.astype(BF16)
            slope = hp + (g * (1.0 - hp)) * (2.0 * root + (6.0 * root * cubic) * sq)
            du[s, :, q * D:(q + 1) * D] = slope.astype(BF16)

    def ffn_hidden_grad(s):
        for q in range(F // D):
            d_gelu = dot(db[s], wdown[q].reshape(F // nz, D), NT)
            at = (s, slice(None), slice(q * D, (q + 1) * D))
            du[at] = (du[at].astype(F32) * d_gelu).astype(BF16)

    RS = ((DOWN, 0), (UP, 0), (OUT, 0), (IN, 0), (IN, 1))
    partial = (wup, wout, gup, gdown)
    r0 = (r0u, r0o, r0u, r0d)
    r1 = ((r1ai, r1bi), (r1ao, r1bo), (r1au, r1bu), (r1ad, r1bd))
    r2 = ((r2ai, r2bi), (r2ao, r2bo), (r2au, r2bu), (r2ad, r2bd))
    r3 = ((r3ai, r3bi), (r3ao, r3bo), (r3au, r3bu), (r3ad, r3bd))
    finals = (sum_in, sum_out, sum_up, sum_down)

    def wide_cols(r, h):
        w, part = RS[r]
        n = full[w].shape[5] // 2
        if w == IN:
            return slice(h * n + part * D, h * n + (part + 1) * D), slice(part * D, (part + 1) * D)
        return slice(h * n, (h + 1) * n), slice(0, n)

    def rs_copies(r, stage, halves=(0, 1)):
        w = RS[r][0]
        out = []
        for h in halves:
            n, m = wide_cols(r, h)

            def add(src, dst, sem, dev):
                out.append(remote(src, dst, rs_send.at[r, sem], rs_recv.at[r, sem], dev))

            if stage == 0:
                add(partial[w].at[:, :, :, 1 - c, :, n], r0[w].at[:, :, :, :, n], h, pc)
            elif stage == 1:
                src = r0[w].at[:, 1 - y, :, :, n] if h == 0 else r0[w].at[:, :, 1 - x, :, n]
                add(src, r1[w][h].at[:, :, :, m], 2 + h, (py, px)[h])
            elif stage == 2:
                away = 1 - x if h == 0 else 1 - y
                add(r1[w][h].at[:, away, :, m], r2[w][h].at[:, :, m], 4 + h, (px, py)[h])
            else:
                for dz in range(1, nz):
                    to = lax.rem(z + dz, nz)
                    add(r2[w][h].at[to, :, m], r3[w][h].at[dz - 1, :, m], 6 + 2 * (dz - 1) + h, (to, b))
        return out

    def rs_start(r):
        for cpy in rs_copies(r, 0):
            cpy.start()

    def rs_next(r, stage):
        w = RS[r][0]
        for h in range(2):
            n, m = wide_cols(r, h)
            for cpy in rs_copies(r, stage - 1, (h,)):
                cpy.wait_recv()
            if stage == 1:
                r0[w][:, :, :, :, n] = (
                    r0[w][:, :, :, :, n].astype(F32) + partial[w][:, :, :, c, :, n].astype(F32)
                ).astype(BF16)
            elif stage == 2:
                own = r0[w][:, y, :, :, n] if h == 0 else r0[w][:, :, x, :, n]
                r1[w][h][:, :, :, m] = (r1[w][h][:, :, :, m].astype(F32) + own.astype(F32)).astype(BF16)
            elif stage == 3:
                own = r1[w][h][:, x, :, m] if h == 0 else r1[w][h][:, y, :, m]
                r2[w][h][:, :, m] = (r2[w][h][:, :, m].astype(F32) + own.astype(F32)).astype(BF16)
            else:
                total = r2[w][h][z, :, m].astype(F32)
                for i in range(nz - 1):
                    total = total + r3[w][h][i, :, m].astype(F32)
                finals[w][:, n] = total
            if stage < 4:
                for cpy in rs_copies(r, stage, (h,)):
                    cpy.start()

    def whole(ref, lo, hi):
        v = ref[:, :, lo:hi]
        return v.reshape(SEQS * span, hi - lo)

    def everything(ref):
        return whole(ref, 0, ref.shape[2])

    RD, RU, RO, RI0, RI1 = range(5)

    def grad_rows(out, left, right, q):
        n = left.shape[2] // nz
        g = dot(whole(left, q * n, (q + 1) * n), everything(right), TN)
        out[q] = g.astype(BF16).reshape(out.shape[1:])

    def grad_cols(out, left, right, q):
        g = dot(everything(left), whole(right, q * D, (q + 1) * D), TN)
        out[:, :, :, :, :, q * D:(q + 1) * D] = g.astype(BF16).reshape(out.shape[:5] + (D,))

    vgrad[...] = jnp.zeros_like(vgrad)

    def vec_add(at, v):
        for i in range(v.shape[1] // LANES):
            t = at // LANES + i
            vgrad[t // 8, t % 8] += v[:, i * LANES:(i + 1) * LANES]

    send_halo.wait_send()
    ffn_in(0)
    ag((6, 2))
    ffn_in(1)
    ffn_in(2)
    ag((4, 3))
    ffn_up(0, 0)
    ffn_up(1, 0)
    ag((4, 4), (5, 3))
    ffn_up(2, 0)
    grad_rows(gdown, gl, db, 0)
    ag((5, 4))
    grad_rows(gdown, gl, db, 1)
    ag((6, 3))
    ffn_up(0, 1)
    ffn_up(1, 1)
    ffn_up(2, 1)
    ag((6, 4))
    grad_rows(gdown, gl, db, 2)
    grad_rows(gdown, gl, db, 3)
    rs_start(RD)
    for s in range(SEQS):
        ffn_hidden_grad(s)
    tok_load = pltpu.make_async_copy(tok_hbm, db, io_sem.at[4])
    tok_load.start()
    rs_next(RD, 1)
    for q in range(F // D):
        grad_cols(gup, n2, du, q)
    rs_start(RU)

    def ffn_back(s):
        keep = keep_of(s)
        middle = mid[s]
        gy = cp[s].astype(F32)
        scale = lax.rsqrt(row_mean(middle * middle) + EPS)
        unit = middle * scale
        n2[s] = middle.astype(BF16)
        d_low = dot(du[s], all_of(UP), NT)
        vec_add(D, fold(d_low * unit))
        e = flat(tiles(d_low) * g_two)
        d_middle = gy + scale * (e - unit * row_mean(e * unit))
        mid[s] = d_middle
        d_mixer = (d_middle * keep).astype(BF16)
        cp[s] = d_mixer
        du[s, :, 0:H] = dot(d_mixer, all_of(OUT), NT).astype(BF16)

    ffn_back(0)
    rs_next(RU, 1)
    ffn_back(1)
    ffn_back(2)
    rs_next(RD, 2)

    bsums, bsums_in = (bsums0, bsums1), (bsums_in0, bsums_in1)
    bprefix = {}

    def two_low(s, hh, i):
        at = pl.multiple_of(i * 2 * SUB, 2 * SUB)
        v = du[s, pl.ds(at, 2 * SUB), hh * D:(hh + 1) * D].astype(F32)
        return v[0:SUB], v[SUB:2 * SUB]

    def back_totals(hh):
        def body(k, carry):
            i = nj // 2 - 1 - k
            vals = list(carry)
            for s in range(SEQS):
                ds = two_low(s, hh, i)
                for jj in (1, 0):
                    om = 1.0 - upd[s, tile_at(hh, i * 2 + jj), :]
                    vals[2 * s] = vals[2 * s] * om
                    vals[2 * s + 1] = om * (ds[jj] + vals[2 * s + 1])
            return tuple(vals)

        got = lax.fori_loop(0, nj // 2, body, (one, zero) * SEQS, unroll=2)
        for s in range(SEQS):
            a, d = inclusive(got[2 * s], got[2 * s + 1], True)
            bsums[hh][s:s + 1, :] = a[0:1, :]
            bsums[hh][SEQS + s:SEQS + s + 1, :] = d[0:1, :]
            bprefix[s, hh] = exclusive(a, d, True)
        for dz in range(1, nz):
            @pl.when(z - dz >= 0)
            def _():
                back_copy(hh, dz).start()

    def back_copy(hh, dz):
        return remote(bsums[hh], bsums_in[hh].at[z], b_send.at[hh, dz], b_recv.at[hh, z], (z - dz, b))

    def run_adjoint(hh):
        def leave_from(k, carry):
            i = nz - 1 - k
            remote(bsums[hh], bsums_in[hh].at[i], b_send.at[hh, 0], b_recv.at[hh, i], pc).wait_recv()
            got = bsums_in[hh][i]
            return got[0:SEQS] * carry + got[SEQS:2 * SEQS]

        leaving = lax.fori_loop(0, nz - 1 - z, leave_from, jnp.zeros((SEQS, D), F32))

        def body(k, carry):
            i = nj // 2 - 1 - k
            vals = list(carry)
            at = pl.multiple_of(i * 2 * SUB, 2 * SUB)
            for s in range(SEQS):
                ds = two_low(s, hh, i)
                gates, cands = [None] * 2, [None] * 2
                for jj in (1, 0):
                    u, q = upd[s, tile_at(hh, i * 2 + jj), :], cand[s, tile_at(hh, i * 2 + jj), :]
                    adj = ds[jj] + vals[2 * s]
                    vals[2 * s] = (1.0 - u) * adj
                    gates[jj] = adj * q
                    cands[jj] = adj * u
                    vals[2 * s + 1] = vals[2 * s + 1] + gates[jj]
                du[s, pl.ds(at, 2 * SUB), hh * D:(hh + 1) * D] = jnp.concatenate(gates, axis=0).astype(BF16)
                du[s, pl.ds(at, 2 * SUB), H + hh * D:H + (hh + 1) * D] = jnp.concatenate(cands, axis=0).astype(BF16)
            return tuple(vals)

        init = []
        for s in range(SEQS):
            ek, ed = bprefix[s, hh]
            init += [ek * leaving[s:s + 1] + ed, zero]
        done = lax.fori_loop(0, nj // 2, body, tuple(init), unroll=2)
        vec_add(6 * D + hh * D, done[1] + done[3] + done[5])

    back_totals(0)
    back_totals(1)
    ag_left(OUT)
    for q in range(nz):
        grad_rows(wout, st, cp, q)
    rs_start(RO)
    run_adjoint(0)
    rs_next(RU, 2)
    run_adjoint(1)

    first = jnp.concatenate([du[s, 0:4 * SUB, :] for s in range(SEQS)], axis=0)
    first = dot(first, all_of(IN), NT)
    for s in range(SEQS):
        for i in range(3):
            r = 3 * s + i
            back_out[r:r + 1, :] = first[(4 * s + i) * SUB:(4 * s + i) * SUB + 1, :]
    send_back = remote(back_out, back_in, h_sem.at[2], h_sem.at[3], up_z(nz - 1))
    send_back.start()
    rs_next(RO, 1)

    ag_left(UP)
    grad_cols(wup, mix, du, 0)
    grad_cols(wup, mix, du, 2)
    for cpy in rs_copies(RU, 1):
        cpy.wait_send()
    pl.semaphore_signal(free_sem, inc=1, device_id=pc, device_id_type=MESH)
    pl.semaphore_wait(free_sem, 1)
    rs_start(RI0)
    rs_next(RD, 3)
    grad_cols(wup, mix, du, 1)
    grad_cols(wup, mix, du, 3)
    rs_start(RI1)
    rs_next(RI0, 1)
    rs_next(RU, 3)

    def back_project(s):
        upd[s, 0:span] = dot(du[s], all_of(IN), NT)

    def ffn_out(s):
        block = (n2[s].astype(F32) + keep_of(s) * dot(gl[s], all_of(DOWN))).astype(BF16)
        n2[s] = dot(perm[...], block, TN).astype(BF16)

    def back_norm(s):
        for i in range(3):
            r = 3 * s + i
            tile = pltpu.roll(upd[s, i * SUB:(i + 1) * SUB, :], SUB - 1, 0)
            edge = jnp.where(z < nz - 1, back_in[r:r + 1, :], 0.0)
            upd[s, span + i * SUB:span + (i + 1) * SUB] = jnp.where(sub0 == SUB - 1, edge, tile)
        unit, scale = unit_of(dot(perm[...], db[s]))
        normed = (tiles(unit) * g_one).astype(BF16).astype(F32)
        d_normed = jnp.zeros((nj, SUB, D), F32)
        for k in range(4):
            ahead = tiles(upd[s, (3 - k) * SUB:(3 - k) * SUB + span])
            d_normed = d_normed + taps[k] * ahead
            vec_add((2 + k) * D, jnp.sum(normed * ahead, axis=0))
        vec_add(0, jnp.sum(d_normed * tiles(unit), axis=0))
        e = flat(d_normed * g_one)
        out = mid[s] + scale * (e - unit * row_mean(e * unit))
        high = out.astype(BF16)
        rest_low = (out - high.astype(F32)).astype(BF16)
        mid[s] = dot(perm[...], high, TN) + dot(perm[...], rest_low, TN)

    back_project(0)
    rs_next(RI1, 1)
    back_project(1)
    rs_next(RO, 2)
    back_project(2)
    rs_next(RI0, 2)
    tok_load.wait()
    send_back.wait_recv()
    back_norm(0)
    rs_next(RI1, 2)
    back_norm(1)
    rs_next(RO, 3)
    rs_next(RI0, 3)
    back_norm(2)
    def quad_copy(d):
        return remote(vgrad.at[:, lax.rem(b + d, 8)], vquad.at[d - 1], g_send.at[d - 1], g_recv.at[d - 1], peer(d))

    def line_copy(d):
        return remote(vsum.at[lax.rem(z + d, nz)], vline.at[d - 1], g_send.at[6 + d], g_recv.at[6 + d], up_z(d))

    for d in range(1, 8):
        quad_copy(d).start()
    grad_store = pltpu.make_async_copy(mid, grad_hbm, io_sem.at[7])
    grad_store.start()
    rs_next(RI1, 3)
    ffn_out(0)
    ffn_out(1)
    for d in range(1, 8):
        quad_copy(d).wait_recv()
    vsum[...] = vgrad[:, b] + jnp.sum(vquad[...], axis=0)
    for d in range(1, nz):
        line_copy(d).start()
    ffn_out(2)
    block_store = pltpu.make_async_copy(n2, block_hbm, io_sem.at[6])
    block_store.start()
    stores = [
        pltpu.make_async_copy(src, dst, io_sem.at[11 + i])
        for i, (src, dst) in enumerate(
            ((sum_down, down_hbm), (sum_up, up_hbm), (sum_out, out_hbm), (sum_in, in_hbm), (sum_vec, sum_vec_hbm))
        )
    ]
    rs_next(RD, 4)
    stores[0].start()
    rs_next(RU, 4)
    stores[1].start()
    rs_next(RO, 4)
    stores[2].start()
    rs_next(RI0, 4)
    rs_next(RI1, 4)
    stores[3].start()
    for d in range(1, nz):
        line_copy(d).wait_recv()
    sum_vec[...] = jnp.sum(vsum[z] + jnp.sum(vline[...], axis=0), axis=0, keepdims=True)

    stores[4].start()

    ag_left(IN, DOWN)
    for r in range(5):
        for stage in range(4):
            if (r, stage) != (RU, 1):
                for cpy in rs_copies(r, stage):
                    cpy.wait_send()
    for d in range(1, nz):
        vec_line(d).wait_send()
        line_copy(d).wait_send()
    for d in range(1, 8):
        vec_peer(d).wait_send()
        quad_copy(d).wait_send()
    send_back.wait_send()
    for dz in range(1, nz):
        for hh in range(2):
            @pl.when(z + dz < nz)
            def _():
                carry_copy(hh, dz).wait_send()

            @pl.when(z - dz >= 0)
            def _():
                back_copy(hh, dz).wait_send()
    block_store.wait()
    grad_store.wait()
    ends_store.wait()
    for cpy in stores:
        cpy.wait()


def adam_math(weight, grad, first, second, rate, decay):
    moment = BETA_ONE * first + (1.0 - BETA_ONE) * grad
    square = BETA_TWO * second + (1.0 - BETA_TWO) * grad * grad
    corr_one = 1.0 - BETA_ONE**STEP
    corr_two = 1.0 - BETA_TWO**STEP
    direction = moment / corr_one / (jnp.sqrt(square / corr_two) + ADAM_EPS)
    fresh = weight - rate * (direction + decay * weight)
    return fresh, moment, square


def adam_kernel(rates, *refs):
    ins, moved_in, outs, moved_out = refs[:20], refs[20:23], refs[23:42], refs[42:45]
    held, made, passing = refs[45:65], refs[65:84], refs[84:87]
    in_sem, out_sem, move_in_sem, move_out_sem = refs[87:]
    loads = [pltpu.make_async_copy(ins[i], held[i], in_sem.at[i]) for i in range(20)]
    parts = [(i, s) for i in range(3) for s in range(SEQS)]
    comes = [pltpu.make_async_copy(moved_in[i].at[s], passing[i].at[s], move_in_sem.at[i, s]) for i, s in parts]
    goes = [pltpu.make_async_copy(passing[i].at[s], moved_out[i].at[s], move_out_sem.at[i, s]) for i, s in parts]
    for cpy in loads:
        cpy.start()
    for cpy in comes:
        cpy.start()
    stores = []
    at = 0
    for k in range(5):
        rate, decay = rates[k]
        for cpy in loads[4 * k:4 * k + 4]:
            cpy.wait()
        w, g, m, v = (r[...] for r in held[4 * k:4 * k + 4])
        fresh, moment, square = adam_math(w, g, m, v, rate, decay)
        for out in (fresh, fresh.astype(BF16), moment, square) if k < 4 else (fresh, moment, square):
            made[at][...] = out
            stores.append(pltpu.make_async_copy(made[at], outs[at], out_sem.at[at]))
            stores[-1].start()
            at += 1
    for come, go in zip(comes, goes):
        come.wait()
        go.start()
    for cpy in stores + goes:
        cpy.wait()


def fast_shards(nz, *args):
    (tokens, cotangent, start, lengths, w_in, w_out, w_up, w_down, vectors,
     m_in, v_in, m_out, v_out, m_up, v_up, m_down, v_down, m_vec, v_vec) = args
    span = tokens.shape[1]
    hbm = pl.BlockSpec(memory_space=pl.ANY)
    smem = pl.BlockSpec(memory_space=pltpu.SMEM)
    rows = [w.shape[0] for w in (w_in, w_out, w_up, w_down)]
    cols = [w.shape[1] for w in (w_in, w_out, w_up, w_down)]
    vec_row = vectors.reshape(1, LANES)

    def S(*shape, dtype=F32):
        return jax.ShapeDtypeStruct(shape, dtype)

    def low(*shape):
        return pltpu.VMEM(shape, BF16)

    def wide(*shape):
        return pltpu.VMEM(shape, F32)

    dma = pltpu.SemaphoreType.DMA
    nsend = 6 + 2 * (nz - 1)
    ndev = nz * 8
    scratch = [
        wide(SEQS, H), wide(1, LANES), wide(SEQS, 1, H), *[wide(r, n) for r, n in zip(rows, cols)], wide(1, LANES),
        low(SEQS, span, D), low(SEQS, span, D),
        *[low(nz, 2, 2, 2, r, n) for r, n in zip(rows, cols)],
        wide(SEQS, 2 * span, D), wide(SEQS, 2 * span, D),
        low(SEQS, span, H), low(SEQS, span, F), low(SEQS, span, F),
        low(SEQS, span, D), low(SEQS, span, D), wide(SEQS, span, D),
        low(nz, 2, 2, 2, rows[3], cols[3]), low(nz, 2, 2, 2, rows[2], cols[2]),
        *[low(nz, 2, 2, r, n) for r, n in zip(rows[1:], cols[1:])],
        *[low(nz, 2, r, n // 2) for r, n in zip(rows, cols) for _ in range(2)],
        *[low(nz, r, n // 2) for r, n in zip(rows, cols) for _ in range(2)],
        *[low(nz - 1, r, n // 2) for r, n in zip(rows, cols) for _ in range(2)],
        low(span, span), wide(span, LANES),
        wide(nz, 8, SUB, LANES), wide(SUB, 8 * D), wide(nz, 8, SUB, LANES),
        wide(7, nz, SUB, LANES), wide(nz, SUB, LANES), wide(nz - 1, SUB, LANES),
        low(SEQS, 2 * SUB, D), wide(16, D), wide(16, D),
        *[wide(SUB, D), wide(SUB, D), wide(nz, SUB, D), wide(nz, SUB, D)] * 2,
        dma((16,)), dma((7, 12)), dma((7, 12)), dma((5, nsend)), dma((5, nsend)),
        dma((10,)), dma((10,)), dma((10,)), dma((10,)), dma((4,)),
        *[dma((2, nz)) for _ in range(4)], pltpu.SemaphoreType.REGULAR,
    ]
    block, ends, grad, s_in, s_out, s_up, s_down, s_vec = pl.pallas_call(
        functools.partial(step_kernel, nz, span),
        out_shape=[
            S(SEQS, span, D, dtype=BF16), S(SEQS, 1, H), S(SEQS, span, D),
            *[S(r, n) for r, n in zip(rows, cols)], S(1, LANES),
        ],
        in_specs=[hbm, hbm, hbm, smem, hbm, hbm, hbm, hbm, hbm],
        out_specs=[hbm] * 8,
        scratch_shapes=scratch,
        compiler_params=pltpu.CompilerParams(
            collective_id=0, has_side_effects=True, vmem_limit_bytes=64 * 2**20 - 2**18
        ),
    )(tokens, cotangent, start, lengths, w_in, w_out, w_up, w_down, vec_row)

    rates = ((D**-0.5, DECAY), (H**-0.5, DECAY), (D**-0.5, DECAY), (F**-0.5, DECAY), (VEC_RATE, 0.0))
    outs = []
    for k in range(4):
        outs += [S(rows[k], cols[k]), S(rows[k], cols[k], dtype=BF16), S(rows[k], cols[k]), S(rows[k], cols[k])]
    outs += [S(1, LANES)] * 3
    ins = (
        w_in, s_in, m_in, v_in, w_out, s_out, m_out, v_out, w_up, s_up, m_up, v_up,
        w_down, s_down, m_down, v_down,
        vec_row, s_vec, m_vec.reshape(1, LANES), v_vec.reshape(1, LANES),
    )
    moved = (block, ends, grad)
    fresh = pl.pallas_call(
        functools.partial(adam_kernel, rates),
        out_shape=outs + [S(*v.shape, dtype=v.dtype) for v in moved],
        in_specs=[hbm] * 23,
        out_specs=[hbm] * 22,
        scratch_shapes=[
            *[pltpu.VMEM(v.shape, F32) for v in ins], *[pltpu.VMEM(v.shape, v.dtype) for v in outs],
            *[pltpu.VMEM(v.shape, v.dtype) for v in moved],
            dma((20,)), dma((19,)), dma((3, SEQS)), dma((3, SEQS)),
        ],
        compiler_params=pltpu.CompilerParams(vmem_limit_bytes=63 * 2**20),
    )(*ins, *moved)
    block, ends, grad = fresh[19:]
    return (block, ends, grad, *fresh[:16], *[v.reshape(LANES) for v in fresh[16:19]])


def entering_2(value, axis, combine, identity, reverse):
    size, mine = (lax.axis_size(axis), lax.axis_index(axis))
    everything = jax.tree.map(lambda part: lax.all_gather(part, axis), value)
    start = jax.tree.map(
        lambda part, zero: jnp.broadcast_to(jnp.asarray(zero, part.dtype), part.shape),
        value,
        identity,
    )

    def step(k, before):
        at = size - 1 - k if reverse else k
        reached = at > mine if reverse else at < mine
        new = combine(before, jax.tree.map(lambda part: part[at], everything))
        return jax.tree.map(lambda a, b: jnp.where(reached, a, b), new, before)

    return lax.fori_loop(0, size, step, start)


def shifted_2(value, axis, by):
    size = lax.axis_size(axis)
    pairs = [(i, i + by) for i in range(size) if 0 <= i + by < size]
    return lax.ppermute(value, axis, pairs)


def combine_affine(earlier, later):
    return (earlier[0] * later[0], later[0] * earlier[1] + later[1])


def carry_forward(keep_total, drive_total):
    return entering_2(
        (keep_total, drive_total),
        "seq",
        combine_affine,
        (jnp.ones_like(keep_total), jnp.zeros_like(drive_total)),
        False,
    )


def carry_backward(keep_total, drive_total):
    return entering_2(
        (keep_total, drive_total),
        "seq",
        combine_affine,
        (jnp.ones_like(keep_total), jnp.zeros_like(drive_total)),
        True,
    )


def adam_step(weight, grad, first, second, rate, decay):
    moment = BETA_ONE * first + (1.0 - BETA_ONE) * grad
    square = BETA_TWO * second + (1.0 - BETA_TWO) * grad * grad
    corr_one = 1.0 - BETA_ONE**STEP
    corr_two = 1.0 - BETA_TWO**STEP
    direction = moment / corr_one / (jnp.sqrt(square / corr_two) + ADAM_EPS)
    fresh = weight - rate * (direction + decay * weight)
    return (fresh, moment, square)


def shards(
    tokens,
    cotangent,
    start_states,
    lengths,
    w_in,
    w_out,
    w_up,
    w_down,
    vectors,
    first_in,
    second_in,
    first_out,
    second_out,
    first_up,
    second_up,
    first_down,
    second_down,
    first_vec,
    second_vec,
):
    f32 = jnp.float32
    bf16 = jnp.bfloat16
    full_in, full_out, full_up, full_down, full_vec = (
        lax.all_gather(w_in.astype(bf16), ("seq", "batch"), axis=0, tiled=True),
        lax.all_gather(w_out.astype(bf16), ("seq", "batch"), axis=0, tiled=True),
        lax.all_gather(w_up.astype(bf16), ("seq", "batch"), axis=0, tiled=True),
        lax.all_gather(w_down.astype(bf16), ("seq", "batch"), axis=0, tiled=True),
        lax.all_gather(vectors.astype(bf16), ("seq", "batch"), axis=0, tiled=True),
    )
    vec_full = full_vec.astype(f32)
    g_one = vec_full[:D]
    g_two = vec_full[D : 2 * D]
    taps = vec_full[2 * D : 6 * D].reshape(4, D)
    bias = vec_full[6 * D :]
    span_len = tokens.shape[1]
    offset = lax.axis_index("seq") * span_len
    valid = ((offset + jnp.arange(span_len))[None, :] < lengths[:, None]).astype(f32)[..., None]
    inputs = tokens.astype(f32)
    scale_one = lax.rsqrt(jnp.mean(inputs * inputs, axis=-1, keepdims=True) + EPS)
    unit_one = inputs * scale_one
    normed = (unit_one * g_one).astype(bf16)
    rim_in = shifted_2(normed[:, span_len - 3 :, :], "seq", 1)
    extended = jnp.concatenate([rim_in, normed], axis=1).astype(f32)
    mixed = sum((taps[tap_idx] * extended[:, tap_idx : tap_idx + span_len] for tap_idx in range(4)))
    mixed_low = mixed.astype(bf16)
    projected = jnp.einsum("scd,dk->sck", mixed_low, full_in, preferred_element_type=f32)
    cand = projected[..., H:]
    gate_sig = jax.nn.sigmoid(projected[..., :H] + bias)
    update = gate_sig * valid
    retain = 1.0 - update
    driven = update * cand
    run_keep, run_drive = lax.associative_scan(combine_affine, (retain, driven), axis=1)
    enter_keep, enter_drive = carry_forward(run_keep[:, -1], run_drive[:, -1])
    entering = enter_keep * start_states + enter_drive
    states = run_keep * entering[:, None] + run_drive
    stretch_end = states[:, span_len - 1 :]
    state_low = states.astype(bf16)
    mixer = jnp.einsum("sch,hd->scd", state_low, full_out, preferred_element_type=f32)
    middle = inputs + valid * mixer
    scale_two = lax.rsqrt(jnp.mean(middle * middle, axis=-1, keepdims=True) + EPS)
    unit_two = middle * scale_two
    normed_two = (unit_two * g_two).astype(bf16)
    up_pre = jnp.einsum("scd,df->scf", normed_two, full_up, preferred_element_type=f32)
    gelu_out, gelu_pull = jax.vjp(jax.nn.gelu, up_pre)
    gelu_low = gelu_out.astype(bf16)
    branch = jnp.einsum("scf,fd->scd", gelu_low, full_down, preferred_element_type=f32)
    block_out = (middle + valid * branch).astype(bf16)
    grad_y = cotangent.astype(f32)
    d_branch = (grad_y * valid).astype(bf16)
    grad_down = jnp.einsum("scf,scd->fd", gelu_low, d_branch, preferred_element_type=f32)
    d_gelu = jnp.einsum("scd,fd->scf", d_branch, full_down, preferred_element_type=f32)
    d_up = gelu_pull(d_gelu)[0].astype(bf16)
    grad_up = jnp.einsum("scd,scf->df", normed_two, d_up, preferred_element_type=f32)
    d_normed_two = jnp.einsum("scf,df->scd", d_up, full_up, preferred_element_type=f32)
    grad_g_two = jnp.sum(d_normed_two * unit_two, axis=(0, 1))
    e_two = d_normed_two * g_two
    d_middle = grad_y + scale_two * (
        e_two - unit_two * jnp.mean(e_two * unit_two, axis=-1, keepdims=True)
    )
    d_mixer = (d_middle * valid).astype(bf16)
    grad_out = jnp.einsum("sch,scd->hd", state_low, d_mixer, preferred_element_type=f32)
    d_states = jnp.einsum("scd,hd->sch", d_mixer, full_out, preferred_element_type=f32)
    shifted = jnp.concatenate([retain[:, 1:], jnp.ones_like(retain[:, :1])], axis=1)
    back_keep, back_drive = lax.associative_scan(
        combine_affine, (shifted, d_states), axis=1, reverse=True
    )
    send_keep = retain[:, 0] * back_keep[:, 0]
    send_drive = retain[:, 0] * back_drive[:, 0]
    unused_keep, incoming = carry_backward(send_keep, send_drive)
    adjoint = back_keep * incoming[:, None] + back_drive
    prev_state = jnp.concatenate([entering[:, None], states[:, :-1]], axis=1)
    d_update = adjoint * (cand - prev_state)
    d_gate = d_update * valid * gate_sig * (1.0 - gate_sig)
    grad_bias = jnp.sum(d_gate, axis=(0, 1))
    gate_low = d_gate.astype(bf16)
    cand_low = (adjoint * update).astype(bf16)
    grad_in = jnp.concatenate(
        [
            jnp.einsum("scd,sck->dk", mixed_low, gate_low, preferred_element_type=f32),
            jnp.einsum("scd,sck->dk", mixed_low, cand_low, preferred_element_type=f32),
        ],
        axis=1,
    )
    d_mixed = jnp.einsum(
        "sck,dk->scd", gate_low, full_in[:, :H], preferred_element_type=f32
    ) + jnp.einsum("sck,dk->scd", cand_low, full_in[:, H:], preferred_element_type=f32)
    grad_taps = jnp.stack(
        [
            jnp.sum(d_mixed * extended[:, tap_idx : tap_idx + span_len], axis=(0, 1))
            for tap_idx in range(4)
        ]
    )
    rim_terms = jnp.stack(
        [
            sum((taps[tap_idx] * d_mixed[:, lead - tap_idx] for tap_idx in range(lead + 1)))
            for lead in range(3)
        ],
        axis=1,
    )
    mixed_tail = jnp.concatenate([d_mixed, jnp.zeros_like(d_mixed[:, :3])], axis=1)
    d_normed = sum(
        (
            taps[tap_idx] * mixed_tail[:, 3 - tap_idx : 3 - tap_idx + span_len]
            for tap_idx in range(4)
        )
    )
    rim_back = shifted_2(rim_terms, "seq", -1)
    d_normed = d_normed.at[:, span_len - 3 :].add(rim_back)
    grad_g_one = jnp.sum(d_normed * unit_one, axis=(0, 1))
    e_one = d_normed * g_one
    grad_tokens = d_middle + scale_one * (
        e_one - unit_one * jnp.mean(e_one * unit_one, axis=-1, keepdims=True)
    )
    grad_vec = jnp.concatenate([grad_g_one, grad_g_two, grad_taps.reshape(-1), grad_bias])
    sum_in, sum_out, sum_up, sum_down, sum_vec = (
        lax.psum_scatter(grad_in, ("seq", "batch"), scatter_dimension=0, tiled=True),
        lax.psum_scatter(grad_out, ("seq", "batch"), scatter_dimension=0, tiled=True),
        lax.psum_scatter(grad_up, ("seq", "batch"), scatter_dimension=0, tiled=True),
        lax.psum_scatter(grad_down, ("seq", "batch"), scatter_dimension=0, tiled=True),
        lax.psum_scatter(grad_vec, ("seq", "batch"), scatter_dimension=0, tiled=True),
    )
    new_in, moment_in, square_in = adam_step(w_in, sum_in, first_in, second_in, D ** (-0.5), DECAY)
    new_out, moment_out, square_out = adam_step(
        w_out, sum_out, first_out, second_out, H ** (-0.5), DECAY
    )
    new_up, moment_up, square_up = adam_step(w_up, sum_up, first_up, second_up, D ** (-0.5), DECAY)
    new_down, moment_down, square_down = adam_step(
        w_down, sum_down, first_down, second_down, F ** (-0.5), DECAY
    )
    new_vec, moment_vec, square_vec = adam_step(
        vectors, sum_vec, first_vec, second_vec, VEC_RATE, 0.0
    )
    return (
        block_out,
        stretch_end,
        grad_tokens,
        new_in,
        new_in.astype(bf16),
        moment_in,
        square_in,
        new_out,
        new_out.astype(bf16),
        moment_out,
        square_out,
        new_up,
        new_up.astype(bf16),
        moment_up,
        square_up,
        new_down,
        new_down.astype(bf16),
        moment_down,
        square_down,
        new_vec,
        moment_vec,
        square_vec,
    )


def solution(mesh):
    placed = (
        P("batch", "seq", None),
        P("batch", "seq", None),
        P("batch", None),
        P("batch"),
        P(("seq", "batch"), None),
        P(("seq", "batch"), None),
        P(("seq", "batch"), None),
        P(("seq", "batch"), None),
        P(("seq", "batch")),
        P(("seq", "batch"), None),
        P(("seq", "batch"), None),
        P(("seq", "batch"), None),
        P(("seq", "batch"), None),
        P(("seq", "batch"), None),
        P(("seq", "batch"), None),
        P(("seq", "batch"), None),
        P(("seq", "batch"), None),
        P(("seq", "batch")),
        P(("seq", "batch")),
    )
    nz, nb = mesh.shape["seq"], mesh.shape["batch"]
    fits = nb == 8 and nz == 4
    return jax.shard_map(
        functools.partial(fast_shards, nz) if fits else shards,
        mesh=mesh,
        in_specs=placed,
        out_specs=(
            P("batch", "seq", None),
            P("batch", "seq", None),
            P("batch", "seq", None),
            P(("seq", "batch"), None),
            P(("seq", "batch"), None),
            P(("seq", "batch"), None),
            P(("seq", "batch"), None),
            P(("seq", "batch"), None),
            P(("seq", "batch"), None),
            P(("seq", "batch"), None),
            P(("seq", "batch"), None),
            P(("seq", "batch"), None),
            P(("seq", "batch"), None),
            P(("seq", "batch"), None),
            P(("seq", "batch"), None),
            P(("seq", "batch"), None),
            P(("seq", "batch"), None),
            P(("seq", "batch"), None),
            P(("seq", "batch"), None),
            P(("seq", "batch")),
            P(("seq", "batch")),
            P(("seq", "batch")),
        ),
        check_vma=False,
    )
```
